32 devices in a mesh: groups: 2 (over y), tm: 2 (over core), space: 8 (over z, x).
Axes of the slice: x: 2, y: 2, z: 4, core: 2. Of those that a mesh axis runs over, the one named last changes fastest.
Arguments:
- initial: float32 [32, 192, 256], P(('groups', 'space')), parts along dimension 0, may hold values from -6 to 6
- reaction: float32 [32, 192, 256], P(('groups', 'space')), parts along dimension 0, may hold values from 0.01 to 0.15
Outputs:
- slab_ends: float32 [4, 16, 192, 256], P(('groups', 'tm'), 'space'), parts along dimension 0
The draws below stay inside these ranges and needn't reach their ends.
There are 2 independent parts, one for each index of `groups`. The reference program is written for one: setup_inputs(seed, part) draws one part's arguments, and reference() takes and returns one part's arrays. A program takes and returns all parts, laid end to end along the dimension named above; each array names one. Nothing has to cross between parts.
All inputs are finite; a program needn't handle non-finite values.
Results may differ from the reference program's by a relative error of at most 0.0001.
Values sent between devices are 32-bit elements; how exact they have to be, the bound alone decides.
No kernel may reach another device: no remote copies, remote signals or barrier semaphores. Data moves between devices by JAX's collectives and lax.ppermute only.
A program may use at most 64 MiB of HBM per device.

```python
import math
import jax
import jax.numpy as jnp

NX = 192
NY = 256
FSTEPS = 16
CSTEPS = 4
ITERS = 1
SLABS = 2
NZ = 16


def steps_of(key, shape, shards, smallest, largest):
    def one(position, parts):
        heights = jax.random.uniform(jax.random.fold_in(jax.random.fold_in(key, 6), position), (parts,), jnp.float32, smallest / len(shards), largest / len(shards))
        return jnp.repeat(jnp.exp(heights), shape[position] // parts).reshape((-1,) + (1,) * (len(shape) - position - 1))

    level = one(*shards[0])
    for cut in shards[1:]:
        level = level * one(*cut)
    return level


def noise(own_key, dims, spread, bound, shards=(), held_as=jnp.bfloat16):
    result = jax.random.normal(own_key, dims, jnp.float32) * spread
    if len(shards) > 0:
        result = steps_of(own_key, dims, shards, -0.22, 0.18) * result
    return jnp.clip(result, min=-bound, max=bound).astype(held_as)


def setup_inputs(seed: int = 0, part: int = 0) -> dict:
    seeds = jax.random.split(jax.random.key(seed), 3)
    own_keys = jax.random.split(jax.random.fold_in(seeds[2], part), 3)
    initial = noise(own_keys[0], (NZ, NX, NY), 1.0, 6.0, ((0, 8),), jnp.float32)
    reaction = jnp.clip(jnp.exp(math.log(0.15) - 2.7080503 * jax.random.uniform(own_keys[1], (NZ, NX, NY), jnp.float32) ** steps_of(own_keys[1], (NZ, NX, NY), ((0, 8),), -0.2, 0.2)), 0.01, 0.15)
    return {"initial": initial, "reaction": reaction}


def stencil(padded, reaction_rate, step_len, diffusion, upwind_scale):
    middle = padded[1:-1]
    lower_plane = padded[:-2]
    upper_plane = padded[2:]
    x_minus = jnp.roll(middle, 1, 1)
    x_plus = jnp.roll(middle, -1, 1)
    y_minus = jnp.roll(middle, 1, 2)
    y_plus = jnp.roll(middle, -1, 2)
    laplace = upper_plane + lower_plane + x_plus + x_minus + y_plus + y_minus - 6.0 * middle
    upwind = 0.13 * (middle - lower_plane) + 0.12 * (middle - x_minus) + 0.10 * (middle - y_minus)
    return middle + step_len * (diffusion * laplace - upwind_scale * upwind - reaction_rate * middle)


def restrict(field):
    depth, rows, cols = field.shape
    return field.reshape(depth // 2, 2, rows // 2, 2, cols // 2, 2).mean(axis=(1, 3, 5))


def prolong(coarse_field):
    return jnp.repeat(jnp.repeat(jnp.repeat(coarse_field, 2, 0), 2, 1), 2, 2)


def fine_run(field, reaction_rate):
    for step_index in range(FSTEPS):
        field = stencil(jnp.pad(field, ((1, 1), (0, 0), (0, 0))), reaction_rate, 0.5, 0.1, 1.0)
    return field


def coarse_run(field, coarse_rate):
    small = restrict(field)
    for step_index in range(CSTEPS):
        small = stencil(jnp.pad(small, ((1, 1), (0, 0), (0, 0))), coarse_rate, 2.0, 0.025, 0.5)
    return prolong(small)


def reference(initial, reaction):
    coarse_rate = restrict(reaction)
    states = [initial]
    previous = []
    for slab_index in range(SLABS):
        guess = coarse_run(states[slab_index], coarse_rate)
        previous.append(guess)
        states.append(guess)
    for iteration in range(ITERS):
        fine_values = [fine_run(states[slab_index], reaction) for slab_index in range(SLABS)]
        fresh = [initial]
        for slab_index in range(SLABS):
            guess = coarse_run(fresh[slab_index], coarse_rate)
            fresh.append((guess + fine_values[slab_index]) - previous[slab_index])
            previous[slab_index] = guess
        states = fresh
    return jnp.stack(states[1:])
```

```python
import functools

import jax
import jax.numpy as jnp
from jax import lax
from jax.experimental import pallas as pl
from jax.experimental.pallas import tpu as pltpu
from jax.sharding import PartitionSpec as P

FSTEPS = 16
CSTEPS = 4


def with_halo(cells, sides, width):
    for axis, dim in sides:
        count = lax.axis_size(axis)
        ends = count - 1
        head = lax.slice_in_dim(cells, 0, width, axis=dim)
        tail = lax.slice_in_dim(cells, cells.shape[dim] - width, cells.shape[dim], axis=dim)
        cells = jnp.concatenate(
            [
                lax.ppermute(tail, axis, [(i, (i + 1) % count) for i in range(ends)]),
                cells,
                lax.ppermute(head, axis, [((i + 1) % count, i) for i in range(ends)]),
            ],
            axis=dim,
        )
    return cells


def passed_along(x, axis, by):
    count = lax.axis_size(axis)
    pairs = [(i, i + by) for i in range(count) if 0 <= i + by < count]
    return lax.ppermute(x, axis, pairs)


def stencil(padded, reaction_rate, step_len, diffusion, upwind_scale):
    middle = padded[1:-1]
    lower_plane = padded[:-2]
    upper_plane = padded[2:]
    x_minus = jnp.roll(middle, 1, 1)
    x_plus = jnp.roll(middle, -1, 1)
    y_minus = jnp.roll(middle, 1, 2)
    y_plus = jnp.roll(middle, -1, 2)
    laplace = upper_plane + lower_plane + x_plus + x_minus + y_plus + y_minus - 6.0 * middle
    upwind = 0.13 * (middle - lower_plane) + 0.12 * (middle - x_minus) + 0.1 * (middle - y_minus)
    return middle + step_len * (
        diffusion * laplace - upwind_scale * upwind - reaction_rate * middle
    )


def restrict(field):
    depth, rows, cols = field.shape
    return field.reshape(depth // 2, 2, rows // 2, 2, cols // 2, 2).mean(axis=(1, 3, 5))


def prolong(coarse_field):
    return jnp.repeat(jnp.repeat(jnp.repeat(coarse_field, 2, 0), 2, 1), 2, 2)


def advance(field, rate_padded, width, steps, exchanger, constants, first_plane, planes_total):
    planes = field.shape[0]

    def block_turn(turn_index, current):
        padded = exchanger(current)
        for inner in range(width):
            rim_after = width - 1 - inner
            rate_slice = rate_padded[inner + 1 : inner + 1 + planes + 2 * rim_after]
            updated = stencil(padded, rate_slice, constants[0], constants[1], constants[2])
            global_plane = first_plane - rim_after + lax.iota(jnp.int32, planes + 2 * rim_after)
            inside = (global_plane >= 0) & (global_plane < planes_total)
            padded = jnp.where(inside[:, None, None], updated, 0.0)
        return padded

    return lax.fori_loop(0, steps // width, block_turn, field)


def local(initial, reaction):
    planes = initial.shape[0]
    planes_total = planes * lax.axis_size("space")
    first_plane = lax.axis_index("space") * planes
    slab_index = lax.axis_index("tm")
    slab_count = lax.axis_size("tm")
    coarse_rate = restrict(reaction)
    no_rim = ((1, 1), (0, 0), (0, 0))
    fine_width = min(planes, FSTEPS)
    fine_rate = with_halo(reaction, (("space", 0),), fine_width)

    def fine_exchange(current):
        return with_halo(current, (("space", 0),), fine_width)

    coarse_width = 1
    coarse_padded = jnp.pad(coarse_rate, no_rim)

    def coarse_exchange(current):
        return with_halo(current, (("space", 0),), 1)

    def coarse_run(field):
        small = advance(
            restrict(field),
            coarse_padded,
            coarse_width,
            CSTEPS,
            coarse_exchange,
            (2.0, 0.025, 0.5),
            first_plane // 2,
            planes_total // 2,
        )
        return prolong(small)

    def sweep(fine_values, previous):
        state = initial
        result = initial
        guess = initial
        for sweep_turn in range(slab_count):
            guess = coarse_run(state)
            if fine_values is None:
                result = guess
            else:
                result = guess + fine_values - previous
            if sweep_turn < slab_count - 1:
                incoming = passed_along(result, "tm", 1)
                state = jnp.where(slab_index == 0, initial, incoming)
        return (result, guess, state)

    result, previous, start = sweep(None, None)
    fine_values = advance(
        start,
        fine_rate,
        fine_width,
        FSTEPS,
        fine_exchange,
        (0.5, 0.1, 1.0),
        first_plane,
        planes_total,
    )
    result, previous, start = sweep(fine_values, previous)
    return result[None]


F_CONST = (0.5, 0.1, 1.0)
C_CONST = (2.0, 0.025, 0.5)
HIGH = lax.Precision.HIGHEST
OWN = 32
EDGE = 16
LANES = 128
PAD = 8
TURNS = (0, 4, 8, 12, 16, 40)


def weights(step_len, diffusion, upwind_scale):
    lead = step_len * diffusion
    lag = step_len * upwind_scale
    centre = (1.0 - 6.0 * lead - 0.35 * lag) / lead
    lows = tuple((lead + lag * part) / lead for part in (0.13, 0.12, 0.10))
    return lead, centre, step_len / lead, lows


def iota(shape, dim):
    return lax.broadcasted_iota(jnp.int32, shape, dim)


def lanes_in(rows, first, last):
    lane = iota((rows, LANES), 1) & 63
    return (lane >= first) & (lane < last)


def roll(x, by):
    by = by % LANES
    return x if by == 0 else pltpu.roll(x, by, 1)


def dot(a, b):
    return lax.dot_general(a, b, (((1,), (0,)), ((), ())), precision=HIGH, preferred_element_type=jnp.float32)


def spread_matrix(scale):
    coarse, fine = iota((LANES, LANES), 0), iota((LANES, LANES), 1)
    hit = ((coarse >> 6) == (fine >> 6)) & ((coarse & 63) == 4 + ((fine & 63) >> 1))
    return jnp.where(hit, jnp.float32(scale), 0.0)


def gather_matrix(first, last, scale):
    fine, coarse = iota((LANES, LANES), 0), iota((LANES, LANES), 1)
    hit = ((coarse >> 6) == (fine >> 6)) & ((coarse & 63) == 4 + ((fine & 63) >> 1))
    hit = hit & ((fine & 63) >= first) & ((fine & 63) < last)
    return jnp.where(hit, jnp.float32(scale), 0.0)


def fill_ends(field, rows):
    for z in range(field.shape[0]):
        field[z, PAD - 1 : PAD, :] = roll(field[z, PAD + rows - 1 : PAD + rows, :], 64)
        field[z, PAD + rows : PAD + rows + 1, :] = roll(field[z, PAD : PAD + 1, :], 64)


def one_step(src, dst, keep, rows, lows, chunk):
    planes = src.shape[0] - 2
    low_z, low_x, low_y = lows
    for first in range(0, rows, chunk):
        below = None
        here = src[1, PAD + first : PAD + first + chunk, :]
        for z in range(planes):
            above = None
            if z + 1 < planes:
                above = src[z + 2, PAD + first : PAD + first + chunk, :]
            x_low = src[z + 1, PAD + first - 1 : PAD + first - 1 + chunk, :]
            x_high = src[z + 1, PAD + first + 1 : PAD + first + 1 + chunk, :]
            out = keep[z, first : first + chunk, :] * here + x_high + roll(here, -1)
            out = out + low_x * x_low + low_y * roll(here, 1)
            if above is not None:
                out = out + above
            if below is not None:
                out = out + low_z * below
            dst[z + 1, PAD + first : PAD + first + chunk, :] = out
            if first == 0:
                dst[z + 1, PAD + rows : PAD + rows + 1, :] = roll(out[0:1], 64)
            if first + chunk == rows:
                dst[z + 1, PAD - 1 : PAD, :] = roll(out[chunk - 1 : chunk], 64)
            below, here = here, above


def pack_kernel(tm_ref, initial, reaction, out, sums):
    tm = tm_ref[0]
    count = out.shape[0]
    half = initial.shape[1] // 2
    coarse_half = half // 2
    part = coarse_half // 2
    step = 32
    lane = iota((step, LANES), 1)
    for z in range(2):
        for first in range(0, half, step):
            tiles = []
            for base in (0, half):
                rows = slice(base + first, base + first + step)
                tiles.append(
                    [
                        jnp.where(tm == 0, initial[z, rows, t * LANES : (t + 1) * LANES], reaction[z, rows, t * LANES : (t + 1) * LANES])
                        for t in range(2)
                    ]
                )
            turned = [roll(t, 64) for t in tiles[1]]
            for s in range(count):
                start = (OWN * s - EDGE) % 256
                tile, off = start // LANES, start % LANES
                if off + 64 <= LANES:
                    a = tiles[0][tile]
                else:
                    a = jnp.where(lane >= off, tiles[0][tile], tiles[0][1 - tile])
                if off >= 64:
                    b = turned[1 - tile] if off + 64 >= LANES else turned[tile]
                    b = jnp.where((lane >= off - 64) & (lane < 64), turned[tile], turned[1 - tile])
                else:
                    b = turned[tile]
                in_a = ((lane - off) & (LANES - 1)) < 64
                out[s, z * half + first : z * half + first + step, :] = roll(jnp.where(in_a, a, b), -off)

    to_coarse = jnp.where((iota((2 * LANES, LANES), 0) >> 1) == iota((2 * LANES, LANES), 1), jnp.float32(0.125), 0.0)
    lane = iota((part, LANES), 1)
    for t in range(2):

        @pl.when(tm == t)
        def _(t=t):
            def small(field):
                whole = None
                for c in range(2):
                    cols = slice(c * LANES, (c + 1) * LANES)
                    for h in range(2):
                        rows = slice(h * half + 2 * part * t, h * half + 2 * part * t + 2 * part)
                        sums[c, 2 * part * h : 2 * part * (h + 1), :] = field[0, rows, cols] + field[1, rows, cols]
                for c in range(2):
                    total = sums[c, pl.ds(0, 2 * part, 2), :] + sums[c, pl.ds(1, 2 * part, 2), :]
                    piece = dot(total, to_coarse[c * LANES : (c + 1) * LANES])
                    whole = piece if whole is None else whole + piece
                return whole[:part], whole[part:]

            fields, rates = small(initial), small(reaction)
            for s in range(count):
                halves = []
                for h in range(2):
                    at = 64 * h
                    own = roll(fields[h], 12 - 16 * s + at)
                    left = roll(rates[h], 52 - 16 * s + at)
                    right = roll(rates[h], 20 - 16 * s + at)
                    here = lane & 63
                    piece = jnp.where(here < 40, own, jnp.where(here < 44, left, jnp.where(here < 48, right, 0.0)))
                    halves.append(piece)
                out[s, 2 * half : 2 * half + part, :] = jnp.where(lane < 64, halves[0], halves[1])


def march_kernel(tm_ref, mine, other, field_out, change_out, fine_a, fine_b, fine_keep, small_a, small_b, small_keep, first_guess, second_guess):
    tm = tm_ref[0]
    planes = fine_keep.shape[0]
    half = fine_keep.shape[1]
    rows = small_keep.shape[1]
    part = rows // 2
    count = planes // 2
    lead, centre, slope, lows = weights(*F_CONST)
    small_lead, small_centre, small_slope, small_lows = weights(*C_CONST)
    small_scale = small_lead**CSTEPS
    scale = lead**FSTEPS

    for field in (fine_a, fine_b):
        for z in (0, planes + 1):
            field[z] = jnp.zeros(field.shape[1:], jnp.float32)
    for field in (small_a, small_b):
        for z in (0, count + 1):
            field[z] = jnp.zeros(field.shape[1:], jnp.float32)

    to_coarse = gather_matrix(0, 64, 0.125)
    left, right = lanes_in(rows, 0, 4), lanes_in(rows, 36, 40)
    for k in range(count):
        for z in range(2):
            at = slice(z * half, (z + 1) * half)
            fine_keep[2 * k + z] = jnp.where(tm == 0, other[k, at, :], mine[k, at, :])
        total = fine_keep[2 * k, pl.ds(0, rows, 2), :] + fine_keep[2 * k, pl.ds(1, rows, 2), :]
        total = total + (fine_keep[2 * k + 1, pl.ds(0, rows, 2), :] + fine_keep[2 * k + 1, pl.ds(1, rows, 2), :])
        at = slice(2 * half, 2 * half + part)
        small_a[k + 1, PAD : PAD + part, :] = jnp.where(tm == 0, mine[k, at, :], other[k, at, :])
        small_a[k + 1, PAD + part : PAD + rows, :] = jnp.where(tm == 0, other[k, at, :], mine[k, at, :])
        window = small_a[k + 1, PAD : PAD + rows, :]
        rate = jnp.where(left, roll(window, -40), jnp.where(right, roll(window, -8), dot(total, to_coarse)))
        small_keep[k] = small_centre - small_slope * rate
        for z in range(2):
            fine_keep[2 * k + z] = centre - slope * fine_keep[2 * k + z]
    fill_ends(small_a, rows)

    def coarse_run():
        for _ in range(CSTEPS // 2):
            one_step(small_a, small_b, small_keep, rows, small_lows, 24)
            one_step(small_b, small_a, small_keep, rows, small_lows, 24)

    coarse_run()
    spread = spread_matrix(small_scale)
    for k in range(count):
        guess = dot(small_a[k + 1, PAD : PAD + rows, :], spread)
        first_guess[k] = guess
        for z in range(2):

            @pl.when(tm == 0)
            def _(k=k, z=z):
                fine_a[2 * k + z + 1, PAD : PAD + half, :] = mine[k, z * half : (z + 1) * half, :]

            @pl.when(tm != 0)
            def _(k=k, z=z, guess=guess):
                fine_a[2 * k + z + 1, pl.ds(PAD, rows, 2), :] = guess
                fine_a[2 * k + z + 1, pl.ds(PAD + 1, rows, 2), :] = guess

    @pl.when(tm != 0)
    def _():
        coarse_run()
        spread = spread_matrix(small_scale * small_scale)
        for k in range(count):
            second_guess[k] = dot(small_a[k + 1, PAD : PAD + rows, :], spread)

    fill_ends(fine_a, half)

    def turn(_, carry):
        one_step(fine_a, fine_b, fine_keep, half, lows, 24)
        one_step(fine_b, fine_a, fine_keep, half, lows, 24)
        return carry

    lax.fori_loop(0, FSTEPS // 2, turn, 0)

    keep_first = lanes_in(rows, 16, 48)
    for k in range(count):
        add = jnp.where(tm == 0, first_guess[k], 0.0)
        less = jnp.where(tm == 0, first_guess[k], second_guess[k])
        for odd in range(2):
            value = []
            for z in range(2):
                fine = fine_a[2 * k + z + 1, pl.ds(PAD + odd, rows, 2), :] * jnp.float32(scale)
                value.append((add + fine) - less)
            field_out[k, pl.ds(odd, rows, 2), :] = jnp.where(keep_first, value[0], roll(value[1], 32))

    @pl.when(tm == 0)
    def _():
        to_own = gather_matrix(16, 48, 0.125)
        for k in range(count):
            total = None
            for z in range(2):
                for odd in range(2):
                    fine = fine_a[2 * k + z + 1, pl.ds(PAD + odd, rows, 2), :] * jnp.float32(scale)
                    fine = (first_guess[k] + fine) - first_guess[k]
                    total = fine if total is None else total + fine
            small_a[k + 1, PAD : PAD + rows, :] = dot(total, to_own)
        fill_ends(small_a, rows)
        coarse_run()
        for k in range(count):
            change_out[k] = small_a[k + 1, PAD : PAD + rows, :] * jnp.float32(small_scale)


def send_kernel(field, guess, out):
    rows = guess.shape[1]
    half = 2 * rows
    spread = spread_matrix(1.0)
    keep_first = lanes_in(rows, 16, 48)
    lane = iota((8, LANES), 1)
    spill = lanes_in(8, 8, 12) | lanes_in(8, 28, 32)
    for k in range(guess.shape[0]):
        full = dot(guess[k], spread)
        both = jnp.where(keep_first, full, roll(full, 32))
        for odd in range(2):
            out[k, pl.ds(odd, rows, 2), :] = field[k, pl.ds(odd, rows, 2), :] + both
        packed = jnp.zeros((8, LANES), jnp.float32)
        for g, by in enumerate(TURNS):
            piece = jnp.where(spill, guess[k, 8 * g : 8 * g + 8, :], 0.0)
            packed = packed + roll(piece, by)
        out[k, half : half + 8, :] = packed


def unpack_kernel(strips, out, spilled):
    count = strips.shape[0]
    half = out.shape[1] // 2
    rows = half // 2
    lane8 = iota((8, LANES), 1)
    for h in range(2):
        for g in range(rows // 8):
            total = None
            for s in range(count):
                piece = roll(strips[s, half : half + 8, :], 16 * s - 4 - (8 + TURNS[g] + 64 * h))
                offset = (lane8 - (16 * s - 4)) & (LANES - 1)
                hit = (offset < 4) | ((offset >= 20) & (offset < 24))
                piece = jnp.where(hit, piece, 0.0)
                total = piece if total is None else total + piece
            at = h * rows + 8 * g
            spilled[pl.ds(2 * at, 8, 2), :] = total
            spilled[pl.ds(2 * at + 1, 8, 2), :] = total
    widen = jnp.where((iota((LANES, 2 * LANES), 1) >> 1) == iota((LANES, 2 * LANES), 0), 1.0, 0.0).astype(jnp.float32)
    step = 32
    lane = iota((step, LANES), 1)
    for h in range(2):
        for first in range(0, half, step):
            wide = dot(spilled[h * half + first : h * half + first + step, :], widen)
            for t in range(2):
                total = [None, None]
                for j in range(4):
                    s = 4 * t + j
                    block = strips[s, first : first + step, :]
                    for z in range(2):
                        piece = roll(block, OWN * j - (16 + 64 * h + 32 * z))
                        total[z] = piece if j == 0 else jnp.where(lane >= OWN * j, piece, total[z])
                for z in range(2):
                    out[z, h * half + first : h * half + first + step, t * LANES : (t + 1) * LANES] = (
                        total[z] + wide[:, t * LANES : (t + 1) * LANES]
                    )


def vmem_call(kernel, out_shapes, scratch, args, scalars=0):
    specs = [pl.BlockSpec(memory_space=pltpu.SMEM)] * scalars
    specs += [pl.BlockSpec(memory_space=pltpu.VMEM)] * (len(args) - scalars)
    shapes = [jax.ShapeDtypeStruct(s, jnp.float32) for s in out_shapes]
    return pl.pallas_call(
        kernel,
        out_shape=shapes,
        in_specs=specs,
        out_specs=[pl.BlockSpec(memory_space=pltpu.VMEM)] * len(shapes),
        scratch_shapes=[pltpu.VMEM(s, jnp.float32) for s in scratch],
        compiler_params=pltpu.CompilerParams(vmem_limit_bytes=48 * 1024 * 1024),
    )(*args)


def strips_local(initial, reaction):
    count = lax.axis_size("space")
    _, nx, _ = initial.shape
    half, rows = nx // 2, nx // 4
    planes = 2 * count
    tm = lax.axis_index("tm").astype(jnp.int32).reshape(1)
    (blocks,) = vmem_call(pack_kernel, [(count, 2 * half + rows // 2, LANES)], [(2, 2 * rows, LANES)], (tm, initial, reaction), 1)
    mine = lax.all_to_all(blocks, "space", 0, 0)
    other = lax.ppermute(mine, "tm", [(0, 1), (1, 0)])
    fine = (planes + 2, half + 2 * PAD, LANES)
    small = (count + 2, rows + 2 * PAD, LANES)
    field, guess = vmem_call(
        march_kernel,
        [(count, half, LANES), (count, rows, LANES)],
        [fine, fine, (planes, half, LANES), small, small, (count, rows, LANES), (count, rows, LANES), (count, rows, LANES)],
        (tm, mine, other),
        1,
    )
    guess = lax.ppermute(guess, "tm", [(0, 1)])
    (blocks,) = vmem_call(send_kernel, [(count, half + 8, LANES)], [], (field, guess))
    strips = lax.all_to_all(blocks, "space", 0, 0)
    (out,) = vmem_call(unpack_kernel, [(2, nx, 2 * LANES)], [(nx, LANES)], (strips,))
    return out[None]


def fits_strips(mesh, initial):
    planes = initial.shape[0] // (mesh.shape["groups"] * mesh.shape["space"])
    return (
        mesh.shape["space"] == 8
        and mesh.shape["tm"] == 2
        and planes == 2
        and initial.shape[1] == 192
        and initial.shape[2] == 256
    )


def solution(mesh):
    in_specs = (P(("groups", "space"), None, None), P(("groups", "space"), None, None))
    out_specs = P(("groups", "tm"), "space", None, None)

    def run(initial, reaction):
        body = strips_local if fits_strips(mesh, initial) else local
        return jax.shard_map(body, mesh=mesh, in_specs=in_specs, out_specs=out_specs, check_vma=False)(initial, reaction)

    return run
```

```python
import functools

import jax
import jax.numpy as jnp
from jax import lax
from jax.experimental import pallas as pl
from jax.experimental.pallas import tpu as pltpu
from jax.sharding import PartitionSpec as P

FSTEPS = 16
CSTEPS = 4


def with_halo(cells, sides, width):
    for axis, dim in sides:
        count = lax.axis_size(axis)
        ends = count - 1
        head = lax.slice_in_dim(cells, 0, width, axis=dim)
        tail = lax.slice_in_dim(cells, cells.shape[dim] - width, cells.shape[dim], axis=dim)
        cells = jnp.concatenate(
            [
                lax.ppermute(tail, axis, [(i, (i + 1) % count) for i in range(ends)]),
                cells,
                lax.ppermute(head, axis, [((i + 1) % count, i) for i in range(ends)]),
            ],
            axis=dim,
        )
    return cells


def passed_along(x, axis, by):
    count = lax.axis_size(axis)
    pairs = [(i, i + by) for i in range(count) if 0 <= i + by < count]
    return lax.ppermute(x, axis, pairs)


def stencil(padded, reaction_rate, step_len, diffusion, upwind_scale):
    middle = padded[1:-1]
    lower_plane = padded[:-2]
    upper_plane = padded[2:]
    x_minus = jnp.roll(middle, 1, 1)
    x_plus = jnp.roll(middle, -1, 1)
    y_minus = jnp.roll(middle, 1, 2)
    y_plus = jnp.roll(middle, -1, 2)
    laplace = upper_plane + lower_plane + x_plus + x_minus + y_plus + y_minus - 6.0 * middle
    upwind = 0.13 * (middle - lower_plane) + 0.12 * (middle - x_minus) + 0.1 * (middle - y_minus)
    return middle + step_len * (
        diffusion * laplace - upwind_scale * upwind - reaction_rate * middle
    )


def restrict(field):
    depth, rows, cols = field.shape
    return field.reshape(depth // 2, 2, rows // 2, 2, cols // 2, 2).mean(axis=(1, 3, 5))


def prolong(coarse_field):
    return jnp.repeat(jnp.repeat(jnp.repeat(coarse_field, 2, 0), 2, 1), 2, 2)


def advance(field, rate_padded, width, steps, exchanger, constants, first_plane, planes_total):
    planes = field.shape[0]

    def block_turn(turn_index, current):
        padded = exchanger(current)
        for inner in range(width):
            rim_after = width - 1 - inner
            rate_slice = rate_padded[inner + 1 : inner + 1 + planes + 2 * rim_after]
            updated = stencil(padded, rate_slice, constants[0], constants[1], constants[2])
            global_plane = first_plane - rim_after + lax.iota(jnp.int32, planes + 2 * rim_after)
            inside = (global_plane >= 0) & (global_plane < planes_total)
            padded = jnp.where(inside[:, None, None], updated, 0.0)
        return padded

    return lax.fori_loop(0, steps // width, block_turn, field)


def local(initial, reaction):
    planes = initial.shape[0]
    planes_total = planes * lax.axis_size("space")
    first_plane = lax.axis_index("space") * planes
    slab_index = lax.axis_index("tm")
    slab_count = lax.axis_size("tm")
    coarse_rate = restrict(reaction)
    no_rim = ((1, 1), (0, 0), (0, 0))
    fine_width = min(planes, FSTEPS)
    fine_rate = with_halo(reaction, (("space", 0),), fine_width)

    def fine_exchange(current):
        return with_halo(current, (("space", 0),), fine_width)

    coarse_width = 1
    coarse_padded = jnp.pad(coarse_rate, no_rim)

    def coarse_exchange(current):
        return with_halo(current, (("space", 0),), 1)

    def coarse_run(field):
        small = advance(
            restrict(field),
            coarse_padded,
            coarse_width,
            CSTEPS,
            coarse_exchange,
            (2.0, 0.025, 0.5),
            first_plane // 2,
            planes_total // 2,
        )
        return prolong(small)

    def sweep(fine_values, previous):
        state = initial
        result = initial
        guess = initial
        for sweep_turn in range(slab_count):
            guess = coarse_run(state)
            if fine_values is None:
                result = guess
            else:
                result = guess + fine_values - previous
            if sweep_turn < slab_count - 1:
                incoming = passed_along(result, "tm", 1)
                state = jnp.where(slab_index == 0, initial, incoming)
        return (result, guess, state)

    result, previous, start = sweep(None, None)
    fine_values = advance(
        start,
        fine_rate,
        fine_width,
        FSTEPS,
        fine_exchange,
        (0.5, 0.1, 1.0),
        first_plane,
        planes_total,
    )
    result, previous, start = sweep(fine_values, previous)
    return result[None]


F_CONST = (0.5, 0.1, 1.0)
C_CONST = (2.0, 0.025, 0.5)
LANES = 128
PAD = 8
SPILL_TURNS = (0, 4, 8)
FINE_CHUNKS = ((0, 16), (32, 16), (16, 16))
HALF_CHUNKS = ((0, 24), (24, 24))
QUARTER_CHUNKS = ((0, 24),)


def weights(step_len, diffusion, upwind_scale):
    lead = step_len * diffusion
    lag = step_len * upwind_scale
    centre = (1.0 - 6.0 * lead - 0.35 * lag) / lead
    lows = tuple((lead + lag * part) / lead for part in (0.13, 0.12, 0.10))
    return lead, centre, step_len / lead, lows


def iota(shape, dim):
    return lax.broadcasted_iota(jnp.int32, shape, dim)


def roll(x, by):
    by = by % LANES
    return x if by == 0 else pltpu.roll(x, by, 1)


def take(x, lanes):
    return jnp.take_along_axis(x, lanes, axis=1, mode="promise_in_bounds")


def inside(index, first, last):
    return (index >= first) & (index < last)


def wrap_rows(field, planes, rows, quarter):
    height = rows + 2 * PAD
    for z in range(0, planes, 8):
        at = (z + 1) * height + PAD
        field[pl.ds(at - 1, 8, height), :] = roll(field[pl.ds(at + rows - 1, 8, height), :], quarter)
        field[pl.ds(at + rows, 8, height), :] = roll(field[pl.ds(at, 8, height), :], -quarter)


def one_step(src, dst, keep, planes, rows, lows, chunks, quarter):
    low_z, low_x, low_y = lows
    height = rows + 2 * PAD
    several = len(src) == 2
    for first, size in chunks:
        below = [None for _ in src]
        here = [s[height + PAD + first : height + PAD + first + size, :] for s in src]
        for z in range(planes):
            at = (z + 1) * height + PAD + first
            above = [s[at + height : at + height + size, :] if z + 1 < planes else None for s in src]
            for e, s in enumerate(src):
                if several:
                    o = here[1 - e]
                    y_low, y_high = (roll(o, 1), o) if e == 0 else (o, roll(o, -1))
                else:
                    y_low, y_high = roll(here[0], 1), roll(here[0], -1)
                out = keep[e][z * rows + first : z * rows + first + size, :] * here[e] + s[at + 1 : at + 1 + size, :]
                out = out + y_high + low_x * s[at - 1 : at - 1 + size, :] + low_y * y_low
                if above[e] is not None:
                    out = out + above[e]
                if below[e] is not None:
                    out = out + low_z * below[e]
                dst[e][at : at + size, :] = out
            below, here = here, above
    for d in dst:
        wrap_rows(d, planes, rows, quarter)


def pack_kernel(tm_ref, initial_hbm, reaction_hbm, out, initial, reaction, sums, arrived):
    tm = tm_ref[0]
    copies = [
        pltpu.make_async_copy(initial_hbm, initial, arrived.at[0]),
        pltpu.make_async_copy(reaction_hbm, reaction, arrived.at[1]),
    ]
    for copy in copies:
        copy.start()
    for copy in copies:
        copy.wait()

    count = out.shape[0]
    rows = initial.shape[1] // 4
    part = rows // 2
    step = 16
    lane = iota((step, LANES), 1)
    low_half = lane < 64
    even_odd = jnp.where(low_half, 2 * lane, 2 * lane - (LANES - 1))
    odd_even = jnp.where(low_half, 2 * lane + 1, 2 * lane - LANES)

    def columns(left, right):
        a, b = take(left, even_odd), take(right, odd_even)
        return jnp.where(low_half, a, b), roll(jnp.where(low_half, b, a), 64)

    for z in range(2):
        for first in range(0, rows, step):
            turned = ([], [])
            for j in range(4):
                at = slice(j * rows + first, j * rows + first + step)
                tiles = [
                    jnp.where(tm == 0, initial[z, at, t * LANES : (t + 1) * LANES], reaction[z, at, t * LANES : (t + 1) * LANES])
                    for t in range(2)
                ]
                for e, x in enumerate(columns(*tiles)):
                    turned[e].append(roll(x, 32 * j))
            for s in range(count):
                by = 16 * s - 8
                quarter = ((lane - by) & (LANES - 1)) >> 5
                for e in range(2):
                    r = turned[e]
                    x = jnp.where(quarter == 0, r[0], jnp.where(quarter == 1, r[1], jnp.where(quarter == 2, r[2], r[3])))
                    at = (2 * z + e) * rows + first
                    out[s, at : at + step, :] = roll(x, -by)

    lane = iota((part, LANES), 1)
    here = lane & 63
    for t in range(2):

        @pl.when(tm == t)
        def _(t=t):
            def small(field):
                parts = []
                for h in range(2):
                    for first in range(0, rows, step):
                        at = slice((2 * h + t) * rows + first, (2 * h + t) * rows + first + step)
                        tiles = [field[0, at, c * LANES : (c + 1) * LANES] + field[1, at, c * LANES : (c + 1) * LANES] for c in range(2)]
                        even, odd = columns(*tiles)
                        sums[first : first + step, :] = (even + odd) * 0.125
                    parts.append(sums[pl.ds(0, part, 2), :] + sums[pl.ds(1, part, 2), :])
                return parts

            fields, rates = small(initial), small(reaction)
            for s in range(count):
                halves = []
                for h in range(2):
                    at = 64 * h
                    own = roll(fields[h], 12 - 16 * s + at)
                    left = roll(rates[h], 52 - 16 * s + at)
                    right = roll(rates[h], 20 - 16 * s + at)
                    halves.append(jnp.where(here < 40, own, jnp.where(here < 44, left, jnp.where(here < 48, right, 0.0))))
                out[s, 4 * rows : 4 * rows + part, :] = jnp.where(lane < 64, halves[0], halves[1])


def march_kernel(
    tm_ref, mine, other, field_out, guess_out,
    even_a, odd_a, even_b, odd_b, even_keep, odd_keep, wide_a, wide_b, wide_keep, small_a, small_b, small_keep, first_guess, second_guess,
):
    tm = tm_ref[0]
    count = mine.shape[0]
    planes = 2 * count
    rows = even_keep.shape[0] // planes
    part = rows // 2
    height, wide_height, small_height = rows + 2 * PAD, rows + 2 * PAD, part + 2 * PAD
    lead, centre, slope, lows = weights(*F_CONST)
    small_lead, small_centre, small_slope, small_lows = weights(*C_CONST)
    small_scale = jnp.float32(small_lead**CSTEPS)
    scale = jnp.float32(lead**FSTEPS)
    fine_a, fine_b, fine_keep = (even_a, odd_a), (even_b, odd_b), (even_keep, odd_keep)
    lane = iota((part, LANES), 1)
    even_quarter = ((lane >> 5) & 1) == 0

    in_half = lane & 63
    for k in range(count):
        total = None
        for z in range(2):
            for e in range(2):
                at = slice((2 * z + e) * rows, (2 * z + e + 1) * rows)
                to = slice((2 * k + z) * rows, (2 * k + z + 1) * rows)
                rate = jnp.where(tm == 0, other[k, at, :], mine[k, at, :])
                fine_keep[e][to, :] = centre - slope * rate
                total = rate if total is None else total + rate
        wide_b[0:rows, :] = total * 0.125
        rate = wide_b[pl.ds(0, part, 2), :] + wide_b[pl.ds(1, part, 2), :]
        small_keep[k * part : (k + 1) * part, :] = small_centre - small_slope * rate
        at = slice(4 * rows, 4 * rows + part)
        windows = [jnp.where(tm == 0, mine[k, at, :], other[k, at, :]), jnp.where(tm == 0, other[k, at, :], mine[k, at, :])]
        for n, by in ((0, 4), (1, -28)):
            to = (k + 1) * wide_height + PAD + n * part
            wide_a[to : to + part, :] = windows[n]
            x = jnp.where(in_half < 4, roll(windows[n], -40), jnp.where(inside(in_half, 36, 40), roll(windows[n], -8), roll(rate, by)))
            wide_keep[k * rows + n * part : k * rows + (n + 1) * part, :] = small_centre - small_slope * x
    wrap_rows(wide_a, count, rows, 64)

    for _ in range(CSTEPS // 2):
        one_step((wide_a,), (wide_b,), (wide_keep,), count, rows, small_lows, HALF_CHUNKS, 64)
        one_step((wide_b,), (wide_a,), (wide_keep,), count, rows, small_lows, HALF_CHUNKS, 64)

    for k in range(count):
        at = (k + 1) * wide_height + PAD
        upper, lower = wide_a[at : at + part, :], wide_a[at + part : at + rows, :]
        guess = jnp.where(even_quarter, roll(upper, -4), roll(lower, 28)) * small_scale
        first_guess[k * part : (k + 1) * part, :] = guess
        to = (k + 1) * small_height + PAD
        small_a[to : to + part, :] = guess
        for z in range(2):
            for e in range(2):
                to = (2 * k + z + 1) * height + PAD

                @pl.when(tm == 0)
                def _(k=k, z=z, e=e, to=to):
                    fine_a[e][to : to + rows, :] = mine[k, (2 * z + e) * rows : (2 * z + e + 1) * rows, :]

                @pl.when(tm != 0)
                def _(e=e, to=to, guess=guess):
                    fine_a[e][pl.ds(to, part, 2), :] = guess
                    fine_a[e][pl.ds(to + 1, part, 2), :] = guess

    def coarse_run():
        wrap_rows(small_a, count, part, 32)
        for _ in range(CSTEPS // 2):
            one_step((small_a,), (small_b,), (small_keep,), count, part, small_lows, QUARTER_CHUNKS, 32)
            one_step((small_b,), (small_a,), (small_keep,), count, part, small_lows, QUARTER_CHUNKS, 32)

    @pl.when(tm != 0)
    def _():
        coarse_run()
        for k in range(count):
            at = (k + 1) * small_height + PAD
            second_guess[k * part : (k + 1) * part, :] = small_a[at : at + part, :] * small_scale

    for field in fine_a:
        wrap_rows(field, planes, rows, 32)

    def turn(_, carry):
        one_step(fine_a, fine_b, fine_keep, planes, rows, lows, FINE_CHUNKS, 32)
        one_step(fine_b, fine_a, fine_keep, planes, rows, lows, FINE_CHUNKS, 32)
        return carry

    lax.fori_loop(0, FSTEPS // 2, turn, 0)

    own = inside(lane & 31, 8, 24)
    for k in range(count):
        guess = first_guess[k * part : (k + 1) * part, :]
        add = jnp.where(tm == 0, guess, 0.0)
        less = jnp.where(tm == 0, guess, second_guess[k * part : (k + 1) * part, :])
        total = None
        for e in range(2):
            for odd in range(2):
                value = []
                for z in range(2):
                    fine = fine_a[e][pl.ds((2 * k + z + 1) * height + PAD + odd, part, 2), :] * scale
                    value.append((add + fine) - less)
                total = value[0] + value[1] if total is None else total + (value[0] + value[1])
                field_out[k, pl.ds(e * rows + odd, part, 2), :] = jnp.where(own, value[0], roll(value[1], 16))
        to = (k + 1) * small_height + PAD
        small_a[to : to + part, :] = jnp.where(own, total * 0.125, 0.0)

    @pl.when(tm == 0)
    def _():
        coarse_run()
        for k in range(count):
            at = (k + 1) * small_height + PAD
            guess_out[k] = small_a[at : at + part, :] * small_scale


def send_kernel(field, guess, out):
    part = guess.shape[1]
    rows = 2 * part
    in_quarter = iota((part, LANES), 1) & 31
    own = inside(in_quarter, 8, 24)
    spill = (inside(in_quarter, 4, 8) | inside(in_quarter, 24, 28))[:8]
    for k in range(guess.shape[0]):
        mine = guess[k]
        both = jnp.where(own, mine, roll(mine, 16))
        for e in range(2):
            for odd in range(2):
                at = pl.ds(e * rows + odd, part, 2)
                out[k, at, :] = field[k, at, :] + both
        packed = None
        for g, by in enumerate(SPILL_TURNS):
            piece = roll(jnp.where(spill, mine[8 * g : 8 * g + 8], 0.0), by)
            packed = piece if packed is None else packed + piece
        out[k, 2 * rows : 2 * rows + 8, :] = packed


def unpack_kernel(strips, out, spilled):
    count = strips.shape[0]
    rows = out.shape[1] // 4
    part = rows // 2

    def lined_up(read, first, size):
        quarter = ((iota((size, LANES), 1) - first) & (LANES - 1)) >> 5
        for c in range(count):
            x = [read((c + 2 * j) % count) for j in range(4)]
            yield jnp.where(quarter == 0, x[0], jnp.where(quarter == 1, x[1], jnp.where(quarter == 2, x[2], x[3])))

    def at_strips(parts, j, hit):
        total = None
        for c, x in enumerate(parts):
            s = (c + 2 * j) % count
            total = jnp.where(hit[s], x, 0.0 if total is None else total)
        return total

    lane = iota((8, LANES), 1)
    hit = []
    for s in range(count):
        off = (lane - (16 * s - 4)) & (LANES - 1)
        hit.append((off < 4) | inside(off, 20, 24))
    pieces = list(lined_up(lambda s: strips[s, 2 * rows : 2 * rows + 8, :], 4, 8))
    for g, by in enumerate(SPILL_TURNS):
        parts = [roll(x, 16 * c - 8 - by) for c, x in enumerate(pieces)]
        for j in range(4):
            x = at_strips(parts, j, hit)
            at = j * rows + 16 * g
            spilled[pl.ds(at, 8, 2), :] = x
            spilled[pl.ds(at + 1, 8, 2), :] = x

    step = 16
    lane = iota((step, LANES), 1)
    low_half = lane < 64
    from_first = ((lane & 1) << 6) + (lane >> 1)
    from_second = from_first ^ 64
    hit = [inside(lane, 16 * s, 16 * s + 16) for s in range(count)]
    for first in range(0, rows, step):
        pieces = [
            list(lined_up(lambda s, e=e: strips[s, e * rows + first : e * rows + first + step, :], 8, step)) for e in range(2)
        ]
        for z in range(2):
            parts = [[roll(x, 16 * c - 8 - 16 * z) for c, x in enumerate(pieces[e])] for e in range(2)]
            for j in range(4):
                at = slice(j * rows + first, j * rows + first + step)
                more = spilled[at, :]
                even, odd = (at_strips(parts[e], j, hit) + more for e in range(2))
                odd = roll(odd, 64)
                out[z, at, :LANES] = take(jnp.where(low_half, even, odd), from_first)
                out[z, at, LANES:] = take(jnp.where(low_half, odd, even), from_second)


VMEM = pl.BlockSpec(memory_space=pltpu.VMEM)
SMEM = pl.BlockSpec(memory_space=pltpu.SMEM)
ANY = pl.BlockSpec(memory_space=pl.ANY)


def on_core(kernel, in_specs, out_shapes, scratch, *args):
    shapes = [jax.ShapeDtypeStruct(s, jnp.float32) for s in out_shapes]
    return pl.pallas_call(
        kernel,
        out_shape=shapes,
        in_specs=in_specs,
        out_specs=[VMEM] * len(shapes),
        scratch_shapes=[pltpu.VMEM(s, jnp.float32) if isinstance(s, tuple) else s for s in scratch],
        compiler_params=pltpu.CompilerParams(vmem_limit_bytes=48 * 1024 * 1024),
    )(*args)


def strips_local(initial, reaction):
    count = lax.axis_size("space")
    _, nx, _ = initial.shape
    rows = nx // 4
    part = rows // 2
    planes = 2 * count
    tm = lax.axis_index("tm").astype(jnp.int32).reshape(1)
    (blocks,) = on_core(
        pack_kernel,
        [SMEM, ANY, ANY],
        [(count, 4 * rows + part, LANES)],
        [initial.shape, reaction.shape, (rows, LANES), pltpu.SemaphoreType.DMA((2,))],
        tm, initial, reaction,
    )
    mine = lax.all_to_all(blocks, "space", 0, 0)
    other = lax.ppermute(mine, "tm", [(0, 1), (1, 0)])
    fine = ((planes + 2) * (rows + 2 * PAD), LANES)
    wide = ((count + 2) * (rows + 2 * PAD), LANES)
    small = ((count + 2) * (part + 2 * PAD), LANES)
    small_cells = (count * part, LANES)
    field, guess = on_core(
        march_kernel,
        [SMEM, VMEM, VMEM],
        [(count, 2 * rows, LANES), (count, part, LANES)],
        [fine] * 4 + [(planes * rows, LANES)] * 2 + [wide, wide, (count * rows, LANES), small, small] + [small_cells] * 3,
        tm, mine, other,
    )
    guess = lax.ppermute(guess, "tm", [(0, 1)])
    (blocks,) = on_core(send_kernel, [VMEM, VMEM], [(count, 2 * rows + 8, LANES)], [], field, guess)
    strips = lax.all_to_all(blocks, "space", 0, 0)
    (out,) = on_core(unpack_kernel, [VMEM], [initial.shape], [(nx, LANES)], strips)
    return out[None]


def fits_strips(mesh, initial):
    planes = initial.shape[0] // (mesh.shape["groups"] * mesh.shape["space"])
    return (
        mesh.shape["space"] == 8
        and mesh.shape["tm"] == 2
        and planes == 2
        and initial.shape[1] == 192
        and initial.shape[2] == 2 * LANES
    )


def solution(mesh):
    in_specs = (P(("groups", "space"), None, None), P(("groups", "space"), None, None))
    out_specs = P(("groups", "tm"), "space", None, None)

    def run(initial, reaction):
        body = strips_local if fits_strips(mesh, initial) else local
        return jax.shard_map(body, mesh=mesh, in_specs=in_specs, out_specs=out_specs, check_vma=False)(initial, reaction)

    return run
```

```python
import functools

import jax
import jax.numpy as jnp
from jax import lax
from jax.experimental import pallas as pl
from jax.experimental.pallas import tpu as pltpu
from jax.sharding import PartitionSpec as P

FSTEPS = 16
CSTEPS = 4


def with_halo(cells, sides, width):
    for axis, dim in sides:
        count = lax.axis_size(axis)
        ends = count - 1
        head = lax.slice_in_dim(cells, 0, width, axis=dim)
        tail = lax.slice_in_dim(cells, cells.shape[dim] - width, cells.shape[dim], axis=dim)
        cells = jnp.concatenate(
            [
                lax.ppermute(tail, axis, [(i, (i + 1) % count) for i in range(ends)]),
                cells,
                lax.ppermute(head, axis, [((i + 1) % count, i) for i in range(ends)]),
            ],
            axis=dim,
        )
    return cells


def passed_along(x, axis, by):
    count = lax.axis_size(axis)
    pairs = [(i, i + by) for i in range(count) if 0 <= i + by < count]
    return lax.ppermute(x, axis, pairs)


def stencil(padded, reaction_rate, step_len, diffusion, upwind_scale):
    middle = padded[1:-1]
    lower_plane = padded[:-2]
    upper_plane = padded[2:]
    x_minus = jnp.roll(middle, 1, 1)
    x_plus = jnp.roll(middle, -1, 1)
    y_minus = jnp.roll(middle, 1, 2)
    y_plus = jnp.roll(middle, -1, 2)
    laplace = upper_plane + lower_plane + x_plus + x_minus + y_plus + y_minus - 6.0 * middle
    upwind = 0.13 * (middle - lower_plane) + 0.12 * (middle - x_minus) + 0.1 * (middle - y_minus)
    return middle + step_len * (
        diffusion * laplace - upwind_scale * upwind - reaction_rate * middle
    )


def restrict(field):
    depth, rows, cols = field.shape
    return field.reshape(depth // 2, 2, rows // 2, 2, cols // 2, 2).mean(axis=(1, 3, 5))


def prolong(coarse_field):
    return jnp.repeat(jnp.repeat(jnp.repeat(coarse_field, 2, 0), 2, 1), 2, 2)


def advance(field, rate_padded, width, steps, exchanger, constants, first_plane, planes_total):
    planes = field.shape[0]

    def block_turn(turn_index, current):
        padded = exchanger(current)
        for inner in range(width):
            rim_after = width - 1 - inner
            rate_slice = rate_padded[inner + 1 : inner + 1 + planes + 2 * rim_after]
            updated = stencil(padded, rate_slice, constants[0], constants[1], constants[2])
            global_plane = first_plane - rim_after + lax.iota(jnp.int32, planes + 2 * rim_after)
            inside = (global_plane >= 0) & (global_plane < planes_total)
            padded = jnp.where(inside[:, None, None], updated, 0.0)
        return padded

    return lax.fori_loop(0, steps // width, block_turn, field)


def local(initial, reaction):
    planes = initial.shape[0]
    planes_total = planes * lax.axis_size("space")
    first_plane = lax.axis_index("space") * planes
    slab_index = lax.axis_index("tm")
    slab_count = lax.axis_size("tm")
    coarse_rate = restrict(reaction)
    no_rim = ((1, 1), (0, 0), (0, 0))
    fine_width = min(planes, FSTEPS)
    fine_rate = with_halo(reaction, (("space", 0),), fine_width)

    def fine_exchange(current):
        return with_halo(current, (("space", 0),), fine_width)

    coarse_width = 1
    coarse_padded = jnp.pad(coarse_rate, no_rim)

    def coarse_exchange(current):
        return with_halo(current, (("space", 0),), 1)

    def coarse_run(field):
        small = advance(
            restrict(field),
            coarse_padded,
            coarse_width,
            CSTEPS,
            coarse_exchange,
            (2.0, 0.025, 0.5),
            first_plane // 2,
            planes_total // 2,
        )
        return prolong(small)

    def sweep(fine_values, previous):
        state = initial
        result = initial
        guess = initial
        for sweep_turn in range(slab_count):
            guess = coarse_run(state)
            if fine_values is None:
                result = guess
            else:
                result = guess + fine_values - previous
            if sweep_turn < slab_count - 1:
                incoming = passed_along(result, "tm", 1)
                state = jnp.where(slab_index == 0, initial, incoming)
        return (result, guess, state)

    result, previous, start = sweep(None, None)
    fine_values = advance(
        start,
        fine_rate,
        fine_width,
        FSTEPS,
        fine_exchange,
        (0.5, 0.1, 1.0),
        first_plane,
        planes_total,
    )
    result, previous, start = sweep(fine_values, previous)
    return result[None]


F_CONST = (0.5, 0.1, 1.0)
C_CONST = (2.0, 0.025, 0.5)
LANES = 128
PAD = 8
SPILL_TURNS = (0, 4, 8)
EXCHANGES = ((7, 1), (6, 5), (2, 4), (3, 0))
EDGE_ROWS = 16
FINE_CHUNKS = ((0, 16), (32, 16), (16, 16))
HALF_CHUNKS = ((0, 24), (24, 24))
QUARTER_CHUNKS = ((0, 24),)


def weights(step_len, diffusion, upwind_scale):
    lead = step_len * diffusion
    lag = step_len * upwind_scale
    centre = (1.0 - 6.0 * lead - 0.35 * lag) / lead
    lows = tuple((lead + lag * part) / lead for part in (0.13, 0.12, 0.10))
    return lead, centre, step_len / lead, lows


def iota(shape, dim):
    return lax.broadcasted_iota(jnp.int32, shape, dim)


def roll(x, by):
    by = by % LANES
    return x if by == 0 else pltpu.roll(x, by, 1)


def take(x, lanes):
    return jnp.take_along_axis(x, lanes, axis=1, mode="promise_in_bounds")


def inside(index, first, last):
    return (index >= first) & (index < last)


def wrap_rows(field, planes, rows, quarter):
    height = rows + 2 * PAD
    for z in range(0, planes, 8):
        at = (z + 1) * height + PAD
        field[pl.ds(at - 1, 8, height), :] = roll(field[pl.ds(at + rows - 1, 8, height), :], quarter)
        field[pl.ds(at + rows, 8, height), :] = roll(field[pl.ds(at, 8, height), :], -quarter)


def one_step(src, dst, keep, planes, rows, lows, chunks, quarter):
    low_z, low_x, low_y = lows
    height = rows + 2 * PAD
    several = len(src) == 2
    for first, size in chunks:
        below = [None for _ in src]
        here = [s[height + PAD + first : height + PAD + first + size, :] for s in src]
        for z in range(planes):
            at = (z + 1) * height + PAD + first
            above = [s[at + height : at + height + size, :] if z + 1 < planes else None for s in src]
            for e, s in enumerate(src):
                if several:
                    o = here[1 - e]
                    y_low, y_high = (roll(o, 1), o) if e == 0 else (o, roll(o, -1))
                else:
                    y_low, y_high = roll(here[0], 1), roll(here[0], -1)
                out = keep[e][z * rows + first : z * rows + first + size, :] * here[e] + s[at + 1 : at + 1 + size, :]
                out = out + y_high + low_x * s[at - 1 : at - 1 + size, :] + low_y * y_low
                if above[e] is not None:
                    out = out + above[e]
                if below[e] is not None:
                    out = out + low_z * below[e]
                dst[e][at : at + size, :] = out
            below, here = here, above
    for d in dst:
        wrap_rows(d, planes, rows, quarter)


def sent_to(masks):
    return lax.axis_index("space") ^ jnp.where(lax.axis_index("tm") == 0, masks[0], masks[1])


def prepare_kernel(turns, field, turned, edges, sums, coarse):
    rows = field.shape[1] // 4
    part = rows // 2
    lane = iota((rows, LANES), 1)
    low_half = lane < 64
    even_odd = jnp.where(low_half, 2 * lane, 2 * lane - (LANES - 1))
    odd_even = jnp.where(low_half, 2 * lane + 1, 2 * lane - LANES)
    for z in range(2):
        for j in range(4):
            at = slice(j * rows, (j + 1) * rows)
            left, right = take(field[z, at, :LANES], even_odd), take(field[z, at, LANES:], odd_even)
            even = jnp.where(low_half, left, right)
            odd = roll(jnp.where(low_half, right, left), 64)
            for e, x in enumerate((even, odd)):
                to = ((2 * z + e) * 4 + j) * rows
                turned[to : to + rows, :] = roll(x, 32 * j)
            if z == 0:
                sums[at, :] = even + odd
            else:
                sums[at, :] = (sums[at, :] + (even + odd)) * 0.125
    for j in range(4):
        at = j * rows
        coarse[j * part : (j + 1) * part, :] = sums[pl.ds(at, part, 2), :] + sums[pl.ds(at + 1, part, 2), :]
    for g in range(2 * rows // EDGE_ROWS):
        x = coarse[g * EDGE_ROWS : (g + 1) * EDGE_ROWS, :]
        place = 64 * (g // 3) + 16 * (g % 3)
        for n, by in enumerate(turns):
            to = (2 * g + n) * EDGE_ROWS
            edges[to : to + EDGE_ROWS, :] = roll(x, place + by)


def fill_kernel(initial_turned, initial_edges, reaction_turned, reaction_edges, *blocks):
    rows = initial_turned.shape[0] // 16
    dests = [sent_to(masks) for masks in EXCHANGES] + [lax.axis_index("space")]
    for dest, block in zip(dests, blocks):
        back = (8 - 16 * dest) & (LANES - 1)
        quarter = ((iota((rows, LANES), 1) + back) & (LANES - 1)) >> 5
        for n in range(8):
            turned = (initial_turned, reaction_turned)[n // 4]
            x = [turned[(4 * (n % 4) + j) * rows : (4 * (n % 4) + j + 1) * rows, :] for j in range(4)]
            x = jnp.where(quarter == 0, x[0], jnp.where(quarter == 1, x[1], jnp.where(quarter == 2, x[2], x[3])))
            block[n * rows : (n + 1) * rows, :] = pltpu.roll(x, back, 1)
        back = (-16 * dest) & (LANES - 1)
        slot = ((iota((EDGE_ROWS, LANES), 1) + back) & (LANES - 1)) >> 2
        x = jnp.zeros((EDGE_ROWS, LANES), jnp.float32)
        for g in range(2 * rows // EDGE_ROWS):
            for n in range(4):
                edges = (initial_edges, reaction_edges)[n // 2]
                at = (2 * g + n % 2) * EDGE_ROWS
                x = jnp.where(slot == 16 * (g // 3) + 4 * (g % 3) + n, edges[at : at + EDGE_ROWS, :], x)
        block[8 * rows : 8 * rows + EDGE_ROWS, :] = pltpu.roll(x, back, 1)


def march_kernel(
    own_block, mine_0, mine_1, mine_2, mine_3, other_0, other_1, other_2, other_3, field_out, guess_out,
    even_a, odd_a, even_b, odd_b, even_keep, odd_keep, wide_a, wide_b, wide_keep, small_a, small_b, small_keep, first_guess, second_guess, sums,
):
    tm, space = lax.axis_index("tm"), lax.axis_index("space")
    rows = (own_block.shape[0] - EDGE_ROWS) // 8
    planes = even_keep.shape[0] // rows
    count = planes // 2
    part = rows // 2
    height, wide_height, small_height = rows + 2 * PAD, rows + 2 * PAD, part + 2 * PAD
    lead, centre, slope, lows = weights(*F_CONST)
    small_lead, small_centre, small_slope, small_lows = weights(*C_CONST)
    small_scale = jnp.float32(small_lead**CSTEPS)
    scale = jnp.float32(lead**FSTEPS)
    fine_a, fine_b, fine_keep = (even_a, odd_a), (even_b, odd_b), (even_keep, odd_keep)
    lane = iota((part, LANES), 1)
    even_quarter = ((lane >> 5) & 1) == 0

    def some(index, height, first, size):
        return pl.ds(pl.multiple_of(index * height + first, 8), size)

    in_half = iota((rows, LANES), 1) & 63
    left, right = in_half < 4, inside(in_half, 36, 40)
    blocks = [(own_block, None, space)]
    for masks, mine, other in zip(EXCHANGES, (mine_0, mine_1, mine_2), (other_0, other_1, other_2)):
        blocks.append((mine, None, sent_to(masks)))
        blocks.append((other, None, sent_to(masks[::-1])))
    blocks.append((mine_3, other_3, space ^ EXCHANGES[3][0]))
    for number, (block, if_second, k) in enumerate(blocks):

        def read(first, size, block=block, if_second=if_second):
            if if_second is None:
                return block[first : first + size, :]
            return jnp.where(tm == 0, block[first : first + size, :], if_second[first : first + size, :])

        totals = []
        for n in range(2):
            total = None
            for z in range(2):
                for e in range(2):
                    x = read((4 * n + 2 * z + e) * rows, rows)
                    if n == 0:
                        fine_a[e][some(2 * k + z + 1, height, PAD, rows), :] = x
                    else:
                        fine_keep[e][some(2 * k + z, rows, 0, rows), :] = centre - slope * x
                    total = x if total is None else total + x
            temp = (2 * number + n) * rows
            sums[temp : temp + rows, :] = total * 0.125
            totals.append(temp)
        edge = read(8 * rows, EDGE_ROWS)
        small = [sums[pl.ds(temp, part, 2), :] + sums[pl.ds(temp + 1, part, 2), :] for temp in totals]
        small_keep[some(k, part, 0, part), :] = small_centre - small_slope * small[1]
        windows = []
        for n in range(2):
            inner = jnp.concatenate([roll(small[n], 4), roll(small[n], -28)], 0)
            lefts = jnp.concatenate([roll(edge, -16 * g - 8 * n) for g in range(rows // EDGE_ROWS)], 0)
            rights = jnp.concatenate([roll(edge, 32 - 16 * g - 8 * n) for g in range(rows // EDGE_ROWS)], 0)
            windows.append(jnp.where(left, lefts, jnp.where(right, rights, inner)))
        wide_a[some(k + 1, wide_height, PAD, rows), :] = windows[0]
        wide_keep[some(k, rows, 0, rows), :] = small_centre - small_slope * windows[1]
    wrap_rows(wide_a, count, rows, 64)

    for _ in range(CSTEPS // 2):
        one_step((wide_a,), (wide_b,), (wide_keep,), count, rows, small_lows, HALF_CHUNKS, 64)
        one_step((wide_b,), (wide_a,), (wide_keep,), count, rows, small_lows, HALF_CHUNKS, 64)

    for k in range(count):
        at = (k + 1) * wide_height + PAD
        upper, lower = wide_a[at : at + part, :], wide_a[at + part : at + rows, :]
        guess = jnp.where(even_quarter, roll(upper, -4), roll(lower, 28)) * small_scale
        first_guess[k * part : (k + 1) * part, :] = guess
        to = (k + 1) * small_height + PAD
        small_a[to : to + part, :] = guess

    def coarse_run():
        wrap_rows(small_a, count, part, 32)
        for _ in range(CSTEPS // 2):
            one_step((small_a,), (small_b,), (small_keep,), count, part, small_lows, QUARTER_CHUNKS, 32)
            one_step((small_b,), (small_a,), (small_keep,), count, part, small_lows, QUARTER_CHUNKS, 32)

    @pl.when(tm != 0)
    def _():
        for k in range(count):
            guess = first_guess[k * part : (k + 1) * part, :]
            for z in range(2):
                for e in range(2):
                    to = (2 * k + z + 1) * height + PAD
                    fine_a[e][pl.ds(to, part, 2), :] = guess
                    fine_a[e][pl.ds(to + 1, part, 2), :] = guess
        coarse_run()
        for k in range(count):
            at = (k + 1) * small_height + PAD
            second_guess[k * part : (k + 1) * part, :] = small_a[at : at + part, :] * small_scale

    for field in fine_a:
        wrap_rows(field, planes, rows, 32)

    def turn(_, carry):
        one_step(fine_a, fine_b, fine_keep, planes, rows, lows, FINE_CHUNKS, 32)
        one_step(fine_b, fine_a, fine_keep, planes, rows, lows, FINE_CHUNKS, 32)
        return carry

    lax.fori_loop(0, FSTEPS // 2, turn, 0)

    own = inside(lane & 31, 8, 24)
    for k in range(count):
        guess = first_guess[k * part : (k + 1) * part, :]
        add = jnp.where(tm == 0, guess, 0.0)
        less = jnp.where(tm == 0, guess, second_guess[k * part : (k + 1) * part, :])
        total = None
        for e in range(2):
            for odd in range(2):
                value = []
                for z in range(2):
                    fine = fine_a[e][pl.ds((2 * k + z + 1) * height + PAD + odd, part, 2), :] * scale
                    value.append((add + fine) - less)
                total = value[0] + value[1] if total is None else total + (value[0] + value[1])
                field_out[k, pl.ds(e * rows + odd, part, 2), :] = jnp.where(own, value[0], roll(value[1], 16))
        to = (k + 1) * small_height + PAD
        small_a[to : to + part, :] = jnp.where(own, total * 0.125, 0.0)

    @pl.when(tm == 0)
    def _():
        coarse_run()
        for k in range(count):
            at = (k + 1) * small_height + PAD
            guess_out[k] = small_a[at : at + part, :] * small_scale


def send_kernel(field, guess, *blocks):
    tm, space = lax.axis_index("tm"), lax.axis_index("space")
    part = guess.shape[1]
    rows = 2 * part
    in_quarter = iota((part, LANES), 1) & 31
    own = inside(in_quarter, 8, 24)
    spill = (inside(in_quarter, 4, 8) | inside(in_quarter, 24, 28))[:8]
    for k, block in enumerate(blocks):
        dest = space ^ k
        mine = jnp.where(tm == 0, 0.0, guess[dest])
        both = jnp.where(own, mine, roll(mine, 16))
        for e in range(2):
            for odd in range(2):
                at = pl.ds(e * rows + odd, part, 2)
                block[at, :] = field[dest, at, :] + both
        packed = None
        for g, by in enumerate(SPILL_TURNS):
            piece = roll(jnp.where(spill, mine[8 * g : 8 * g + 8], 0.0), by)
            packed = piece if packed is None else packed + piece
        block[2 * rows : 2 * rows + 8, :] = packed


def unpack_kernel(*refs):
    blocks, (out_hbm, strips, spilled, out, left) = refs[:-5], refs[-5:]
    count = len(blocks)
    rows = out.shape[1] // 4
    part = rows // 2
    space = lax.axis_index("space")
    for k, block in enumerate(blocks):
        strips[space ^ k] = block[...]

    def lined_up(read, first, size):
        quarter = ((iota((size, LANES), 1) - first) & (LANES - 1)) >> 5
        for c in range(count):
            x = [read((c + 2 * j) % count) for j in range(4)]
            yield jnp.where(quarter == 0, x[0], jnp.where(quarter == 1, x[1], jnp.where(quarter == 2, x[2], x[3])))

    def at_strips(parts, j, hit):
        total = None
        for c, x in enumerate(parts):
            s = (c + 2 * j) % count
            total = jnp.where(hit[s], x, 0.0 if total is None else total)
        return total

    lane = iota((8, LANES), 1)
    hit = []
    for s in range(count):
        off = (lane - (16 * s - 4)) & (LANES - 1)
        hit.append((off < 4) | inside(off, 20, 24))
    pieces = list(lined_up(lambda s: strips[s, 2 * rows : 2 * rows + 8, :], 4, 8))
    for g, by in enumerate(SPILL_TURNS):
        parts = [roll(x, 16 * c - 8 - by) for c, x in enumerate(pieces)]
        for j in range(4):
            x = at_strips(parts, j, hit)
            at = j * rows + 16 * g
            spilled[pl.ds(at, 8, 2), :] = x
            spilled[pl.ds(at + 1, 8, 2), :] = x

    lane = iota((rows, LANES), 1)
    low_half = lane < 64
    from_first = ((lane & 1) << 6) + (lane >> 1)
    from_second = from_first ^ 64
    hit = [inside(lane, 16 * s, 16 * s + 16) for s in range(count)]
    copies = []
    for z in range(2):
        parts = []
        for e in range(2):
            pieces = lined_up(lambda s, e=e: strips[s, e * rows : (e + 1) * rows, :], 8, rows)
            parts.append([roll(x, 16 * c - 8 - 16 * z) for c, x in enumerate(pieces)])
        for j in range(4):
            at = slice(j * rows, (j + 1) * rows)
            more = spilled[at, :]
            even, odd = (at_strips(parts[e], j, hit) + more for e in range(2))
            odd = roll(odd, 64)
            out[z, at, :LANES] = take(jnp.where(low_half, even, odd), from_first)
            out[z, at, LANES:] = take(jnp.where(low_half, odd, even), from_second)
        copies.append(pltpu.make_async_copy(out.at[z], out_hbm.at[z], left.at[z]))
        copies[-1].start()
    for copy in copies:
        copy.wait()


VMEM = pl.BlockSpec(memory_space=pltpu.VMEM)


def on_core(kernel, inputs, out_shapes, scratch=(), out_spec=VMEM):
    shapes = [jax.ShapeDtypeStruct(s, jnp.float32) for s in out_shapes]
    return pl.pallas_call(
        kernel,
        out_shape=shapes,
        in_specs=[VMEM] * len(inputs),
        out_specs=[out_spec] * len(shapes),
        scratch_shapes=[pltpu.VMEM(s, jnp.float32) if isinstance(s, tuple) else s for s in scratch],
        compiler_params=pltpu.CompilerParams(vmem_limit_bytes=48 * 1024 * 1024),
    )(*inputs)


def strips_local(initial, reaction):
    count = lax.axis_size("space")
    _, nx, _ = initial.shape
    rows = nx // 4
    part = rows // 2
    planes = 2 * count
    block = (8 * rows + EDGE_ROWS, LANES)
    prepared = []
    for field, turns in ((initial, (12, -20)), (reaction, (20, -12))):
        prepared += on_core(
            functools.partial(prepare_kernel, turns),
            [field],
            [(16 * rows, LANES), (4 * rows, LANES)],
            [(4 * rows, LANES), (2 * rows, LANES)],
        )
    *blocks, own_block = on_core(fill_kernel, prepared, [block] * 5)
    mine, other = [], []
    for x, masks in zip(blocks, EXCHANGES):
        pairs = [(t * count + i, t * count + (i ^ masks[t])) for t in range(2) if masks[t] for i in range(count)]
        mine.append(lax.ppermute(x, ("tm", "space"), pairs))
        other.append(lax.ppermute(mine[-1], "tm", [(0, 1), (1, 0)]))
    fine = ((planes + 2) * (rows + 2 * PAD), LANES)
    wide = ((count + 2) * (rows + 2 * PAD), LANES)
    small = ((count + 2) * (part + 2 * PAD), LANES)
    small_cells = (count * part, LANES)
    field, guess = on_core(
        march_kernel,
        [own_block, *mine, *other],
        [(count, 2 * rows, LANES), (count, part, LANES)],
        [fine] * 4
        + [(planes * rows, LANES)] * 2
        + [wide, wide, (count * rows, LANES), small, small]
        + [small_cells] * 3
        + [(planes * rows, LANES)],
    )
    guess = lax.ppermute(guess, "tm", [(0, 1), (1, 0)])
    own_strip, *strips = on_core(send_kernel, [field, guess], [(2 * rows + 8, LANES)] * count)
    strips = [lax.ppermute(x, "space", [(i, i ^ k) for i in range(count)]) for k, x in enumerate(strips, 1)]
    (out,) = on_core(
        unpack_kernel,
        [own_strip, *strips],
        [initial.shape],
        [(count, 2 * rows + 8, LANES), (nx, LANES), initial.shape, pltpu.SemaphoreType.DMA((2,))],
        pl.BlockSpec(memory_space=pltpu.HBM),
    )
    return out[None]


def fits_strips(mesh, initial):
    planes = initial.shape[0] // (mesh.shape["groups"] * mesh.shape["space"])
    return (
        mesh.shape["space"] == 8
        and mesh.shape["tm"] == 2
        and planes == 2
        and initial.shape[1] == 192
        and initial.shape[2] == 2 * LANES
    )


def solution(mesh):
    in_specs = (P(("groups", "space"), None, None), P(("groups", "space"), None, None))
    out_specs = P(("groups", "tm"), "space", None, None)

    def run(initial, reaction):
        body = strips_local if fits_strips(mesh, initial) else local
        return jax.shard_map(body, mesh=mesh, in_specs=in_specs, out_specs=out_specs, check_vma=False)(initial, reaction)

    return run
```

```python
import functools

import jax
import jax.numpy as jnp
from jax import lax
from jax.experimental import pallas as pl
from jax.experimental.pallas import tpu as pltpu
from jax.sharding import PartitionSpec as P

FSTEPS = 16
CSTEPS = 4


def with_halo(cells, sides, width):
    for axis, dim in sides:
        count = lax.axis_size(axis)
        ends = count - 1
        head = lax.slice_in_dim(cells, 0, width, axis=dim)
        tail = lax.slice_in_dim(cells, cells.shape[dim] - width, cells.shape[dim], axis=dim)
        cells = jnp.concatenate(
            [
                lax.ppermute(tail, axis, [(i, (i + 1) % count) for i in range(ends)]),
                cells,
                lax.ppermute(head, axis, [((i + 1) % count, i) for i in range(ends)]),
            ],
            axis=dim,
        )
    return cells


def passed_along(x, axis, by):
    count = lax.axis_size(axis)
    pairs = [(i, i + by) for i in range(count) if 0 <= i + by < count]
    return lax.ppermute(x, axis, pairs)


def stencil(padded, reaction_rate, step_len, diffusion, upwind_scale):
    middle = padded[1:-1]
    lower_plane = padded[:-2]
    upper_plane = padded[2:]
    x_minus = jnp.roll(middle, 1, 1)
    x_plus = jnp.roll(middle, -1, 1)
    y_minus = jnp.roll(middle, 1, 2)
    y_plus = jnp.roll(middle, -1, 2)
    laplace = upper_plane + lower_plane + x_plus + x_minus + y_plus + y_minus - 6.0 * middle
    upwind = 0.13 * (middle - lower_plane) + 0.12 * (middle - x_minus) + 0.1 * (middle - y_minus)
    return middle + step_len * (
        diffusion * laplace - upwind_scale * upwind - reaction_rate * middle
    )


def restrict(field):
    depth, rows, cols = field.shape
    return field.reshape(depth // 2, 2, rows // 2, 2, cols // 2, 2).mean(axis=(1, 3, 5))


def prolong(coarse_field):
    return jnp.repeat(jnp.repeat(jnp.repeat(coarse_field, 2, 0), 2, 1), 2, 2)


def advance(field, rate_padded, width, steps, exchanger, constants, first_plane, planes_total):
    planes = field.shape[0]

    def block_turn(turn_index, current):
        padded = exchanger(current)
        for inner in range(width):
            rim_after = width - 1 - inner
            rate_slice = rate_padded[inner + 1 : inner + 1 + planes + 2 * rim_after]
            updated = stencil(padded, rate_slice, constants[0], constants[1], constants[2])
            global_plane = first_plane - rim_after + lax.iota(jnp.int32, planes + 2 * rim_after)
            inside = (global_plane >= 0) & (global_plane < planes_total)
            padded = jnp.where(inside[:, None, None], updated, 0.0)
        return padded

    return lax.fori_loop(0, steps // width, block_turn, field)


def local(initial, reaction):
    planes = initial.shape[0]
    planes_total = planes * lax.axis_size("space")
    first_plane = lax.axis_index("space") * planes
    slab_index = lax.axis_index("tm")
    slab_count = lax.axis_size("tm")
    coarse_rate = restrict(reaction)
    no_rim = ((1, 1), (0, 0), (0, 0))
    fine_width = min(planes, FSTEPS)
    fine_rate = with_halo(reaction, (("space", 0),), fine_width)

    def fine_exchange(current):
        return with_halo(current, (("space", 0),), fine_width)

    coarse_width = 1
    coarse_padded = jnp.pad(coarse_rate, no_rim)

    def coarse_exchange(current):
        return with_halo(current, (("space", 0),), 1)

    def coarse_run(field):
        small = advance(
            restrict(field),
            coarse_padded,
            coarse_width,
            CSTEPS,
            coarse_exchange,
            (2.0, 0.025, 0.5),
            first_plane // 2,
            planes_total // 2,
        )
        return prolong(small)

    def sweep(fine_values, previous):
        state = initial
        result = initial
        guess = initial
        for sweep_turn in range(slab_count):
            guess = coarse_run(state)
            if fine_values is None:
                result = guess
            else:
                result = guess + fine_values - previous
            if sweep_turn < slab_count - 1:
                incoming = passed_along(result, "tm", 1)
                state = jnp.where(slab_index == 0, initial, incoming)
        return (result, guess, state)

    result, previous, start = sweep(None, None)
    fine_values = advance(
        start,
        fine_rate,
        fine_width,
        FSTEPS,
        fine_exchange,
        (0.5, 0.1, 1.0),
        first_plane,
        planes_total,
    )
    result, previous, start = sweep(fine_values, previous)
    return result[None]


F_CONST = (0.5, 0.1, 1.0)
C_CONST = (2.0, 0.025, 0.5)
LANES = 128
PAD = 8
SPILL_TURNS = (0, 4, 8)
WAY_IN = ((1, 2), (3, 4), (5, 6), (7, 0))
WAY_OUT = ((4, 5), (6, 7), (1, 2), (3, 0))
EDGE_ROWS = 16
FINE_CHUNKS = ((0, 16), (32, 16), (16, 16))
HALF_CHUNKS = ((0, 24), (24, 24))
QUARTER_CHUNKS = ((0, 24),)


def weights(step_len, diffusion, upwind_scale):
    lead = step_len * diffusion
    lag = step_len * upwind_scale
    centre = (1.0 - 6.0 * lead - 0.35 * lag) / lead
    lows = tuple((lead + lag * part) / lead for part in (0.13, 0.12, 0.10))
    return lead, centre, step_len / lead, lows


def iota(shape, dim):
    return lax.broadcasted_iota(jnp.int32, shape, dim)


def roll(x, by):
    by = by % LANES
    return x if by == 0 else pltpu.roll(x, by, 1)


def take(x, lanes):
    return jnp.take_along_axis(x, lanes, axis=1, mode="promise_in_bounds")


def inside(index, first, last):
    return (index >= first) & (index < last)


def wrap_rows(field, planes, rows, quarter):
    height = rows + 2 * PAD
    for z in range(0, planes, 8):
        at = (z + 1) * height + PAD
        field[pl.ds(at - 1, 8, height), :] = roll(field[pl.ds(at + rows - 1, 8, height), :], quarter)
        field[pl.ds(at + rows, 8, height), :] = roll(field[pl.ds(at, 8, height), :], -quarter)


def one_step(src, dst, keep, planes, rows, lows, chunks, quarter):
    low_z, low_x, low_y = lows
    height = rows + 2 * PAD
    several = len(src) == 2
    for first, size in chunks:
        below = [None for _ in src]
        here = [s[height + PAD + first : height + PAD + first + size, :] for s in src]
        for z in range(planes):
            at = (z + 1) * height + PAD + first
            above = [s[at + height : at + height + size, :] if z + 1 < planes else None for s in src]
            for e, s in enumerate(src):
                if several:
                    o = here[1 - e]
                    y_low, y_high = (roll(o, 1), o) if e == 0 else (o, roll(o, -1))
                else:
                    y_low, y_high = roll(here[0], 1), roll(here[0], -1)
                out = keep[e][z * rows + first : z * rows + first + size, :] * here[e] + s[at + 1 : at + 1 + size, :]
                out = out + y_high + low_x * s[at - 1 : at - 1 + size, :] + low_y * y_low
                if above[e] is not None:
                    out = out + above[e]
                if below[e] is not None:
                    out = out + low_z * below[e]
                dst[e][at : at + size, :] = out
            below, here = here, above
    for d in dst:
        wrap_rows(d, planes, rows, quarter)


def sent_to(masks):
    return lax.axis_index("space") ^ jnp.where(lax.axis_index("tm") == 0, masks[0], masks[1])


def prepare_kernel(turns, field, turned, edges, sums, coarse):
    rows = field.shape[1] // 4
    part = rows // 2
    lane = iota((rows, LANES), 1)
    low_half = lane < 64
    even_odd = jnp.where(low_half, 2 * lane, 2 * lane - (LANES - 1))
    odd_even = jnp.where(low_half, 2 * lane + 1, 2 * lane - LANES)
    for z in range(2):
        for j in range(4):
            at = slice(j * rows, (j + 1) * rows)
            left, right = take(field[z, at, :LANES], even_odd), take(field[z, at, LANES:], odd_even)
            even = jnp.where(low_half, left, right)
            odd = roll(jnp.where(low_half, right, left), 64)
            for e, x in enumerate((even, odd)):
                to = ((2 * z + e) * 4 + j) * rows
                turned[to : to + rows, :] = roll(x, 32 * j)
            if z == 0:
                sums[at, :] = even + odd
            else:
                sums[at, :] = (sums[at, :] + (even + odd)) * 0.125
    for j in range(4):
        at = j * rows
        coarse[j * part : (j + 1) * part, :] = sums[pl.ds(at, part, 2), :] + sums[pl.ds(at + 1, part, 2), :]
    for g in range(2 * rows // EDGE_ROWS):
        x = coarse[g * EDGE_ROWS : (g + 1) * EDGE_ROWS, :]
        place = 64 * (g // 3) + 16 * (g % 3)
        for n, by in enumerate(turns):
            to = (2 * g + n) * EDGE_ROWS
            edges[to : to + EDGE_ROWS, :] = roll(x, place + by)


def fill_kernel(initial_turned, initial_edges, reaction_turned, reaction_edges, *blocks):
    rows = initial_turned.shape[0] // 16
    dests = [sent_to(masks) for masks in WAY_IN] + [lax.axis_index("space")]
    for dest, block in zip(dests, blocks):
        back = (8 - 16 * dest) & (LANES - 1)
        quarter = ((iota((rows, LANES), 1) + back) & (LANES - 1)) >> 5
        for n in range(8):
            turned = (initial_turned, reaction_turned)[n // 4]
            x = [turned[(4 * (n % 4) + j) * rows : (4 * (n % 4) + j + 1) * rows, :] for j in range(4)]
            x = jnp.where(quarter == 0, x[0], jnp.where(quarter == 1, x[1], jnp.where(quarter == 2, x[2], x[3])))
            block[n * rows : (n + 1) * rows, :] = pltpu.roll(x, back, 1)
        back = (-16 * dest) & (LANES - 1)
        slot = ((iota((EDGE_ROWS, LANES), 1) + back) & (LANES - 1)) >> 2
        x = jnp.zeros((EDGE_ROWS, LANES), jnp.float32)
        for g in range(2 * rows // EDGE_ROWS):
            for n in range(4):
                edges = (initial_edges, reaction_edges)[n // 2]
                at = (2 * g + n % 2) * EDGE_ROWS
                x = jnp.where(slot == 16 * (g // 3) + 4 * (g % 3) + n, edges[at : at + EDGE_ROWS, :], x)
        block[8 * rows : 8 * rows + EDGE_ROWS, :] = pltpu.roll(x, back, 1)


def march_kernel(
    own_block, mine_0, mine_1, mine_2, mine_3, other_0, other_1, other_2, other_3, strip,
    even_a, odd_a, even_b, odd_b, even_keep, odd_keep, wide_a, wide_b, wide_keep, small_a, small_b, small_keep, first_guess, second_guess, sums,
):
    tm, space = lax.axis_index("tm"), lax.axis_index("space")
    rows = (own_block.shape[0] - EDGE_ROWS) // 8
    planes = even_keep.shape[0] // rows
    count = planes // 2
    part = rows // 2
    height, wide_height, small_height = rows + 2 * PAD, rows + 2 * PAD, part + 2 * PAD
    lead, centre, slope, lows = weights(*F_CONST)
    small_lead, small_centre, small_slope, small_lows = weights(*C_CONST)
    small_scale = jnp.float32(small_lead**CSTEPS)
    scale = jnp.float32(lead**FSTEPS)
    fine_a, fine_b, fine_keep = (even_a, odd_a), (even_b, odd_b), (even_keep, odd_keep)
    lane = iota((part, LANES), 1)
    even_quarter = ((lane >> 5) & 1) == 0

    def some(index, height, first, size):
        return pl.ds(pl.multiple_of(index * height + first, 8), size)

    in_half = iota((rows, LANES), 1) & 63
    left, right = in_half < 4, inside(in_half, 36, 40)
    blocks = [(own_block, None, space)]
    for masks, mine, other in zip(WAY_IN, (mine_0, mine_1, mine_2), (other_0, other_1, other_2)):
        blocks.append((mine, None, sent_to(masks)))
        blocks.append((other, None, sent_to(masks[::-1])))
    blocks.append((mine_3, other_3, space ^ WAY_IN[3][0]))
    for number, (block, if_second, k) in enumerate(blocks):

        def read(first, size, block=block, if_second=if_second):
            if if_second is None:
                return block[first : first + size, :]
            return jnp.where(tm == 0, block[first : first + size, :], if_second[first : first + size, :])

        totals = []
        for n in range(2):
            total = None
            for z in range(2):
                for e in range(2):
                    x = read((4 * n + 2 * z + e) * rows, rows)
                    if n == 0:
                        fine_a[e][some(2 * k + z + 1, height, PAD, rows), :] = x
                    else:
                        fine_keep[e][some(2 * k + z, rows, 0, rows), :] = centre - slope * x
                    total = x if total is None else total + x
            temp = (2 * number + n) * rows
            sums[temp : temp + rows, :] = total * 0.125
            totals.append(temp)
        edge = read(8 * rows, EDGE_ROWS)
        small = [sums[pl.ds(temp, part, 2), :] + sums[pl.ds(temp + 1, part, 2), :] for temp in totals]
        small_keep[some(k, part, 0, part), :] = small_centre - small_slope * small[1]
        windows = []
        for n in range(2):
            inner = jnp.concatenate([roll(small[n], 4), roll(small[n], -28)], 0)
            lefts = jnp.concatenate([roll(edge, -16 * g - 8 * n) for g in range(rows // EDGE_ROWS)], 0)
            rights = jnp.concatenate([roll(edge, 32 - 16 * g - 8 * n) for g in range(rows // EDGE_ROWS)], 0)
            windows.append(jnp.where(left, lefts, jnp.where(right, rights, inner)))
        wide_a[some(k + 1, wide_height, PAD, rows), :] = windows[0]
        wide_keep[some(k, rows, 0, rows), :] = small_centre - small_slope * windows[1]
    wrap_rows(wide_a, count, rows, 64)

    for _ in range(CSTEPS // 2):
        one_step((wide_a,), (wide_b,), (wide_keep,), count, rows, small_lows, HALF_CHUNKS, 64)
        one_step((wide_b,), (wide_a,), (wide_keep,), count, rows, small_lows, HALF_CHUNKS, 64)

    for k in range(count):
        at = (k + 1) * wide_height + PAD
        upper, lower = wide_a[at : at + part, :], wide_a[at + part : at + rows, :]
        guess = jnp.where(even_quarter, roll(upper, -4), roll(lower, 28)) * small_scale
        first_guess[k * part : (k + 1) * part, :] = guess
        to = (k + 1) * small_height + PAD
        small_a[to : to + part, :] = guess

    def coarse_run():
        wrap_rows(small_a, count, part, 32)
        for _ in range(CSTEPS // 2):
            one_step((small_a,), (small_b,), (small_keep,), count, part, small_lows, QUARTER_CHUNKS, 32)
            one_step((small_b,), (small_a,), (small_keep,), count, part, small_lows, QUARTER_CHUNKS, 32)

    @pl.when(tm != 0)
    def _():
        for k in range(count):
            guess = first_guess[k * part : (k + 1) * part, :]
            for z in range(2):
                for e in range(2):
                    to = (2 * k + z + 1) * height + PAD
                    fine_a[e][pl.ds(to, part, 2), :] = guess
                    fine_a[e][pl.ds(to + 1, part, 2), :] = guess
        coarse_run()
        for k in range(count):
            at = (k + 1) * small_height + PAD
            second_guess[k * part : (k + 1) * part, :] = small_a[at : at + part, :] * small_scale

    for field in fine_a:
        wrap_rows(field, planes, rows, 32)

    def turn(_, carry):
        one_step(fine_a, fine_b, fine_keep, planes, rows, lows, FINE_CHUNKS, 32)
        one_step(fine_b, fine_a, fine_keep, planes, rows, lows, FINE_CHUNKS, 32)
        return carry

    lax.fori_loop(0, FSTEPS // 2, turn, 0)

    own = inside(lane & 31, 8, 24)
    for k in range(count):
        guess = first_guess[k * part : (k + 1) * part, :]
        add = jnp.where(tm == 0, guess, 0.0)
        less = jnp.where(tm == 0, guess, second_guess[k * part : (k + 1) * part, :])
        total = None
        for e in range(2):
            for odd in range(2):
                value = []
                for z in range(2):
                    fine = fine_a[e][pl.ds((2 * k + z + 1) * height + PAD + odd, part, 2), :] * scale
                    value.append((add + fine) - less)
                total = value[0] + value[1] if total is None else total + (value[0] + value[1])
                strip[k, pl.ds(e * rows + odd, part, 2), :] = jnp.where(own, value[0], roll(value[1], 16))
        to = (k + 1) * small_height + PAD
        small_a[to : to + part, :] = jnp.where(own, total * 0.125, 0.0)

    @pl.when(tm == 0)
    def _():
        coarse_run()
        for k in range(count):
            at = (k + 1) * small_height + PAD
            strip[k, 2 * rows :, :] = small_a[at : at + part, :] * small_scale


def send_kernel(mine, other, *blocks):
    tm = lax.axis_index("tm")
    part = mine.shape[1] // 5
    rows = 2 * part
    in_quarter = iota((part, LANES), 1) & 31
    own = inside(in_quarter, 8, 24)
    spill = (inside(in_quarter, 4, 8) | inside(in_quarter, 24, 28))[:8]
    dests = [sent_to(masks) for masks in WAY_OUT] + [lax.axis_index("space")]
    for dest, block in zip(dests, blocks):
        guess = jnp.where(tm == 0, mine[dest, 2 * rows :, :], other[dest, 2 * rows :, :])
        both = jnp.where(own, guess, roll(guess, 16))
        block[: 2 * rows, :] = jnp.where(tm == 0, mine[dest, : 2 * rows, :], other[dest, : 2 * rows, :])
        for e in range(2):
            for odd in range(2):
                at = pl.ds(e * rows + odd, part, 2)
                to = pl.ds((2 + e) * rows + odd, part, 2)
                block[to, :] = jnp.where(tm == 0, other[dest, at, :], mine[dest, at, :]) + both
        packed = None
        for g, by in enumerate(SPILL_TURNS):
            piece = roll(jnp.where(spill, guess[8 * g : 8 * g + 8], 0.0), by)
            packed = piece if packed is None else packed + piece
        block[4 * rows : 4 * rows + 8, :] = packed


def unpack_kernel(own_block, mine_0, mine_1, mine_2, mine_3, other_0, other_1, other_2, other_3, out_hbm, strips, spilled, out, left):
    tm, space = lax.axis_index("tm"), lax.axis_index("space")
    count = strips.shape[0]
    rows = out.shape[1] // 4
    part = rows // 2
    blocks = [(own_block, None, space)]
    for masks, mine, other in zip(WAY_OUT, (mine_0, mine_1, mine_2), (other_0, other_1, other_2)):
        blocks.append((mine, None, sent_to(masks)))
        blocks.append((other, None, sent_to(masks[::-1])))
    blocks.append((mine_3, other_3, space ^ WAY_OUT[3][0]))
    for block, if_second, k in blocks:
        slabs = [block[: 2 * rows, :], block[2 * rows :, :]]
        if if_second is not None:
            slabs = [jnp.where(tm == 0, x, y) for x, y in zip(slabs, (if_second[: 2 * rows, :], if_second[2 * rows :, :]))]
        strips[k, : 2 * rows, :] = jnp.where(tm == 0, slabs[0], slabs[1][: 2 * rows])
        strips[k, 2 * rows :, :] = jnp.where(tm == 0, 0.0, slabs[1][2 * rows :])

    def lined_up(read, first, size):
        quarter = ((iota((size, LANES), 1) - first) & (LANES - 1)) >> 5
        for c in range(count):
            x = [read((c + 2 * j) % count) for j in range(4)]
            yield jnp.where(quarter == 0, x[0], jnp.where(quarter == 1, x[1], jnp.where(quarter == 2, x[2], x[3])))

    def at_strips(parts, j, hit):
        total = None
        for c, x in enumerate(parts):
            s = (c + 2 * j) % count
            total = jnp.where(hit[s], x, 0.0 if total is None else total)
        return total

    lane = iota((8, LANES), 1)
    hit = []
    for s in range(count):
        off = (lane - (16 * s - 4)) & (LANES - 1)
        hit.append((off < 4) | inside(off, 20, 24))
    pieces = list(lined_up(lambda s: strips[s, 2 * rows : 2 * rows + 8, :], 4, 8))
    for g, by in enumerate(SPILL_TURNS):
        parts = [roll(x, 16 * c - 8 - by) for c, x in enumerate(pieces)]
        for j in range(4):
            x = at_strips(parts, j, hit)
            at = j * rows + 16 * g
            spilled[pl.ds(at, 8, 2), :] = x
            spilled[pl.ds(at + 1, 8, 2), :] = x

    lane = iota((rows, LANES), 1)
    low_half = lane < 64
    from_first = ((lane & 1) << 6) + (lane >> 1)
    from_second = from_first ^ 64
    hit = [inside(lane, 16 * s, 16 * s + 16) for s in range(count)]
    copies = []
    for z in range(2):
        parts = []
        for e in range(2):
            pieces = lined_up(lambda s, e=e: strips[s, e * rows : (e + 1) * rows, :], 8, rows)
            parts.append([roll(x, 16 * c - 8 - 16 * z) for c, x in enumerate(pieces)])
        for j in range(4):
            at = slice(j * rows, (j + 1) * rows)
            more = spilled[at, :]
            even, odd = (at_strips(parts[e], j, hit) + more for e in range(2))
            odd = roll(odd, 64)
            out[z, at, :LANES] = take(jnp.where(low_half, even, odd), from_first)
            out[z, at, LANES:] = take(jnp.where(low_half, odd, even), from_second)
        copies.append(pltpu.make_async_copy(out.at[z], out_hbm.at[z], left.at[z]))
        copies[-1].start()
    for copy in copies:
        copy.wait()


VMEM = pl.BlockSpec(memory_space=pltpu.VMEM)


def on_core(kernel, inputs, out_shapes, scratch=(), out_spec=VMEM):
    shapes = [jax.ShapeDtypeStruct(s, jnp.float32) for s in out_shapes]
    return pl.pallas_call(
        kernel,
        out_shape=shapes,
        in_specs=[VMEM] * len(inputs),
        out_specs=[out_spec] * len(shapes),
        scratch_shapes=[pltpu.VMEM(s, jnp.float32) if isinstance(s, tuple) else s for s in scratch],
        compiler_params=pltpu.CompilerParams(vmem_limit_bytes=48 * 1024 * 1024),
    )(*inputs)


def swapped(x):
    return lax.ppermute(x, "tm", [(0, 1), (1, 0)])


def exchanged(blocks, way):
    count = lax.axis_size("space")
    mine = []
    for block, masks in zip(blocks, way):
        pairs = [(t * count + i, t * count + (i ^ masks[t])) for t in range(2) if masks[t] for i in range(count)]
        mine.append(lax.ppermute(block, ("tm", "space"), pairs))
    return mine, [swapped(x) for x in mine]


def strips_local(initial, reaction):
    count = lax.axis_size("space")
    _, nx, _ = initial.shape
    rows = nx // 4
    part = rows // 2
    planes = 2 * count
    block = (8 * rows + EDGE_ROWS, LANES)
    prepared = []
    for field, turns in ((initial, (12, -20)), (reaction, (20, -12))):
        prepared += on_core(
            functools.partial(prepare_kernel, turns),
            [field],
            [(16 * rows, LANES), (4 * rows, LANES)],
            [(4 * rows, LANES), (2 * rows, LANES)],
        )
    *blocks, own_block = on_core(fill_kernel, prepared, [block] * 5)
    mine, other = exchanged(blocks, WAY_IN)
    fine = ((planes + 2) * (rows + 2 * PAD), LANES)
    wide = ((count + 2) * (rows + 2 * PAD), LANES)
    small = ((count + 2) * (part + 2 * PAD), LANES)
    small_cells = (count * part, LANES)
    (strip,) = on_core(
        march_kernel,
        [own_block, *mine, *other],
        [(count, 5 * part, LANES)],
        [fine] * 4
        + [(planes * rows, LANES)] * 2
        + [wide, wide, (count * rows, LANES), small, small]
        + [small_cells] * 3
        + [(planes * rows, LANES)],
    )
    *blocks, own_block = on_core(send_kernel, [strip, swapped(strip)], [(4 * rows + 8, LANES)] * 5)
    mine, other = exchanged(blocks, WAY_OUT)
    (out,) = on_core(
        unpack_kernel,
        [own_block, *mine, *other],
        [initial.shape],
        [(count, 2 * rows + 8, LANES), (nx, LANES), initial.shape, pltpu.SemaphoreType.DMA((2,))],
        pl.BlockSpec(memory_space=pltpu.HBM),
    )
    return out[None]


def fits_strips(mesh, initial):
    planes = initial.shape[0] // (mesh.shape["groups"] * mesh.shape["space"])
    return (
        mesh.shape["space"] == 8
        and mesh.shape["tm"] == 2
        and planes == 2
        and initial.shape[1] == 192
        and initial.shape[2] == 2 * LANES
    )


def solution(mesh):
    in_specs = (P(("groups", "space"), None, None), P(("groups", "space"), None, None))
    out_specs = P(("groups", "tm"), "space", None, None)

    def run(initial, reaction):
        body = strips_local if fits_strips(mesh, initial) else local
        return jax.shard_map(body, mesh=mesh, in_specs=in_specs, out_specs=out_specs, check_vma=False)(initial, reaction)

    return run
```

```python
import functools

import jax
import jax.numpy as jnp
from jax import lax
from jax.experimental import pallas as pl
from jax.experimental.pallas import tpu as pltpu
from jax.sharding import PartitionSpec as P

FSTEPS = 16
CSTEPS = 4


def with_halo(cells, sides, width):
    for axis, dim in sides:
        count = lax.axis_size(axis)
        ends = count - 1
        head = lax.slice_in_dim(cells, 0, width, axis=dim)
        tail = lax.slice_in_dim(cells, cells.shape[dim] - width, cells.shape[dim], axis=dim)
        cells = jnp.concatenate(
            [
                lax.ppermute(tail, axis, [(i, (i + 1) % count) for i in range(ends)]),
                cells,
                lax.ppermute(head, axis, [((i + 1) % count, i) for i in range(ends)]),
            ],
            axis=dim,
        )
    return cells


def passed_along(x, axis, by):
    count = lax.axis_size(axis)
    pairs = [(i, i + by) for i in range(count) if 0 <= i + by < count]
    return lax.ppermute(x, axis, pairs)


def stencil(padded, reaction_rate, step_len, diffusion, upwind_scale):
    middle = padded[1:-1]
    lower_plane = padded[:-2]
    upper_plane = padded[2:]
    x_minus = jnp.roll(middle, 1, 1)
    x_plus = jnp.roll(middle, -1, 1)
    y_minus = jnp.roll(middle, 1, 2)
    y_plus = jnp.roll(middle, -1, 2)
    laplace = upper_plane + lower_plane + x_plus + x_minus + y_plus + y_minus - 6.0 * middle
    upwind = 0.13 * (middle - lower_plane) + 0.12 * (middle - x_minus) + 0.1 * (middle - y_minus)
    return middle + step_len * (
        diffusion * laplace - upwind_scale * upwind - reaction_rate * middle
    )


def restrict(field):
    depth, rows, cols = field.shape
    return field.reshape(depth // 2, 2, rows // 2, 2, cols // 2, 2).mean(axis=(1, 3, 5))


def prolong(coarse_field):
    return jnp.repeat(jnp.repeat(jnp.repeat(coarse_field, 2, 0), 2, 1), 2, 2)


def advance(field, rate_padded, width, steps, exchanger, constants, first_plane, planes_total):
    planes = field.shape[0]

    def block_turn(turn_index, current):
        padded = exchanger(current)
        for inner in range(width):
            rim_after = width - 1 - inner
            rate_slice = rate_padded[inner + 1 : inner + 1 + planes + 2 * rim_after]
            updated = stencil(padded, rate_slice, constants[0], constants[1], constants[2])
            global_plane = first_plane - rim_after + lax.iota(jnp.int32, planes + 2 * rim_after)
            inside = (global_plane >= 0) & (global_plane < planes_total)
            padded = jnp.where(inside[:, None, None], updated, 0.0)
        return padded

    return lax.fori_loop(0, steps // width, block_turn, field)


def local(initial, reaction):
    planes = initial.shape[0]
    planes_total = planes * lax.axis_size("space")
    first_plane = lax.axis_index("space") * planes
    slab_index = lax.axis_index("tm")
    slab_count = lax.axis_size("tm")
    coarse_rate = restrict(reaction)
    no_rim = ((1, 1), (0, 0), (0, 0))
    fine_width = min(planes, FSTEPS)
    fine_rate = with_halo(reaction, (("space", 0),), fine_width)

    def fine_exchange(current):
        return with_halo(current, (("space", 0),), fine_width)

    coarse_width = 1
    coarse_padded = jnp.pad(coarse_rate, no_rim)

    def coarse_exchange(current):
        return with_halo(current, (("space", 0),), 1)

    def coarse_run(field):
        small = advance(
            restrict(field),
            coarse_padded,
            coarse_width,
            CSTEPS,
            coarse_exchange,
            (2.0, 0.025, 0.5),
            first_plane // 2,
            planes_total // 2,
        )
        return prolong(small)

    def sweep(fine_values, previous):
        state = initial
        result = initial
        guess = initial
        for sweep_turn in range(slab_count):
            guess = coarse_run(state)
            if fine_values is None:
                result = guess
            else:
                result = guess + fine_values - previous
            if sweep_turn < slab_count - 1:
                incoming = passed_along(result, "tm", 1)
                state = jnp.where(slab_index == 0, initial, incoming)
        return (result, guess, state)

    result, previous, start = sweep(None, None)
    fine_values = advance(
        start,
        fine_rate,
        fine_width,
        FSTEPS,
        fine_exchange,
        (0.5, 0.1, 1.0),
        first_plane,
        planes_total,
    )
    result, previous, start = sweep(fine_values, previous)
    return result[None]


F_CONST = (0.5, 0.1, 1.0)
C_CONST = (2.0, 0.025, 0.5)
LANES = 128
PAD = 8
SPILL_TURNS = (0, 4, 8)
WAY_IN = ((1, 4), (5, 2), (3, 6), (7, 0))
WAY_OUT = ((4, 5), (6, 7), (1, 2), (3, 0))
EDGE_ROWS = 16
FINE_CHUNKS = ((0, 16), (32, 16), (16, 16))
HALF_CHUNKS = ((0, 16), (32, 16), (16, 16))
QUARTER_CHUNKS = ((0, 24),)


def weights(step_len, diffusion, upwind_scale):
    lead = step_len * diffusion
    lag = step_len * upwind_scale
    centre = (1.0 - 6.0 * lead - 0.35 * lag) / lead
    lows = tuple((lead + lag * part) / lead for part in (0.13, 0.12, 0.10))
    return lead, centre, step_len / lead, lows


def iota(shape, dim):
    return lax.broadcasted_iota(jnp.int32, shape, dim)


def roll(x, by):
    by = by % LANES
    return x if by == 0 else pltpu.roll(x, by, 1)


def take(x, lanes):
    return jnp.take_along_axis(x, lanes, axis=1, mode="promise_in_bounds")


def inside(index, first, last):
    return (index >= first) & (index < last)


def wrap_rows(field, planes, rows, quarter):
    height = rows + 2 * PAD
    for z in range(0, planes, 8):
        at = (z + 1) * height + PAD
        field[pl.ds(at - 1, 8, height), :] = roll(field[pl.ds(at + rows - 1, 8, height), :], quarter)
        field[pl.ds(at + rows, 8, height), :] = roll(field[pl.ds(at, 8, height), :], -quarter)


def one_step(src, dst, keep, planes, rows, lows, chunks, quarter):
    low_z, low_x, low_y = lows
    height = rows + 2 * PAD
    several = len(src) == 2
    for first, size in chunks:
        below = [None for _ in src]
        here = [s[height + PAD + first : height + PAD + first + size, :] for s in src]
        for z in range(planes):
            at = (z + 1) * height + PAD + first
            above = [s[at + height : at + height + size, :] if z + 1 < planes else None for s in src]
            for e, s in enumerate(src):
                if several:
                    o = here[1 - e]
                    y_low, y_high = (roll(o, 1), o) if e == 0 else (o, roll(o, -1))
                else:
                    y_low, y_high = roll(here[0], 1), roll(here[0], -1)
                out = keep[e][z * rows + first : z * rows + first + size, :] * here[e] + s[at + 1 : at + 1 + size, :]
                out = out + y_high + low_x * s[at - 1 : at - 1 + size, :] + low_y * y_low
                if above[e] is not None:
                    out = out + above[e]
                if below[e] is not None:
                    out = out + low_z * below[e]
                dst[e][at : at + size, :] = out
            below, here = here, above
    for d in dst:
        wrap_rows(d, planes, rows, quarter)


def sent_to(masks):
    return lax.axis_index("space") ^ jnp.where(lax.axis_index("tm") == 0, masks[0], masks[1])


def served(way, other_core=False):
    return [sent_to(masks[::-1] if other_core else masks) for masks in way] + [lax.axis_index("space")]


def prepare_kernel(turns, field, turned, edges, sums, coarse):
    rows = field.shape[1] // 4
    part = rows // 2
    lane = iota((rows, LANES), 1)
    low_half = lane < 64
    even_odd = jnp.where(low_half, 2 * lane, 2 * lane - (LANES - 1))
    odd_even = jnp.where(low_half, 2 * lane + 1, 2 * lane - LANES)
    for z in range(2):
        for j in range(4):
            at = slice(j * rows, (j + 1) * rows)
            left, right = take(field[z, at, :LANES], even_odd), take(field[z, at, LANES:], odd_even)
            even = jnp.where(low_half, left, right)
            odd = roll(jnp.where(low_half, right, left), 64)
            for e, x in enumerate((even, odd)):
                to = ((2 * z + e) * 4 + j) * rows
                turned[to : to + rows, :] = roll(x, 32 * j)
            if z == 0:
                sums[at, :] = even + odd
            else:
                sums[at, :] = (sums[at, :] + (even + odd)) * 0.125
    for j in range(4):
        at = j * rows
        coarse[j * part : (j + 1) * part, :] = sums[pl.ds(at, part, 2), :] + sums[pl.ds(at + 1, part, 2), :]
    for g in range(2 * rows // EDGE_ROWS):
        x = coarse[g * EDGE_ROWS : (g + 1) * EDGE_ROWS, :]
        place = 64 * (g // 3) + 16 * (g % 3)
        for n, by in enumerate(turns):
            to = (2 * g + n) * EDGE_ROWS
            edges[to : to + EDGE_ROWS, :] = roll(x, place + by)


def fill_kernel(initial_turned, initial_edges, reaction_turned, reaction_edges, *blocks):
    rows = initial_turned.shape[0] // 16
    for dest, block in zip(served(WAY_IN), blocks):
        back = (8 - 16 * dest) & (LANES - 1)
        quarter = ((iota((rows, LANES), 1) + back) & (LANES - 1)) >> 5
        for n in range(8):
            turned = (initial_turned, reaction_turned)[n // 4]
            x = [turned[(4 * (n % 4) + j) * rows : (4 * (n % 4) + j + 1) * rows, :] for j in range(4)]
            x = jnp.where(quarter == 0, x[0], jnp.where(quarter == 1, x[1], jnp.where(quarter == 2, x[2], x[3])))
            block[n * rows : (n + 1) * rows, :] = pltpu.roll(x, back, 1)
        back = (-16 * dest) & (LANES - 1)
        slot = ((iota((EDGE_ROWS, LANES), 1) + back) & (LANES - 1)) >> 2
        x = jnp.zeros((EDGE_ROWS, LANES), jnp.float32)
        for g in range(2 * rows // EDGE_ROWS):
            for n in range(4):
                edges = (initial_edges, reaction_edges)[n // 2]
                at = (2 * g + n % 2) * EDGE_ROWS
                x = jnp.where(slot == 16 * (g // 3) + 4 * (g % 3) + n, edges[at : at + EDGE_ROWS, :], x)
        block[8 * rows : 8 * rows + EDGE_ROWS, :] = pltpu.roll(x, back, 1)


def march_kernel(
    own_block, mine_0, mine_1, mine_2, mine_3, other_0, other_1, other_2, other_3, strip, given,
    even_a, odd_a, even_b, odd_b, even_keep, odd_keep, wide_a, wide_b, wide_keep, small_a, small_b, small_keep, second_guess, sums,
):
    tm, space = lax.axis_index("tm"), lax.axis_index("space")
    rows = (own_block.shape[0] - EDGE_ROWS) // 8
    planes = even_keep.shape[0] // rows
    count = planes // 2
    part = rows // 2
    height, wide_height, small_height = rows + 2 * PAD, rows + 2 * PAD, part + 2 * PAD
    lead, centre, slope, lows = weights(*F_CONST)
    small_lead, small_centre, small_slope, small_lows = weights(*C_CONST)
    small_scale = jnp.float32(small_lead**CSTEPS)
    scale = jnp.float32(lead**FSTEPS)
    fine_a, fine_b, fine_keep = (even_a, odd_a), (even_b, odd_b), (even_keep, odd_keep)
    lane = iota((part, LANES), 1)
    even_quarter = ((lane >> 5) & 1) == 0

    def some(index, height, first, size):
        return pl.ds(pl.multiple_of(index * height + first, 8), size)

    in_half = iota((rows, LANES), 1) & 63
    left, right = in_half < 4, inside(in_half, 36, 40)
    blocks = [(own_block, None, space)]
    for masks, mine, other in zip(WAY_IN, (mine_0, mine_1, mine_2), (other_0, other_1, other_2)):
        blocks.append((mine, None, sent_to(masks)))
        blocks.append((other, None, sent_to(masks[::-1])))
    blocks.append((mine_3, other_3, space ^ WAY_IN[3][0]))
    for number, (block, if_second, k) in enumerate(blocks):

        def read(first, size, block=block, if_second=if_second):
            if if_second is None:
                return block[first : first + size, :]
            return jnp.where(tm == 0, block[first : first + size, :], if_second[first : first + size, :])

        totals = []
        for n in range(2):
            total = None
            for z in range(2):
                for e in range(2):
                    x = read((4 * n + 2 * z + e) * rows, rows)
                    if n == 0:
                        fine_a[e][some(2 * k + z + 1, height, PAD, rows), :] = x
                    else:
                        fine_keep[e][some(2 * k + z, rows, 0, rows), :] = centre - slope * x
                    total = x if total is None else total + x
            temp = (2 * number + n) * rows
            sums[temp : temp + rows, :] = total * 0.125
            totals.append(temp)
        edge = read(8 * rows, EDGE_ROWS)
        small = [sums[pl.ds(temp, part, 2), :] + sums[pl.ds(temp + 1, part, 2), :] for temp in totals]
        small_keep[some(k, part, 0, part), :] = small_centre - small_slope * small[1]
        windows = []
        for n in range(2):
            inner = jnp.concatenate([roll(small[n], 4), roll(small[n], -28)], 0)
            lefts = jnp.concatenate([roll(edge, -16 * g - 8 * n) for g in range(rows // EDGE_ROWS)], 0)
            rights = jnp.concatenate([roll(edge, 32 - 16 * g - 8 * n) for g in range(rows // EDGE_ROWS)], 0)
            windows.append(jnp.where(left, lefts, jnp.where(right, rights, inner)))
        wide_a[some(k + 1, wide_height, PAD, rows), :] = windows[0]
        wide_keep[some(k, rows, 0, rows), :] = small_centre - small_slope * windows[1]
    def coarse_run():
        wrap_rows(small_a, count, part, 32)
        for _ in range(CSTEPS // 2):
            one_step((small_a,), (small_b,), (small_keep,), count, part, small_lows, QUARTER_CHUNKS, 32)
            one_step((small_b,), (small_a,), (small_keep,), count, part, small_lows, QUARTER_CHUNKS, 32)

    @pl.when(tm != 0)
    def _():
        wrap_rows(wide_a, count, rows, 64)
        for _ in range(CSTEPS // 2):
            one_step((wide_a,), (wide_b,), (wide_keep,), count, rows, small_lows, HALF_CHUNKS, 64)
            one_step((wide_b,), (wide_a,), (wide_keep,), count, rows, small_lows, HALF_CHUNKS, 64)
        for k in range(count):
            at = (k + 1) * wide_height + PAD
            upper, lower = wide_a[at : at + part, :], wide_a[at + part : at + rows, :]
            guess = jnp.where(even_quarter, roll(upper, -4), roll(lower, 28)) * small_scale
            strip[k, 2 * rows :, :] = guess
            to = (k + 1) * small_height + PAD
            small_a[to : to + part, :] = guess
            for z in range(2):
                for e in range(2):
                    to = (2 * k + z + 1) * height + PAD
                    fine_a[e][pl.ds(to, part, 2), :] = guess
                    fine_a[e][pl.ds(to + 1, part, 2), :] = guess
        coarse_run()
        for k in range(count):
            at = (k + 1) * small_height + PAD
            second_guess[k * part : (k + 1) * part, :] = small_a[at : at + part, :] * small_scale

    for field in fine_a:
        wrap_rows(field, planes, rows, 32)

    def turn(_, carry):
        one_step(fine_a, fine_b, fine_keep, planes, rows, lows, FINE_CHUNKS, 32)
        one_step(fine_b, fine_a, fine_keep, planes, rows, lows, FINE_CHUNKS, 32)
        return carry

    lax.fori_loop(0, FSTEPS // 2, turn, 0)

    own = inside(lane & 31, 8, 24)
    for k in range(count):
        less = jnp.where(tm == 0, 0.0, second_guess[k * part : (k + 1) * part, :])
        total = None
        for e in range(2):
            for odd in range(2):
                value = [fine_a[e][pl.ds((2 * k + z + 1) * height + PAD + odd, part, 2), :] * scale - less for z in range(2)]
                total = value[0] + value[1] if total is None else total + (value[0] + value[1])
                strip[k, pl.ds(e * rows + odd, part, 2), :] = jnp.where(own, value[0], roll(value[1], 16))
        to = (k + 1) * small_height + PAD
        small_a[to : to + part, :] = jnp.where(own, total * 0.125, 0.0)

    @pl.when(tm == 0)
    def _():
        coarse_run()
        for k in range(count):
            at = (k + 1) * small_height + PAD
            strip[k, 2 * rows :, :] = small_a[at : at + part, :] * small_scale

    for n, dest in enumerate(served(WAY_OUT, True)):
        given[n] = strip[dest]


def send_kernel(mine, other, *blocks):
    tm = lax.axis_index("tm")
    part = mine.shape[1] // 5
    rows = 2 * part
    in_quarter = iota((part, LANES), 1) & 31
    own = inside(in_quarter, 8, 24)
    spill = (inside(in_quarter, 4, 8) | inside(in_quarter, 24, 28))[:8]
    for n, (dest, block) in enumerate(zip(served(WAY_OUT), blocks)):
        kept, came = mine[dest, 2 * rows :, :], other[n, 2 * rows :, :]
        change, first = jnp.where(tm == 0, kept, came), jnp.where(tm == 0, came, kept)
        h = [jnp.where(own, x, roll(x, 16)) for x in (first, change)]
        for e in range(2):
            for odd in range(2):
                at = pl.ds(e * rows + odd, part, 2)
                to = pl.ds((2 + e) * rows + odd, part, 2)
                kept, came = mine[dest, at, :], other[n, at, :]
                block[at, :] = (h[0] + jnp.where(tm == 0, kept, came)) - h[0]
                block[to, :] = h[1] + jnp.where(tm == 0, came, kept)
        packed = None
        for g, by in enumerate(SPILL_TURNS):
            piece = roll(jnp.where(spill, change[8 * g : 8 * g + 8], 0.0), by)
            packed = piece if packed is None else packed + piece
        block[4 * rows : 4 * rows + 8, :] = packed


def unpack_kernel(own_block, mine_0, mine_1, mine_2, mine_3, other_0, other_1, other_2, other_3, out_hbm, strips, spilled, halves, out, left):
    tm, space = lax.axis_index("tm"), lax.axis_index("space")
    count = strips.shape[0]
    rows = out.shape[1] // 4
    part = rows // 2
    blocks = [(own_block, None, space)]
    for masks, mine, other in zip(WAY_OUT, (mine_0, mine_1, mine_2), (other_0, other_1, other_2)):
        blocks.append((mine, None, sent_to(masks)))
        blocks.append((other, None, sent_to(masks[::-1])))
    blocks.append((mine_3, other_3, space ^ WAY_OUT[3][0]))
    for block, if_second, k in blocks:
        slabs = [block[: 2 * rows, :], block[2 * rows :, :]]
        if if_second is not None:
            slabs = [jnp.where(tm == 0, x, y) for x, y in zip(slabs, (if_second[: 2 * rows, :], if_second[2 * rows :, :]))]
        strips[k, : 2 * rows, :] = jnp.where(tm == 0, slabs[0], slabs[1][: 2 * rows])
        strips[k, 2 * rows :, :] = jnp.where(tm == 0, 0.0, slabs[1][2 * rows :])

    def lined_up(read, first, size):
        quarter = ((iota((size, LANES), 1) - first) & (LANES - 1)) >> 5
        for c in range(count):
            x = [read((c + 2 * j) % count) for j in range(4)]
            yield jnp.where(quarter == 0, x[0], jnp.where(quarter == 1, x[1], jnp.where(quarter == 2, x[2], x[3])))

    def at_strips(parts, j, hit):
        total = None
        for c, x in enumerate(parts):
            s = (c + 2 * j) % count
            total = jnp.where(hit[s], x, 0.0 if total is None else total)
        return total

    lane = iota((8, LANES), 1)
    hit = []
    for s in range(count):
        off = (lane - (16 * s - 4)) & (LANES - 1)
        hit.append((off < 4) | inside(off, 20, 24))
    pieces = list(lined_up(lambda s: strips[s, 2 * rows : 2 * rows + 8, :], 4, 8))
    for g, by in enumerate(SPILL_TURNS):
        parts = [roll(x, 16 * c - 8 - by) for c, x in enumerate(pieces)]
        for j in range(4):
            x = at_strips(parts, j, hit)
            at = j * rows + 16 * g
            spilled[pl.ds(at, 8, 2), :] = x
            spilled[pl.ds(at + 1, 8, 2), :] = x

    lane = iota((rows, LANES), 1)
    low_half = lane < 64
    from_first = ((lane & 1) << 6) + (lane >> 1)
    from_second = from_first ^ 64
    hit = [inside(lane, 16 * s, 16 * s + 16) for s in range(count)]
    for e in range(2):
        pieces = list(lined_up(lambda s, e=e: strips[s, e * rows : (e + 1) * rows, :], 8, rows))
        for z in range(2):
            parts = [roll(x, 16 * c - 8 - 16 * z) for c, x in enumerate(pieces)]
            for j in range(4):
                to = ((2 * z + e) * 4 + j) * rows
                halves[to : to + rows, :] = at_strips(parts, j, hit)
    copies = []
    for z in range(2):
        for j in range(4):
            at = slice(j * rows, (j + 1) * rows)
            more = spilled[at, :]
            even, odd = (halves[((2 * z + e) * 4 + j) * rows : ((2 * z + e) * 4 + j + 1) * rows, :] + more for e in range(2))
            odd = roll(odd, 64)
            out[z, at, :LANES] = take(jnp.where(low_half, even, odd), from_first)
            out[z, at, LANES:] = take(jnp.where(low_half, odd, even), from_second)
        copies.append(pltpu.make_async_copy(out.at[z], out_hbm.at[z], left.at[z]))
        copies[-1].start()
    for copy in copies:
        copy.wait()


VMEM = pl.BlockSpec(memory_space=pltpu.VMEM)


def on_core(kernel, inputs, out_shapes, scratch=(), out_spec=VMEM):
    shapes = [jax.ShapeDtypeStruct(s, jnp.float32) for s in out_shapes]
    return pl.pallas_call(
        kernel,
        out_shape=shapes,
        in_specs=[VMEM] * len(inputs),
        out_specs=[out_spec] * len(shapes),
        scratch_shapes=[pltpu.VMEM(s, jnp.float32) if isinstance(s, tuple) else s for s in scratch],
        compiler_params=pltpu.CompilerParams(vmem_limit_bytes=48 * 1024 * 1024),
    )(*inputs)


def swapped(x):
    return lax.ppermute(x, "tm", [(0, 1), (1, 0)])


def exchanged(blocks, way):
    count = lax.axis_size("space")
    mine = []
    for block, masks in zip(blocks, way):
        pairs = [(t * count + i, t * count + (i ^ masks[t])) for t in range(2) if masks[t] for i in range(count)]
        mine.append(lax.ppermute(block, ("tm", "space"), pairs))
    return mine, [swapped(x) for x in mine]


def strips_local(initial, reaction):
    count = lax.axis_size("space")
    _, nx, _ = initial.shape
    rows = nx // 4
    part = rows // 2
    planes = 2 * count
    block = (8 * rows + EDGE_ROWS, LANES)
    prepared = []
    for field, turns in ((initial, (12, -20)), (reaction, (20, -12))):
        prepared += on_core(
            functools.partial(prepare_kernel, turns),
            [field],
            [(16 * rows, LANES), (4 * rows, LANES)],
            [(4 * rows, LANES), (2 * rows, LANES)],
        )
    *blocks, own_block = on_core(fill_kernel, prepared, [block] * 5)
    mine, other = exchanged(blocks, WAY_IN)
    fine = ((planes + 2) * (rows + 2 * PAD), LANES)
    wide = ((count + 2) * (rows + 2 * PAD), LANES)
    small = ((count + 2) * (part + 2 * PAD), LANES)
    small_cells = (count * part, LANES)
    strip, given = on_core(
        march_kernel,
        [own_block, *mine, *other],
        [(count, 5 * part, LANES), (len(WAY_OUT) + 1, 5 * part, LANES)],
        [fine] * 4
        + [(planes * rows, LANES)] * 2
        + [wide, wide, (count * rows, LANES), small, small]
        + [small_cells] * 2
        + [(planes * rows, LANES)],
    )
    *blocks, own_block = on_core(send_kernel, [strip, swapped(given)], [(4 * rows + 8, LANES)] * 5)
    mine, other = exchanged(blocks, WAY_OUT)
    (out,) = on_core(
        unpack_kernel,
        [own_block, *mine, *other],
        [initial.shape],
        [(count, 2 * rows + 8, LANES), (nx, LANES), (16 * rows, LANES), initial.shape, pltpu.SemaphoreType.DMA((2,))],
        pl.BlockSpec(memory_space=pltpu.HBM),
    )
    return out[None]


def fits_strips(mesh, initial):
    planes = initial.shape[0] // (mesh.shape["groups"] * mesh.shape["space"])
    return (
        mesh.shape["space"] == 8
        and mesh.shape["tm"] == 2
        and planes == 2
        and initial.shape[1] == 192
        and initial.shape[2] == 2 * LANES
    )


def solution(mesh):
    in_specs = (P(("groups", "space"), None, None), P(("groups", "space"), None, None))
    out_specs = P(("groups", "tm"), "space", None, None)

    def run(initial, reaction):
        body = strips_local if fits_strips(mesh, initial) else local
        return jax.shard_map(body, mesh=mesh, in_specs=in_specs, out_specs=out_specs, check_vma=False)(initial, reaction)

    return run
```

```python
import functools

import jax
import jax.numpy as jnp
from jax import lax
from jax.experimental import pallas as pl
from jax.experimental.pallas import tpu as pltpu
from jax.sharding import PartitionSpec as P

FSTEPS = 16
CSTEPS = 4


def with_halo(cells, sides, width):
    for axis, dim in sides:
        count = lax.axis_size(axis)
        ends = count - 1
        head = lax.slice_in_dim(cells, 0, width, axis=dim)
        tail = lax.slice_in_dim(cells, cells.shape[dim] - width, cells.shape[dim], axis=dim)
        cells = jnp.concatenate(
            [
                lax.ppermute(tail, axis, [(i, (i + 1) % count) for i in range(ends)]),
                cells,
                lax.ppermute(head, axis, [((i + 1) % count, i) for i in range(ends)]),
            ],
            axis=dim,
        )
    return cells


def passed_along(x, axis, by):
    count = lax.axis_size(axis)
    pairs = [(i, i + by) for i in range(count) if 0 <= i + by < count]
    return lax.ppermute(x, axis, pairs)


def stencil(padded, reaction_rate, step_len, diffusion, upwind_scale):
    middle = padded[1:-1]
    lower_plane = padded[:-2]
    upper_plane = padded[2:]
    x_minus = jnp.roll(middle, 1, 1)
    x_plus = jnp.roll(middle, -1, 1)
    y_minus = jnp.roll(middle, 1, 2)
    y_plus = jnp.roll(middle, -1, 2)
    laplace = upper_plane + lower_plane + x_plus + x_minus + y_plus + y_minus - 6.0 * middle
    upwind = 0.13 * (middle - lower_plane) + 0.12 * (middle - x_minus) + 0.1 * (middle - y_minus)
    return middle + step_len * (
        diffusion * laplace - upwind_scale * upwind - reaction_rate * middle
    )


def restrict(field):
    depth, rows, cols = field.shape
    return field.reshape(depth // 2, 2, rows // 2, 2, cols // 2, 2).mean(axis=(1, 3, 5))


def prolong(coarse_field):
    return jnp.repeat(jnp.repeat(jnp.repeat(coarse_field, 2, 0), 2, 1), 2, 2)


def advance(field, rate_padded, width, steps, exchanger, constants, first_plane, planes_total):
    planes = field.shape[0]

    def block_turn(turn_index, current):
        padded = exchanger(current)
        for inner in range(width):
            rim_after = width - 1 - inner
            rate_slice = rate_padded[inner + 1 : inner + 1 + planes + 2 * rim_after]
            updated = stencil(padded, rate_slice, constants[0], constants[1], constants[2])
            global_plane = first_plane - rim_after + lax.iota(jnp.int32, planes + 2 * rim_after)
            inside = (global_plane >= 0) & (global_plane < planes_total)
            padded = jnp.where(inside[:, None, None], updated, 0.0)
        return padded

    return lax.fori_loop(0, steps // width, block_turn, field)


def local(initial, reaction):
    planes = initial.shape[0]
    planes_total = planes * lax.axis_size("space")
    first_plane = lax.axis_index("space") * planes
    slab_index = lax.axis_index("tm")
    slab_count = lax.axis_size("tm")
    coarse_rate = restrict(reaction)
    no_rim = ((1, 1), (0, 0), (0, 0))
    fine_width = min(planes, FSTEPS)
    fine_rate = with_halo(reaction, (("space", 0),), fine_width)

    def fine_exchange(current):
        return with_halo(current, (("space", 0),), fine_width)

    coarse_width = 1
    coarse_padded = jnp.pad(coarse_rate, no_rim)

    def coarse_exchange(current):
        return with_halo(current, (("space", 0),), 1)

    def coarse_run(field):
        small = advance(
            restrict(field),
            coarse_padded,
            coarse_width,
            CSTEPS,
            coarse_exchange,
            (2.0, 0.025, 0.5),
            first_plane // 2,
            planes_total // 2,
        )
        return prolong(small)

    def sweep(fine_values, previous):
        state = initial
        result = initial
        guess = initial
        for sweep_turn in range(slab_count):
            guess = coarse_run(state)
            if fine_values is None:
                result = guess
            else:
                result = guess + fine_values - previous
            if sweep_turn < slab_count - 1:
                incoming = passed_along(result, "tm", 1)
                state = jnp.where(slab_index == 0, initial, incoming)
        return (result, guess, state)

    result, previous, start = sweep(None, None)
    fine_values = advance(
        start,
        fine_rate,
        fine_width,
        FSTEPS,
        fine_exchange,
        (0.5, 0.1, 1.0),
        first_plane,
        planes_total,
    )
    result, previous, start = sweep(fine_values, previous)
    return result[None]


F_CONST = (0.5, 0.1, 1.0)
C_CONST = (2.0, 0.025, 0.5)
LANES = 128
PAD = 8
SPILL_TURNS = (0, 4, 8)
WAY_IN = ((1, 4), (5, 2), (3, 6), (7, 0))
WAY_OUT = ((4, 5), (6, 7), (1, 2), (3, 0))
EDGE_ROWS = 16
FINE_CHUNKS = ((0, 16), (32, 16), (16, 16))
HALF_CHUNKS = ((0, 16), (32, 16), (16, 16))
QUARTER_CHUNKS = ((0, 24),)


def weights(step_len, diffusion, upwind_scale):
    lead = step_len * diffusion
    lag = step_len * upwind_scale
    centre = (1.0 - 6.0 * lead - 0.35 * lag) / lead
    lows = tuple((lead + lag * part) / lead for part in (0.13, 0.12, 0.10))
    return lead, centre, step_len / lead, lows


def iota(shape, dim):
    return lax.broadcasted_iota(jnp.int32, shape, dim)


def roll(x, by):
    by = by % LANES
    return x if by == 0 else pltpu.roll(x, by, 1)


def take(x, lanes):
    return jnp.take_along_axis(x, lanes, axis=1, mode="promise_in_bounds")


def inside(index, first, last):
    return (index >= first) & (index < last)


def wrap_rows(field, planes, rows, quarter):
    height = rows + 2 * PAD
    for z in range(0, planes, 8):
        at = (z + 1) * height + PAD
        field[pl.ds(at - 1, 8, height), :] = roll(field[pl.ds(at + rows - 1, 8, height), :], quarter)
        field[pl.ds(at + rows, 8, height), :] = roll(field[pl.ds(at, 8, height), :], -quarter)


def one_step(src, dst, keep, planes, rows, lows, chunks, quarter):
    low_z, low_x, low_y = lows
    height = rows + 2 * PAD
    several = len(src) == 2
    for first, size in chunks:
        below = [None for _ in src]
        here = [s[height + PAD + first : height + PAD + first + size, :] for s in src]
        for z in range(planes):
            at = (z + 1) * height + PAD + first
            above = [s[at + height : at + height + size, :] if z + 1 < planes else None for s in src]
            for e, s in enumerate(src):
                if several:
                    o = here[1 - e]
                    y_low, y_high = (roll(o, 1), o) if e == 0 else (o, roll(o, -1))
                else:
                    y_low, y_high = roll(here[0], 1), roll(here[0], -1)
                out = keep[e][z * rows + first : z * rows + first + size, :] * here[e] + s[at + 1 : at + 1 + size, :]
                out = out + y_high + low_x * s[at - 1 : at - 1 + size, :] + low_y * y_low
                if above[e] is not None:
                    out = out + above[e]
                if below[e] is not None:
                    out = out + low_z * below[e]
                dst[e][at : at + size, :] = out
            below, here = here, above
    for d in dst:
        wrap_rows(d, planes, rows, quarter)


def sent_to(masks):
    return lax.axis_index("space") ^ jnp.where(lax.axis_index("tm") == 0, masks[0], masks[1])


def served(way, other_core=False):
    return [sent_to(masks[::-1] if other_core else masks) for masks in way] + [lax.axis_index("space")]


def prepare_kernel(turns, field, turned, edges, split, sums, coarse):
    rows = field.shape[1] // 4
    part = rows // 2
    lane = iota((rows, LANES), 1)
    low_half = lane < 64
    even_odd = jnp.where(low_half, 2 * lane, 2 * lane - (LANES - 1))
    odd_even = jnp.where(low_half, 2 * lane + 1, 2 * lane - LANES)
    for z in range(2):
        for j in range(4):
            at = slice(j * rows, (j + 1) * rows)
            for n, (x, lanes) in enumerate(((field[z, at, :LANES], even_odd), (field[z, at, LANES:], odd_even))):
                to = ((2 * z + n) * 4 + j) * rows
                split[to : to + rows, :] = take(x, lanes)
    for z in range(2):
        for j in range(4):
            at = slice(j * rows, (j + 1) * rows)
            left, right = (split[((2 * z + n) * 4 + j) * rows : ((2 * z + n) * 4 + j + 1) * rows, :] for n in range(2))
            even = roll(jnp.where(low_half, left, right), 32 * j)
            odd = roll(jnp.where(low_half, right, left), 32 * j + 64)
            for e, x in enumerate((even, odd)):
                to = ((2 * z + e) * 4 + j) * rows
                turned[to : to + rows, :] = x
            if z == 0:
                sums[at, :] = even + odd
            else:
                sums[at, :] = (sums[at, :] + (even + odd)) * 0.125
    for j in range(4):
        at = j * rows
        x = sums[pl.ds(at, part, 2), :] + sums[pl.ds(at + 1, part, 2), :]
        coarse[j * part : (j + 1) * part, :] = roll(x, -32 * j)
    for g in range(2 * rows // EDGE_ROWS):
        x = coarse[g * EDGE_ROWS : (g + 1) * EDGE_ROWS, :]
        place = 64 * (g // 3) + 16 * (g % 3)
        for n, by in enumerate(turns):
            to = (2 * g + n) * EDGE_ROWS
            edges[to : to + EDGE_ROWS, :] = roll(x, place + by)


def fill_kernel(initial_turned, initial_edges, reaction_turned, reaction_edges, *blocks):
    rows = initial_turned.shape[0] // 16
    for dest, block in zip(served(WAY_IN), blocks):
        back = (8 - 16 * dest) & (LANES - 1)
        quarter = ((iota((rows, LANES), 1) + back) & (LANES - 1)) >> 5
        for n in range(8):
            turned = (initial_turned, reaction_turned)[n // 4]
            x = [turned[(4 * (n % 4) + j) * rows : (4 * (n % 4) + j + 1) * rows, :] for j in range(4)]
            x = jnp.where(quarter == 0, x[0], jnp.where(quarter == 1, x[1], jnp.where(quarter == 2, x[2], x[3])))
            block[n * rows : (n + 1) * rows, :] = pltpu.roll(x, back, 1)
        back = (-16 * dest) & (LANES - 1)
        slot = ((iota((EDGE_ROWS, LANES), 1) + back) & (LANES - 1)) >> 2
        x = jnp.zeros((EDGE_ROWS, LANES), jnp.float32)
        for g in range(2 * rows // EDGE_ROWS):
            for n in range(4):
                edges = (initial_edges, reaction_edges)[n // 2]
                at = (2 * g + n % 2) * EDGE_ROWS
                x = jnp.where(slot == 16 * (g // 3) + 4 * (g % 3) + n, edges[at : at + EDGE_ROWS, :], x)
        block[8 * rows : 8 * rows + EDGE_ROWS, :] = pltpu.roll(x, back, 1)


def march_kernel(
    own_block, mine_0, mine_1, mine_2, mine_3, other_0, other_1, other_2, other_3, strip, given,
    even_a, odd_a, even_b, odd_b, even_keep, odd_keep, wide_a, wide_b, wide_keep, small_a, small_b, small_keep, second_guess, sums,
):
    tm, space = lax.axis_index("tm"), lax.axis_index("space")
    rows = (own_block.shape[0] - EDGE_ROWS) // 8
    planes = even_keep.shape[0] // rows
    count = planes // 2
    part = rows // 2
    height, wide_height, small_height = rows + 2 * PAD, rows + 2 * PAD, part + 2 * PAD
    lead, centre, slope, lows = weights(*F_CONST)
    small_lead, small_centre, small_slope, small_lows = weights(*C_CONST)
    small_scale = jnp.float32(small_lead**CSTEPS)
    scale = jnp.float32(lead**FSTEPS)
    fine_a, fine_b, fine_keep = (even_a, odd_a), (even_b, odd_b), (even_keep, odd_keep)
    lane = iota((part, LANES), 1)
    even_quarter = ((lane >> 5) & 1) == 0

    def some(index, height, first, size):
        return pl.ds(pl.multiple_of(index * height + first, 8), size)

    in_half = iota((rows, LANES), 1) & 63
    left, right = in_half < 4, inside(in_half, 36, 40)
    blocks = [(own_block, None, space)]
    for masks, mine, other in zip(WAY_IN, (mine_0, mine_1, mine_2), (other_0, other_1, other_2)):
        blocks.append((mine, None, sent_to(masks)))
        blocks.append((other, None, sent_to(masks[::-1])))
    blocks.append((mine_3, other_3, space ^ WAY_IN[3][0]))
    for number, (block, if_second, k) in enumerate(blocks):

        def read(first, size, block=block, if_second=if_second):
            if if_second is None:
                return block[first : first + size, :]
            return jnp.where(tm == 0, block[first : first + size, :], if_second[first : first + size, :])

        totals = []
        for n in range(2):
            total = None
            for z in range(2):
                for e in range(2):
                    x = read((4 * n + 2 * z + e) * rows, rows)
                    if n == 0:
                        fine_a[e][some(2 * k + z + 1, height, PAD, rows), :] = x
                    else:
                        fine_keep[e][some(2 * k + z, rows, 0, rows), :] = centre - slope * x
                    total = x if total is None else total + x
            temp = (2 * number + n) * rows
            sums[temp : temp + rows, :] = total * 0.125
            totals.append(temp)
        edge = read(8 * rows, EDGE_ROWS)
        small = [sums[pl.ds(temp, part, 2), :] + sums[pl.ds(temp + 1, part, 2), :] for temp in totals]
        small_keep[some(k, part, 0, part), :] = small_centre - small_slope * small[1]
        windows = []
        for n in range(2):
            inner = jnp.concatenate([roll(small[n], 4), roll(small[n], -28)], 0)
            lefts = jnp.concatenate([roll(edge, -16 * g - 8 * n) for g in range(rows // EDGE_ROWS)], 0)
            rights = jnp.concatenate([roll(edge, 32 - 16 * g - 8 * n) for g in range(rows // EDGE_ROWS)], 0)
            windows.append(jnp.where(left, lefts, jnp.where(right, rights, inner)))
        wide_a[some(k + 1, wide_height, PAD, rows), :] = windows[0]
        wide_keep[some(k, rows, 0, rows), :] = small_centre - small_slope * windows[1]
    def coarse_run():
        wrap_rows(small_a, count, part, 32)
        for _ in range(CSTEPS // 2):
            one_step((small_a,), (small_b,), (small_keep,), count, part, small_lows, QUARTER_CHUNKS, 32)
            one_step((small_b,), (small_a,), (small_keep,), count, part, small_lows, QUARTER_CHUNKS, 32)

    @pl.when(tm != 0)
    def _():
        wrap_rows(wide_a, count, rows, 64)
        for _ in range(CSTEPS // 2):
            one_step((wide_a,), (wide_b,), (wide_keep,), count, rows, small_lows, HALF_CHUNKS, 64)
            one_step((wide_b,), (wide_a,), (wide_keep,), count, rows, small_lows, HALF_CHUNKS, 64)
        for k in range(count):
            at = (k + 1) * wide_height + PAD
            upper, lower = wide_a[at : at + part, :], wide_a[at + part : at + rows, :]
            guess = jnp.where(even_quarter, roll(upper, -4), roll(lower, 28)) * small_scale
            strip[k, 2 * rows :, :] = guess
            to = (k + 1) * small_height + PAD
            small_a[to : to + part, :] = guess
            for z in range(2):
                for e in range(2):
                    to = (2 * k + z + 1) * height + PAD
                    fine_a[e][pl.ds(to, part, 2), :] = guess
                    fine_a[e][pl.ds(to + 1, part, 2), :] = guess
        coarse_run()
        for k in range(count):
            at = (k + 1) * small_height + PAD
            second_guess[k * part : (k + 1) * part, :] = small_a[at : at + part, :] * small_scale

    for field in fine_a:
        wrap_rows(field, planes, rows, 32)

    def turn(_, carry):
        one_step(fine_a, fine_b, fine_keep, planes, rows, lows, FINE_CHUNKS, 32)
        one_step(fine_b, fine_a, fine_keep, planes, rows, lows, FINE_CHUNKS, 32)
        return carry

    lax.fori_loop(0, FSTEPS // 2, turn, 0)

    own = inside(lane & 31, 8, 24)
    for k in range(count):
        less = jnp.where(tm == 0, 0.0, second_guess[k * part : (k + 1) * part, :])
        total = None
        for e in range(2):
            for odd in range(2):
                value = [fine_a[e][pl.ds((2 * k + z + 1) * height + PAD + odd, part, 2), :] * scale - less for z in range(2)]
                total = value[0] + value[1] if total is None else total + (value[0] + value[1])
                strip[k, pl.ds(e * rows + odd, part, 2), :] = jnp.where(own, value[0], roll(value[1], 16))
        to = (k + 1) * small_height + PAD
        small_a[to : to + part, :] = jnp.where(own, total * 0.125, 0.0)

    @pl.when(tm == 0)
    def _():
        coarse_run()
        for k in range(count):
            at = (k + 1) * small_height + PAD
            strip[k, 2 * rows :, :] = small_a[at : at + part, :] * small_scale

    for n, dest in enumerate(served(WAY_OUT, True)):
        given[n] = strip[dest]


def send_kernel(mine, other, *blocks):
    tm = lax.axis_index("tm")
    part = mine.shape[1] // 5
    rows = 2 * part
    in_quarter = iota((part, LANES), 1) & 31
    own = inside(in_quarter, 8, 24)
    spill = (inside(in_quarter, 4, 8) | inside(in_quarter, 24, 28))[:8]
    for n, (dest, block) in enumerate(zip(served(WAY_OUT), blocks)):
        kept, came = mine[dest, 2 * rows :, :], other[n, 2 * rows :, :]
        change, first = jnp.where(tm == 0, kept, came), jnp.where(tm == 0, came, kept)
        h = [jnp.where(own, x, roll(x, 16)) for x in (first, change)]
        for e in range(2):
            for odd in range(2):
                at = pl.ds(e * rows + odd, part, 2)
                to = pl.ds((2 + e) * rows + odd, part, 2)
                kept, came = mine[dest, at, :], other[n, at, :]
                block[at, :] = (h[0] + jnp.where(tm == 0, kept, came)) - h[0]
                block[to, :] = h[1] + jnp.where(tm == 0, came, kept)
        packed = None
        for g, by in enumerate(SPILL_TURNS):
            piece = roll(jnp.where(spill, change[8 * g : 8 * g + 8], 0.0), by)
            packed = piece if packed is None else packed + piece
        block[4 * rows : 4 * rows + 8, :] = packed


def unpack_kernel(own_block, mine_0, mine_1, mine_2, mine_3, other_0, other_1, other_2, other_3, out_hbm, strips, spilled, turned, halves, out, left):
    tm, space = lax.axis_index("tm"), lax.axis_index("space")
    count = strips.shape[0]
    rows = out.shape[1] // 4
    part = rows // 2
    blocks = [(own_block, None, space)]
    for masks, mine, other in zip(WAY_OUT, (mine_0, mine_1, mine_2), (other_0, other_1, other_2)):
        blocks.append((mine, None, sent_to(masks)))
        blocks.append((other, None, sent_to(masks[::-1])))
    blocks.append((mine_3, other_3, space ^ WAY_OUT[3][0]))
    for block, if_second, k in blocks:
        slabs = [block[: 2 * rows, :], block[2 * rows :, :]]
        if if_second is not None:
            slabs = [jnp.where(tm == 0, x, y) for x, y in zip(slabs, (if_second[: 2 * rows, :], if_second[2 * rows :, :]))]
        strips[k, : 2 * rows, :] = jnp.where(tm == 0, slabs[0], slabs[1][: 2 * rows])
        strips[k, 2 * rows :, :] = jnp.where(tm == 0, 0.0, slabs[1][2 * rows :])

    def lined_up(read, first, size):
        quarter = ((iota((size, LANES), 1) - first) & (LANES - 1)) >> 5
        for c in range(count):
            x = [read((c + 2 * j) % count) for j in range(4)]
            yield jnp.where(quarter == 0, x[0], jnp.where(quarter == 1, x[1], jnp.where(quarter == 2, x[2], x[3])))

    def at_strips(parts, j, hit):
        total = None
        for c, x in enumerate(parts):
            s = (c + 2 * j) % count
            total = jnp.where(hit[s], x, 0.0 if total is None else total)
        return total

    lane = iota((8, LANES), 1)
    hit = []
    for s in range(count):
        off = (lane - (16 * s - 4)) & (LANES - 1)
        hit.append((off < 4) | inside(off, 20, 24))
    pieces = list(lined_up(lambda s: strips[s, 2 * rows : 2 * rows + 8, :], 4, 8))
    for g, by in enumerate(SPILL_TURNS):
        parts = [roll(x, 16 * c - 8 - by) for c, x in enumerate(pieces)]
        for j in range(4):
            x = at_strips(parts, j, hit)
            at = j * rows + 16 * g
            spilled[pl.ds(at, 8, 2), :] = x
            spilled[pl.ds(at + 1, 8, 2), :] = x

    lane = iota((rows, LANES), 1)
    low_half = lane < 64
    from_first = ((lane & 1) << 6) + (lane >> 1)
    from_second = from_first ^ 64
    hit = [[inside((lane + 64 * e) & (LANES - 1), 16 * s, 16 * s + 16) for s in range(count)] for e in range(2)]
    for e in range(2):
        pieces = list(lined_up(lambda s, e=e: strips[s, e * rows : (e + 1) * rows, :], 8, rows))
        for z in range(2):
            parts = [roll(x, 16 * c - 8 - 16 * z + 64 * e) for c, x in enumerate(pieces)]
            for j in range(4):
                to = ((2 * z + e) * 4 + j) * rows
                halves[to : to + rows, :] = at_strips(parts, j, hit[e])
    for j in range(4):
        at = slice(j * rows, (j + 1) * rows)
        turned[at, :] = roll(spilled[at, :], 64)
    copies = []
    for z in range(2):
        for j in range(4):
            at = slice(j * rows, (j + 1) * rows)
            even, odd = (halves[((2 * z + e) * 4 + j) * rows : ((2 * z + e) * 4 + j + 1) * rows, :] for e in range(2))
            even, odd = even + spilled[at, :], odd + turned[at, :]
            out[z, at, :LANES] = take(jnp.where(low_half, even, odd), from_first)
            out[z, at, LANES:] = take(jnp.where(low_half, odd, even), from_second)
        copies.append(pltpu.make_async_copy(out.at[z], out_hbm.at[z], left.at[z]))
        copies[-1].start()
    for copy in copies:
        copy.wait()


VMEM = pl.BlockSpec(memory_space=pltpu.VMEM)


def on_core(kernel, inputs, out_shapes, scratch=(), out_spec=VMEM):
    shapes = [jax.ShapeDtypeStruct(s, jnp.float32) for s in out_shapes]
    return pl.pallas_call(
        kernel,
        out_shape=shapes,
        in_specs=[VMEM] * len(inputs),
        out_specs=[out_spec] * len(shapes),
        scratch_shapes=[pltpu.VMEM(s, jnp.float32) if isinstance(s, tuple) else s for s in scratch],
        compiler_params=pltpu.CompilerParams(vmem_limit_bytes=48 * 1024 * 1024),
    )(*inputs)


def swapped(x):
    return lax.ppermute(x, "tm", [(0, 1), (1, 0)])


def exchanged(blocks, way):
    count = lax.axis_size("space")
    mine = []
    for block, masks in zip(blocks, way):
        pairs = [(t * count + i, t * count + (i ^ masks[t])) for t in range(2) if masks[t] for i in range(count)]
        mine.append(lax.ppermute(block, ("tm", "space"), pairs))
    return mine, [swapped(x) for x in mine]


def strips_local(initial, reaction):
    count = lax.axis_size("space")
    _, nx, _ = initial.shape
    rows = nx // 4
    part = rows // 2
    planes = 2 * count
    block = (8 * rows + EDGE_ROWS, LANES)
    prepared = []
    for field, turns in ((initial, (12, -20)), (reaction, (20, -12))):
        prepared += on_core(
            functools.partial(prepare_kernel, turns),
            [field],
            [(16 * rows, LANES), (4 * rows, LANES)],
            [(16 * rows, LANES), (4 * rows, LANES), (2 * rows, LANES)],
        )
    *blocks, own_block = on_core(fill_kernel, prepared, [block] * 5)
    mine, other = exchanged(blocks, WAY_IN)
    fine = ((planes + 2) * (rows + 2 * PAD), LANES)
    wide = ((count + 2) * (rows + 2 * PAD), LANES)
    small = ((count + 2) * (part + 2 * PAD), LANES)
    small_cells = (count * part, LANES)
    strip, given = on_core(
        march_kernel,
        [own_block, *mine, *other],
        [(count, 5 * part, LANES), (len(WAY_OUT) + 1, 5 * part, LANES)],
        [fine] * 4
        + [(planes * rows, LANES)] * 2
        + [wide, wide, (count * rows, LANES), small, small]
        + [small_cells] * 2
        + [(planes * rows, LANES)],
    )
    *blocks, own_block = on_core(send_kernel, [strip, swapped(given)], [(4 * rows + 8, LANES)] * 5)
    mine, other = exchanged(blocks, WAY_OUT)
    (out,) = on_core(
        unpack_kernel,
        [own_block, *mine, *other],
        [initial.shape],
        [(count, 2 * rows + 8, LANES), (nx, LANES), (nx, LANES), (16 * rows, LANES), initial.shape, pltpu.SemaphoreType.DMA((2,))],
        pl.BlockSpec(memory_space=pltpu.HBM),
    )
    return out[None]


def fits_strips(mesh, initial):
    planes = initial.shape[0] // (mesh.shape["groups"] * mesh.shape["space"])
    return (
        mesh.shape["space"] == 8
        and mesh.shape["tm"] == 2
        and planes == 2
        and initial.shape[1] == 192
        and initial.shape[2] == 2 * LANES
    )


def solution(mesh):
    in_specs = (P(("groups", "space"), None, None), P(("groups", "space"), None, None))
    out_specs = P(("groups", "tm"), "space", None, None)

    def run(initial, reaction):
        body = strips_local if fits_strips(mesh, initial) else local
        return jax.shard_map(body, mesh=mesh, in_specs=in_specs, out_specs=out_specs, check_vma=False)(initial, reaction)

    return run
```

```python
import functools

import jax
import jax.numpy as jnp
from jax import lax
from jax.experimental import pallas as pl
from jax.experimental.pallas import tpu as pltpu
from jax.sharding import PartitionSpec as P

FSTEPS = 16
CSTEPS = 4


def with_halo(cells, sides, width):
    for axis, dim in sides:
        count = lax.axis_size(axis)
        ends = count - 1
        head = lax.slice_in_dim(cells, 0, width, axis=dim)
        tail = lax.slice_in_dim(cells, cells.shape[dim] - width, cells.shape[dim], axis=dim)
        cells = jnp.concatenate(
            [
                lax.ppermute(tail, axis, [(i, (i + 1) % count) for i in range(ends)]),
                cells,
                lax.ppermute(head, axis, [((i + 1) % count, i) for i in range(ends)]),
            ],
            axis=dim,
        )
    return cells


def passed_along(x, axis, by):
    count = lax.axis_size(axis)
    pairs = [(i, i + by) for i in range(count) if 0 <= i + by < count]
    return lax.ppermute(x, axis, pairs)


def stencil(padded, reaction_rate, step_len, diffusion, upwind_scale):
    middle = padded[1:-1]
    lower_plane = padded[:-2]
    upper_plane = padded[2:]
    x_minus = jnp.roll(middle, 1, 1)
    x_plus = jnp.roll(middle, -1, 1)
    y_minus = jnp.roll(middle, 1, 2)
    y_plus = jnp.roll(middle, -1, 2)
    laplace = upper_plane + lower_plane + x_plus + x_minus + y_plus + y_minus - 6.0 * middle
    upwind = 0.13 * (middle - lower_plane) + 0.12 * (middle - x_minus) + 0.1 * (middle - y_minus)
    return middle + step_len * (
        diffusion * laplace - upwind_scale * upwind - reaction_rate * middle
    )


def restrict(field):
    depth, rows, cols = field.shape
    return field.reshape(depth // 2, 2, rows // 2, 2, cols // 2, 2).mean(axis=(1, 3, 5))


def prolong(coarse_field):
    return jnp.repeat(jnp.repeat(jnp.repeat(coarse_field, 2, 0), 2, 1), 2, 2)


def advance(field, rate_padded, width, steps, exchanger, constants, first_plane, planes_total):
    planes = field.shape[0]

    def block_turn(turn_index, current):
        padded = exchanger(current)
        for inner in range(width):
            rim_after = width - 1 - inner
            rate_slice = rate_padded[inner + 1 : inner + 1 + planes + 2 * rim_after]
            updated = stencil(padded, rate_slice, constants[0], constants[1], constants[2])
            global_plane = first_plane - rim_after + lax.iota(jnp.int32, planes + 2 * rim_after)
            inside = (global_plane >= 0) & (global_plane < planes_total)
            padded = jnp.where(inside[:, None, None], updated, 0.0)
        return padded

    return lax.fori_loop(0, steps // width, block_turn, field)


def local(initial, reaction):
    planes = initial.shape[0]
    planes_total = planes * lax.axis_size("space")
    first_plane = lax.axis_index("space") * planes
    slab_index = lax.axis_index("tm")
    slab_count = lax.axis_size("tm")
    coarse_rate = restrict(reaction)
    no_rim = ((1, 1), (0, 0), (0, 0))
    fine_width = min(planes, FSTEPS)
    fine_rate = with_halo(reaction, (("space", 0),), fine_width)

    def fine_exchange(current):
        return with_halo(current, (("space", 0),), fine_width)

    coarse_width = 1
    coarse_padded = jnp.pad(coarse_rate, no_rim)

    def coarse_exchange(current):
        return with_halo(current, (("space", 0),), 1)

    def coarse_run(field):
        small = advance(
            restrict(field),
            coarse_padded,
            coarse_width,
            CSTEPS,
            coarse_exchange,
            (2.0, 0.025, 0.5),
            first_plane // 2,
            planes_total // 2,
        )
        return prolong(small)

    def sweep(fine_values, previous):
        state = initial
        result = initial
        guess = initial
        for sweep_turn in range(slab_count):
            guess = coarse_run(state)
            if fine_values is None:
                result = guess
            else:
                result = guess + fine_values - previous
            if sweep_turn < slab_count - 1:
                incoming = passed_along(result, "tm", 1)
                state = jnp.where(slab_index == 0, initial, incoming)
        return (result, guess, state)

    result, previous, start = sweep(None, None)
    fine_values = advance(
        start,
        fine_rate,
        fine_width,
        FSTEPS,
        fine_exchange,
        (0.5, 0.1, 1.0),
        first_plane,
        planes_total,
    )
    result, previous, start = sweep(fine_values, previous)
    return result[None]


F_CONST = (0.5, 0.1, 1.0)
C_CONST = (2.0, 0.025, 0.5)
LANES = 128
PAD = 8
SPILL_TURNS = (0, 4, 8)
WAY_IN = ((1, 4), (5, 2), (3, 6), (7, 7))
WAY_OUT = ((5, 7), (6, 1), (2, 3), (4, 4))
JOIN_COST = pl.CostEstimate(flops=10**10, bytes_accessed=10**7, transcendentals=0)
EDGE_ROWS = 16
FINE_CHUNKS = ((0, 16), (32, 16), (16, 16))
HALF_CHUNKS = ((0, 16), (32, 16), (16, 16))
QUARTER_CHUNKS = ((0, 24),)


def weights(step_len, diffusion, upwind_scale):
    lead = step_len * diffusion
    lag = step_len * upwind_scale
    centre = (1.0 - 6.0 * lead - 0.35 * lag) / lead
    lows = tuple((lead + lag * part) / lead for part in (0.13, 0.12, 0.10))
    return lead, centre, step_len / lead, lows


def iota(shape, dim):
    return lax.broadcasted_iota(jnp.int32, shape, dim)


def roll(x, by):
    by = by % LANES
    return x if by == 0 else pltpu.roll(x, by, 1)


def take(x, lanes):
    return jnp.take_along_axis(x, lanes, axis=1, mode="promise_in_bounds")


def inside(index, first, last):
    return (index >= first) & (index < last)


def wrap_rows(field, planes, rows, quarter):
    height = rows + 2 * PAD
    for z in range(0, planes, 8):
        at = (z + 1) * height + PAD
        field[pl.ds(at - 1, 8, height), :] = roll(field[pl.ds(at + rows - 1, 8, height), :], quarter)
        field[pl.ds(at + rows, 8, height), :] = roll(field[pl.ds(at, 8, height), :], -quarter)


def one_step(src, dst, keep, planes, rows, lows, chunks, quarter):
    low_z, low_x, low_y = lows
    height = rows + 2 * PAD
    several = len(src) == 2
    for first, size in chunks:
        below = [None for _ in src]
        here = [s[height + PAD + first : height + PAD + first + size, :] for s in src]
        for z in range(planes):
            at = (z + 1) * height + PAD + first
            above = [s[at + height : at + height + size, :] if z + 1 < planes else None for s in src]
            for e, s in enumerate(src):
                if several:
                    o = here[1 - e]
                    y_low, y_high = (roll(o, 1), o) if e == 0 else (o, roll(o, -1))
                else:
                    y_low, y_high = roll(here[0], 1), roll(here[0], -1)
                out = keep[e][z * rows + first : z * rows + first + size, :] * here[e] + s[at + 1 : at + 1 + size, :]
                out = out + y_high + low_x * s[at - 1 : at - 1 + size, :] + low_y * y_low
                if above[e] is not None:
                    out = out + above[e]
                if below[e] is not None:
                    out = out + low_z * below[e]
                dst[e][at : at + size, :] = out
            below, here = here, above
    for d in dst:
        wrap_rows(d, planes, rows, quarter)


def sent_to(masks):
    return lax.axis_index("space") ^ jnp.where(lax.axis_index("tm") == 0, masks[0], masks[1])


def served(way, other_core=False):
    return [sent_to(masks[::-1] if other_core else masks) for masks in way] + [lax.axis_index("space")]


def prepare_kernel(turns, field, turned, edges, split, sums, coarse):
    rows = field.shape[1] // 4
    part = rows // 2
    lane = iota((rows, LANES), 1)
    low_half = lane < 64
    even_odd = jnp.where(low_half, 2 * lane, 2 * lane - (LANES - 1))
    odd_even = jnp.where(low_half, 2 * lane + 1, 2 * lane - LANES)
    for z in range(2):
        for j in range(4):
            at = slice(j * rows, (j + 1) * rows)
            for n, (x, lanes) in enumerate(((field[z, at, :LANES], even_odd), (field[z, at, LANES:], odd_even))):
                to = ((2 * z + n) * 4 + j) * rows
                split[to : to + rows, :] = take(x, lanes)
    for z in range(2):
        for j in range(4):
            at = slice(j * rows, (j + 1) * rows)
            left, right = (split[((2 * z + n) * 4 + j) * rows : ((2 * z + n) * 4 + j + 1) * rows, :] for n in range(2))
            even = roll(jnp.where(low_half, left, right), 32 * j)
            odd = roll(jnp.where(low_half, right, left), 32 * j + 64)
            for e, x in enumerate((even, odd)):
                to = ((2 * z + e) * 4 + j) * rows
                turned[to : to + rows, :] = x
            if z == 0:
                sums[at, :] = even + odd
            else:
                sums[at, :] = (sums[at, :] + (even + odd)) * 0.125
    for j in range(4):
        at = j * rows
        x = sums[pl.ds(at, part, 2), :] + sums[pl.ds(at + 1, part, 2), :]
        coarse[j * part : (j + 1) * part, :] = roll(x, -32 * j)
    for g in range(2 * rows // EDGE_ROWS):
        x = coarse[g * EDGE_ROWS : (g + 1) * EDGE_ROWS, :]
        place = 64 * (g // 3) + 16 * (g % 3)
        for n, by in enumerate(turns):
            to = (2 * g + n) * EDGE_ROWS
            edges[to : to + EDGE_ROWS, :] = roll(x, place + by)


def fill_kernel(initial_turned, initial_edges, reaction_turned, reaction_edges, *blocks):
    rows = initial_turned.shape[0] // 16
    for dest, block in zip(served(WAY_IN), blocks):
        back = (8 - 16 * dest) & (LANES - 1)
        quarter = ((iota((rows, LANES), 1) + back) & (LANES - 1)) >> 5
        short = block.shape[0] < 8 * rows
        for n in range(4 if short else 8):

            def read(j, n=n):
                at = slice((4 * (n % 4) + j) * rows, (4 * (n % 4) + j + 1) * rows)
                if short:
                    return jnp.where(lax.axis_index("tm") == 0, initial_turned[at, :], reaction_turned[at, :])
                return (initial_turned, reaction_turned)[n // 4][at, :]

            x = [read(j) for j in range(4)]
            x = jnp.where(quarter == 0, x[0], jnp.where(quarter == 1, x[1], jnp.where(quarter == 2, x[2], x[3])))
            block[n * rows : (n + 1) * rows, :] = pltpu.roll(x, back, 1)
        back = (-16 * dest) & (LANES - 1)
        slot = ((iota((EDGE_ROWS, LANES), 1) + back) & (LANES - 1)) >> 2
        x = jnp.zeros((EDGE_ROWS, LANES), jnp.float32)
        for g in range(2 * rows // EDGE_ROWS):
            for n in range(4):
                edges = (initial_edges, reaction_edges)[n // 2]
                at = (2 * g + n % 2) * EDGE_ROWS
                x = jnp.where(slot == 16 * (g // 3) + 4 * (g % 3) + n, edges[at : at + EDGE_ROWS, :], x)
        block[block.shape[0] - EDGE_ROWS :, :] = pltpu.roll(x, back, 1)


def march_kernel(
    own_block, mine_0, mine_1, mine_2, mine_3, other_0, other_1, other_2, other_3, strip, given,
    even_a, odd_a, even_b, odd_b, even_keep, odd_keep, wide_a, wide_b, wide_keep, small_a, small_b, small_keep, second_guess, sums,
):
    tm, space = lax.axis_index("tm"), lax.axis_index("space")
    rows = (own_block.shape[0] - EDGE_ROWS) // 8
    planes = even_keep.shape[0] // rows
    count = planes // 2
    part = rows // 2
    height, wide_height, small_height = rows + 2 * PAD, rows + 2 * PAD, part + 2 * PAD
    lead, centre, slope, lows = weights(*F_CONST)
    small_lead, small_centre, small_slope, small_lows = weights(*C_CONST)
    small_scale = jnp.float32(small_lead**CSTEPS)
    scale = jnp.float32(lead**FSTEPS)
    fine_a, fine_b, fine_keep = (even_a, odd_a), (even_b, odd_b), (even_keep, odd_keep)
    lane = iota((part, LANES), 1)
    even_quarter = ((lane >> 5) & 1) == 0

    def some(index, height, first, size):
        return pl.ds(pl.multiple_of(index * height + first, 8), size)

    in_half = iota((rows, LANES), 1) & 63
    left, right = in_half < 4, inside(in_half, 36, 40)
    blocks = [(own_block, None, space)]
    for masks, mine, other in zip(WAY_IN, (mine_0, mine_1, mine_2), (other_0, other_1, other_2)):
        blocks.append((mine, None, sent_to(masks)))
        blocks.append((other, None, sent_to(masks[::-1])))
    blocks.append((mine_3, other_3, space ^ WAY_IN[-1][0]))
    for number, (block, if_second, k) in enumerate(blocks):

        def read(first, size, block=block, if_second=if_second):
            if if_second is None:
                return block[first : first + size, :]
            if first < 4 * rows:
                return jnp.where(tm == 0, block[first : first + size, :], if_second[first : first + size, :])
            first -= 4 * rows
            return jnp.where(tm == 0, if_second[first : first + size, :], block[first : first + size, :])

        totals = []
        for n in range(2):
            total = None
            for z in range(2):
                for e in range(2):
                    x = read((4 * n + 2 * z + e) * rows, rows)
                    if n == 0:
                        fine_a[e][some(2 * k + z + 1, height, PAD, rows), :] = x
                    else:
                        fine_keep[e][some(2 * k + z, rows, 0, rows), :] = centre - slope * x
                    total = x if total is None else total + x
            temp = (2 * number + n) * rows
            sums[temp : temp + rows, :] = total * 0.125
            totals.append(temp)
        edge = read(8 * rows, EDGE_ROWS)
        small = [sums[pl.ds(temp, part, 2), :] + sums[pl.ds(temp + 1, part, 2), :] for temp in totals]
        small_keep[some(k, part, 0, part), :] = small_centre - small_slope * small[1]
        windows = []
        for n in range(2):
            inner = jnp.concatenate([roll(small[n], 4), roll(small[n], -28)], 0)
            lefts = jnp.concatenate([roll(edge, -16 * g - 8 * n) for g in range(rows // EDGE_ROWS)], 0)
            rights = jnp.concatenate([roll(edge, 32 - 16 * g - 8 * n) for g in range(rows // EDGE_ROWS)], 0)
            windows.append(jnp.where(left, lefts, jnp.where(right, rights, inner)))
        wide_a[some(k + 1, wide_height, PAD, rows), :] = windows[0]
        wide_keep[some(k, rows, 0, rows), :] = small_centre - small_slope * windows[1]
    def coarse_run():
        wrap_rows(small_a, count, part, 32)
        for _ in range(CSTEPS // 2):
            one_step((small_a,), (small_b,), (small_keep,), count, part, small_lows, QUARTER_CHUNKS, 32)
            one_step((small_b,), (small_a,), (small_keep,), count, part, small_lows, QUARTER_CHUNKS, 32)

    @pl.when(tm != 0)
    def _():
        wrap_rows(wide_a, count, rows, 64)
        for _ in range(CSTEPS // 2):
            one_step((wide_a,), (wide_b,), (wide_keep,), count, rows, small_lows, HALF_CHUNKS, 64)
            one_step((wide_b,), (wide_a,), (wide_keep,), count, rows, small_lows, HALF_CHUNKS, 64)
        for k in range(count):
            at = (k + 1) * wide_height + PAD
            upper, lower = wide_a[at : at + part, :], wide_a[at + part : at + rows, :]
            guess = jnp.where(even_quarter, roll(upper, -4), roll(lower, 28)) * small_scale
            strip[k, 2 * rows :, :] = guess
            to = (k + 1) * small_height + PAD
            small_a[to : to + part, :] = guess
            for z in range(2):
                for e in range(2):
                    to = (2 * k + z + 1) * height + PAD
                    fine_a[e][pl.ds(to, part, 2), :] = guess
                    fine_a[e][pl.ds(to + 1, part, 2), :] = guess
        coarse_run()
        for k in range(count):
            at = (k + 1) * small_height + PAD
            second_guess[k * part : (k + 1) * part, :] = small_a[at : at + part, :] * small_scale

    for field in fine_a:
        wrap_rows(field, planes, rows, 32)

    def turn(_, carry):
        one_step(fine_a, fine_b, fine_keep, planes, rows, lows, FINE_CHUNKS, 32)
        one_step(fine_b, fine_a, fine_keep, planes, rows, lows, FINE_CHUNKS, 32)
        return carry

    lax.fori_loop(0, FSTEPS // 2, turn, 0)

    own = inside(lane & 31, 8, 24)
    for k in range(count):
        less = jnp.where(tm == 0, 0.0, second_guess[k * part : (k + 1) * part, :])
        total = None
        for e in range(2):
            for odd in range(2):
                value = [fine_a[e][pl.ds((2 * k + z + 1) * height + PAD + odd, part, 2), :] * scale - less for z in range(2)]
                total = value[0] + value[1] if total is None else total + (value[0] + value[1])
                strip[k, pl.ds(e * rows + odd, part, 2), :] = jnp.where(own, value[0], roll(value[1], 16))
        to = (k + 1) * small_height + PAD
        small_a[to : to + part, :] = jnp.where(own, total * 0.125, 0.0)

    @pl.when(tm == 0)
    def _():
        coarse_run()
        for k in range(count):
            at = (k + 1) * small_height + PAD
            strip[k, 2 * rows :, :] = small_a[at : at + part, :] * small_scale

    for n, dest in enumerate(served(WAY_OUT, True)):
        given[n] = strip[dest]


def send_kernel(mine, other, *blocks):
    tm = lax.axis_index("tm")
    part = mine.shape[1] // 5
    rows = 2 * part
    in_quarter = iota((part, LANES), 1) & 31
    own = inside(in_quarter, 8, 24)
    spill = (inside(in_quarter, 4, 8) | inside(in_quarter, 24, 28))[:8]
    for n, (dest, block) in enumerate(zip(served(WAY_OUT), blocks)):
        kept, came = mine[dest, 2 * rows :, :], other[n, 2 * rows :, :]
        change, first = jnp.where(tm == 0, kept, came), jnp.where(tm == 0, came, kept)
        short = block.shape[0] < 4 * rows
        if short:
            change, first = jnp.where(tm == 0, 0.0, came), came
        h = [jnp.where(own, x, roll(x, 16)) for x in (first, change)]
        for e in range(2):
            for odd in range(2):
                at = pl.ds(e * rows + odd, part, 2)
                to = pl.ds((2 + e) * rows + odd, part, 2)
                if short:
                    block[at, :] = (h[0] + mine[dest, at, :]) - jnp.where(tm == 0, h[0], 0.0)
                else:
                    kept, came = mine[dest, at, :], other[n, at, :]
                    block[at, :] = (h[0] + jnp.where(tm == 0, kept, came)) - h[0]
                    block[to, :] = h[1] + jnp.where(tm == 0, came, kept)
        packed = None
        for g, by in enumerate(SPILL_TURNS):
            piece = roll(jnp.where(spill, change[8 * g : 8 * g + 8], 0.0), by)
            packed = piece if packed is None else packed + piece
        block[block.shape[0] - 8 :, :] = packed


def join_kernel(own_block, last_block, both):
    both[0] = own_block[...]
    both[1] = last_block[...]


def unpack_kernel(both, mine_0, mine_1, mine_2, other_0, other_1, other_2, out_hbm, strips, spilled, turned, halves, out, left):
    tm, space = lax.axis_index("tm"), lax.axis_index("space")
    count = strips.shape[0]
    rows = out.shape[1] // 4
    part = rows // 2
    strips[space] = both[0]
    strips[space ^ WAY_OUT[-1][0]] = both[1]
    blocks = []
    for masks, mine, other in zip(WAY_OUT, (mine_0, mine_1, mine_2), (other_0, other_1, other_2)):
        blocks += [(mine, sent_to(masks)), (other, sent_to(masks[::-1]))]
    for block, k in blocks:
        strips[k, : 2 * rows, :] = jnp.where(tm == 0, block[: 2 * rows, :], block[2 * rows : 4 * rows, :])
        strips[k, 2 * rows :, :] = jnp.where(tm == 0, 0.0, block[4 * rows :, :])

    def lined_up(read, first, size):
        quarter = ((iota((size, LANES), 1) - first) & (LANES - 1)) >> 5
        for c in range(count):
            x = [read((c + 2 * j) % count) for j in range(4)]
            yield jnp.where(quarter == 0, x[0], jnp.where(quarter == 1, x[1], jnp.where(quarter == 2, x[2], x[3])))

    def at_strips(parts, j, hit):
        total = None
        for c, x in enumerate(parts):
            s = (c + 2 * j) % count
            total = jnp.where(hit[s], x, 0.0 if total is None else total)
        return total

    lane = iota((8, LANES), 1)
    hit = []
    for s in range(count):
        off = (lane - (16 * s - 4)) & (LANES - 1)
        hit.append((off < 4) | inside(off, 20, 24))
    pieces = list(lined_up(lambda s: strips[s, 2 * rows : 2 * rows + 8, :], 4, 8))
    for g, by in enumerate(SPILL_TURNS):
        parts = [roll(x, 16 * c - 8 - by) for c, x in enumerate(pieces)]
        for j in range(4):
            x = at_strips(parts, j, hit)
            at = j * rows + 16 * g
            spilled[pl.ds(at, 8, 2), :] = x
            spilled[pl.ds(at + 1, 8, 2), :] = x

    lane = iota((rows, LANES), 1)
    low_half = lane < 64
    from_first = ((lane & 1) << 6) + (lane >> 1)
    from_second = from_first ^ 64
    hit = [[inside((lane + 64 * e) & (LANES - 1), 16 * s, 16 * s + 16) for s in range(count)] for e in range(2)]
    for e in range(2):
        pieces = list(lined_up(lambda s, e=e: strips[s, e * rows : (e + 1) * rows, :], 8, rows))
        for z in range(2):
            parts = [roll(x, 16 * c - 8 - 16 * z + 64 * e) for c, x in enumerate(pieces)]
            for j in range(4):
                to = ((2 * z + e) * 4 + j) * rows
                halves[to : to + rows, :] = at_strips(parts, j, hit[e])
    for j in range(4):
        at = slice(j * rows, (j + 1) * rows)
        turned[at, :] = roll(spilled[at, :], 64)
    copies = []
    for z in range(2):
        for j in range(4):
            at = slice(j * rows, (j + 1) * rows)
            even, odd = (halves[((2 * z + e) * 4 + j) * rows : ((2 * z + e) * 4 + j + 1) * rows, :] for e in range(2))
            even, odd = even + spilled[at, :], odd + turned[at, :]
            out[z, at, :LANES] = take(jnp.where(low_half, even, odd), from_first)
            out[z, at, LANES:] = take(jnp.where(low_half, odd, even), from_second)
        copies.append(pltpu.make_async_copy(out.at[z], out_hbm.at[z], left.at[z]))
        copies[-1].start()
    for copy in copies:
        copy.wait()


VMEM = pl.BlockSpec(memory_space=pltpu.VMEM)


def on_core(kernel, inputs, out_shapes, scratch=(), out_spec=VMEM, cost=None):
    shapes = [jax.ShapeDtypeStruct(s, jnp.float32) for s in out_shapes]
    return pl.pallas_call(
        kernel,
        out_shape=shapes,
        in_specs=[VMEM] * len(inputs),
        out_specs=[out_spec] * len(shapes),
        cost_estimate=cost,
        scratch_shapes=[pltpu.VMEM(s, jnp.float32) if isinstance(s, tuple) else s for s in scratch],
        compiler_params=pltpu.CompilerParams(vmem_limit_bytes=48 * 1024 * 1024),
    )(*inputs)


def swapped(x):
    return lax.ppermute(x, "tm", [(0, 1), (1, 0)])


def exchanged(blocks, way):
    count = lax.axis_size("space")
    came = []
    for block, masks in zip(blocks, way):
        pairs = [(t * count + i, t * count + (i ^ masks[t])) for t in range(2) for i in range(count)]
        came.append(lax.ppermute(block, ("tm", "space"), pairs))
    return came


def strips_local(initial, reaction):
    count = lax.axis_size("space")
    _, nx, _ = initial.shape
    rows = nx // 4
    part = rows // 2
    planes = 2 * count
    block = (8 * rows + EDGE_ROWS, LANES)
    prepared = []
    for field, turns in ((initial, (12, -20)), (reaction, (20, -12))):
        prepared += on_core(
            functools.partial(prepare_kernel, turns),
            [field],
            [(16 * rows, LANES), (4 * rows, LANES)],
            [(16 * rows, LANES), (4 * rows + PAD, LANES), (2 * rows, LANES)],
        )
    *blocks, own_block = on_core(fill_kernel, prepared, [block] * 3 + [(4 * rows + EDGE_ROWS, LANES), block])
    mine = exchanged(blocks, WAY_IN)
    other = [swapped(x) for x in mine]
    fine = ((planes + 2) * (rows + 2 * PAD), LANES)
    wide = ((count + 2) * (rows + 2 * PAD), LANES)
    small = ((count + 2) * (part + 2 * PAD), LANES)
    small_cells = (count * part, LANES)
    strip, given = on_core(
        march_kernel,
        [own_block, *mine, *other],
        [(count, 5 * part, LANES), (len(WAY_OUT) + 1, 5 * part, LANES)],
        [fine] * 4
        + [(planes * rows, LANES)] * 2
        + [wide, wide, (count * rows, LANES), small, small]
        + [small_cells] * 2
        + [(planes * rows + PAD, LANES)],
    )
    *blocks, own_block = on_core(send_kernel, [strip, swapped(given)], [(4 * rows + 8, LANES)] * 3 + [(2 * rows + 8, LANES)] * 2)
    *mine, last = exchanged(blocks, WAY_OUT)
    other = [swapped(x) for x in mine]
    (both,) = on_core(join_kernel, [own_block, last], [(2, 2 * rows + 8, LANES)], cost=JOIN_COST)
    (out,) = on_core(
        unpack_kernel,
        [both, *mine, *other],
        [initial.shape],
        [(count, 2 * rows + 8, LANES), (nx + PAD, LANES), (nx, LANES), (16 * rows, LANES), initial.shape, pltpu.SemaphoreType.DMA((2,))],
        pl.BlockSpec(memory_space=pltpu.HBM),
    )
    return out[None]


def fits_strips(mesh, initial):
    planes = initial.shape[0] // (mesh.shape["groups"] * mesh.shape["space"])
    return (
        mesh.shape["space"] == 8
        and mesh.shape["tm"] == 2
        and planes == 2
        and initial.shape[1] == 192
        and initial.shape[2] == 2 * LANES
    )


def solution(mesh):
    in_specs = (P(("groups", "space"), None, None), P(("groups", "space"), None, None))
    out_specs = P(("groups", "tm"), "space", None, None)

    def run(initial, reaction):
        body = strips_local if fits_strips(mesh, initial) else local
        return jax.shard_map(body, mesh=mesh, in_specs=in_specs, out_specs=out_specs, check_vma=False)(initial, reaction)

    return run
```

```python
import functools

import jax
import jax.numpy as jnp
from jax import lax
from jax.experimental import pallas as pl
from jax.experimental.pallas import tpu as pltpu
from jax.sharding import PartitionSpec as P

FSTEPS = 16
CSTEPS = 4


def with_halo(cells, sides, width):
    for axis, dim in sides:
        count = lax.axis_size(axis)
        ends = count - 1
        head = lax.slice_in_dim(cells, 0, width, axis=dim)
        tail = lax.slice_in_dim(cells, cells.shape[dim] - width, cells.shape[dim], axis=dim)
        cells = jnp.concatenate(
            [
                lax.ppermute(tail, axis, [(i, (i + 1) % count) for i in range(ends)]),
                cells,
                lax.ppermute(head, axis, [((i + 1) % count, i) for i in range(ends)]),
            ],
            axis=dim,
        )
    return cells


def passed_along(x, axis, by):
    count = lax.axis_size(axis)
    pairs = [(i, i + by) for i in range(count) if 0 <= i + by < count]
    return lax.ppermute(x, axis, pairs)


def stencil(padded, reaction_rate, step_len, diffusion, upwind_scale):
    middle = padded[1:-1]
    lower_plane = padded[:-2]
    upper_plane = padded[2:]
    x_minus = jnp.roll(middle, 1, 1)
    x_plus = jnp.roll(middle, -1, 1)
    y_minus = jnp.roll(middle, 1, 2)
    y_plus = jnp.roll(middle, -1, 2)
    laplace = upper_plane + lower_plane + x_plus + x_minus + y_plus + y_minus - 6.0 * middle
    upwind = 0.13 * (middle - lower_plane) + 0.12 * (middle - x_minus) + 0.1 * (middle - y_minus)
    return middle + step_len * (
        diffusion * laplace - upwind_scale * upwind - reaction_rate * middle
    )


def restrict(field):
    depth, rows, cols = field.shape
    return field.reshape(depth // 2, 2, rows // 2, 2, cols // 2, 2).mean(axis=(1, 3, 5))


def prolong(coarse_field):
    return jnp.repeat(jnp.repeat(jnp.repeat(coarse_field, 2, 0), 2, 1), 2, 2)


def advance(field, rate_padded, width, steps, exchanger, constants, first_plane, planes_total):
    planes = field.shape[0]

    def block_turn(turn_index, current):
        padded = exchanger(current)
        for inner in range(width):
            rim_after = width - 1 - inner
            rate_slice = rate_padded[inner + 1 : inner + 1 + planes + 2 * rim_after]
            updated = stencil(padded, rate_slice, constants[0], constants[1], constants[2])
            global_plane = first_plane - rim_after + lax.iota(jnp.int32, planes + 2 * rim_after)
            inside = (global_plane >= 0) & (global_plane < planes_total)
            padded = jnp.where(inside[:, None, None], updated, 0.0)
        return padded

    return lax.fori_loop(0, steps // width, block_turn, field)


def local(initial, reaction):
    planes = initial.shape[0]
    planes_total = planes * lax.axis_size("space")
    first_plane = lax.axis_index("space") * planes
    slab_index = lax.axis_index("tm")
    slab_count = lax.axis_size("tm")
    coarse_rate = restrict(reaction)
    no_rim = ((1, 1), (0, 0), (0, 0))
    fine_width = min(planes, FSTEPS)
    fine_rate = with_halo(reaction, (("space", 0),), fine_width)

    def fine_exchange(current):
        return with_halo(current, (("space", 0),), fine_width)

    coarse_width = 1
    coarse_padded = jnp.pad(coarse_rate, no_rim)

    def coarse_exchange(current):
        return with_halo(current, (("space", 0),), 1)

    def coarse_run(field):
        small = advance(
            restrict(field),
            coarse_padded,
            coarse_width,
            CSTEPS,
            coarse_exchange,
            (2.0, 0.025, 0.5),
            first_plane // 2,
            planes_total // 2,
        )
        return prolong(small)

    def sweep(fine_values, previous):
        state = initial
        result = initial
        guess = initial
        for sweep_turn in range(slab_count):
            guess = coarse_run(state)
            if fine_values is None:
                result = guess
            else:
                result = guess + fine_values - previous
            if sweep_turn < slab_count - 1:
                incoming = passed_along(result, "tm", 1)
                state = jnp.where(slab_index == 0, initial, incoming)
        return (result, guess, state)

    result, previous, start = sweep(None, None)
    fine_values = advance(
        start,
        fine_rate,
        fine_width,
        FSTEPS,
        fine_exchange,
        (0.5, 0.1, 1.0),
        first_plane,
        planes_total,
    )
    result, previous, start = sweep(fine_values, previous)
    return result[None]


F_CONST = (0.5, 0.1, 1.0)
C_CONST = (2.0, 0.025, 0.5)
LANES = 128
PAD = 8
SPILL_TURNS = (0, 4, 8)
WAY_IN = ((1, 4), (5, 2), (3, 6), (7, 7))
WAY_OUT = ((5, 7), (1, 6), (2, 3), (4, 4))
JOIN_COST = pl.CostEstimate(flops=10**10, bytes_accessed=10**7, transcendentals=0)
EDGE_ROWS = 16
PACK_ROOM = 54080
FINE_CHUNKS = ((0, 16), (32, 16), (16, 16))
HALF_CHUNKS = ((0, 16), (32, 16), (16, 16))
QUARTER_CHUNKS = ((0, 24),)


def weights(step_len, diffusion, upwind_scale):
    lead = step_len * diffusion
    lag = step_len * upwind_scale
    centre = (1.0 - 6.0 * lead - 0.35 * lag) / lead
    lows = tuple((lead + lag * part) / lead for part in (0.13, 0.12, 0.10))
    return lead, centre, step_len / lead, lows


def iota(shape, dim):
    return lax.broadcasted_iota(jnp.int32, shape, dim)


def roll(x, by):
    by = by % LANES
    return x if by == 0 else pltpu.roll(x, by, 1)


def take(x, lanes):
    return jnp.take_along_axis(x, lanes, axis=1, mode="promise_in_bounds")


def inside(index, first, last):
    return (index >= first) & (index < last)


def wrap_rows(field, planes, rows, quarter):
    height = rows + 2 * PAD
    for z in range(0, planes, 8):
        at = (z + 1) * height + PAD
        field[pl.ds(at - 1, 8, height), :] = roll(field[pl.ds(at + rows - 1, 8, height), :], quarter)
        field[pl.ds(at + rows, 8, height), :] = roll(field[pl.ds(at, 8, height), :], -quarter)


def one_step(src, dst, keep, planes, rows, lows, chunks, quarter):
    low_z, low_x, low_y = lows
    height = rows + 2 * PAD
    several = len(src) == 2
    for first, size in chunks:
        below = [None for _ in src]
        here = [s[height + PAD + first : height + PAD + first + size, :] for s in src]
        for z in range(planes):
            at = (z + 1) * height + PAD + first
            above = [s[at + height : at + height + size, :] if z + 1 < planes else None for s in src]
            for e, s in enumerate(src):
                if several:
                    o = here[1 - e]
                    y_low, y_high = (roll(o, 1), o) if e == 0 else (o, roll(o, -1))
                else:
                    y_low, y_high = roll(here[0], 1), roll(here[0], -1)
                out = keep[e][z * rows + first : z * rows + first + size, :] * here[e] + s[at + 1 : at + 1 + size, :]
                out = out + y_high + low_x * s[at - 1 : at - 1 + size, :] + low_y * y_low
                if above[e] is not None:
                    out = out + above[e]
                if below[e] is not None:
                    out = out + low_z * below[e]
                dst[e][at : at + size, :] = out
            below, here = here, above
    for d in dst:
        wrap_rows(d, planes, rows, quarter)


def sent_to(masks):
    return lax.axis_index("space") ^ jnp.where(lax.axis_index("tm") == 0, masks[0], masks[1])


def served(way, other_core=False):
    return [sent_to(masks[::-1] if other_core else masks) for masks in way] + [lax.axis_index("space")]


def given_rows(way, part):
    sizes = [part if a == b else 5 * part for a, b in way] + [part]
    return [(sum(sizes[:n]), sum(sizes[: n + 1])) for n in range(len(sizes))]


def by_kind(way):
    return [m for m in way if m[0] != m[1]], [m for m in way if m[0] == m[1]]


def prepare(turns, field, arriving, turned, edges, split, sums, coarse):
    rows = field.shape[1] // 4
    part = rows // 2
    lane = iota((rows, LANES), 1)
    low_half = lane < 64
    even_odd = jnp.where(low_half, 2 * lane, 2 * lane - (LANES - 1))
    odd_even = jnp.where(low_half, 2 * lane + 1, 2 * lane - LANES)
    for z in range(2):
        if z == 0:
            arriving[0].wait()
        for j in range(4):
            at = slice(j * rows, (j + 1) * rows)
            for n, (x, lanes) in enumerate(((field[z, at, :LANES], even_odd), (field[z, at, LANES:], odd_even))):
                to = ((2 * z + n) * 4 + j) * rows
                split[to : to + rows, :] = take(x, lanes)
    for z in range(2):
        for j in range(4):
            at = slice(j * rows, (j + 1) * rows)
            left, right = (split[((2 * z + n) * 4 + j) * rows : ((2 * z + n) * 4 + j + 1) * rows, :] for n in range(2))
            even = roll(jnp.where(low_half, left, right), 32 * j)
            odd = roll(jnp.where(low_half, right, left), 32 * j + 64)
            for e, x in enumerate((even, odd)):
                to = ((2 * z + e) * 4 + j) * rows
                turned[to : to + rows, :] = x
            if z == 0:
                sums[at, :] = even + odd
            else:
                sums[at, :] = (sums[at, :] + (even + odd)) * 0.125
    for j in range(4):
        at = j * rows
        x = sums[pl.ds(at, part, 2), :] + sums[pl.ds(at + 1, part, 2), :]
        coarse[j * part : (j + 1) * part, :] = roll(x, -32 * j)
    for g in range(2 * rows // EDGE_ROWS):
        x = coarse[g * EDGE_ROWS : (g + 1) * EDGE_ROWS, :]
        place = 64 * (g // 3) + 16 * (g % 3)
        for n, by in enumerate(turns):
            to = (2 * g + n) * EDGE_ROWS
            edges[to : to + EDGE_ROWS, :] = roll(x, place + by)


def pack_kernel(initial_hbm, reaction_hbm, *refs):
    blocks, (initial, reaction, initial_turned, reaction_turned, initial_edges, reaction_edges), scratch = refs[:5], refs[5:11], refs[11:]
    *scratch, arrived = scratch
    copies = [
        [pltpu.make_async_copy(source, target, arrived.at[n])]
        for n, (source, target) in enumerate(((initial_hbm, initial), (reaction_hbm, reaction)))
    ]
    for copy in copies[0] + copies[1]:
        copy.start()
    prepare((12, -20), initial, copies[0], initial_turned, initial_edges, *scratch)
    prepare((20, -12), reaction, copies[1], reaction_turned, reaction_edges, *scratch)
    rows = initial_turned.shape[0] // 16
    for dest, block in zip(served(WAY_IN), blocks):
        back = (8 - 16 * dest) & (LANES - 1)
        quarter = ((iota((rows, LANES), 1) + back) & (LANES - 1)) >> 5
        short = block.shape[0] < 8 * rows
        for n in range(4 if short else 8):

            def read(j, n=n):
                at = slice((4 * (n % 4) + j) * rows, (4 * (n % 4) + j + 1) * rows)
                if short:
                    return jnp.where(lax.axis_index("tm") == 0, initial_turned[at, :], reaction_turned[at, :])
                return (initial_turned, reaction_turned)[n // 4][at, :]

            x = [read(j) for j in range(4)]
            x = jnp.where(quarter == 0, x[0], jnp.where(quarter == 1, x[1], jnp.where(quarter == 2, x[2], x[3])))
            block[n * rows : (n + 1) * rows, :] = pltpu.roll(x, back, 1)
        back = (-16 * dest) & (LANES - 1)
        slot = ((iota((EDGE_ROWS, LANES), 1) + back) & (LANES - 1)) >> 2
        x = jnp.zeros((EDGE_ROWS, LANES), jnp.float32)
        for g in range(2 * rows // EDGE_ROWS):
            for n in range(4):
                edges = (initial_edges, reaction_edges)[n // 2]
                at = (2 * g + n % 2) * EDGE_ROWS
                x = jnp.where(slot == 16 * (g // 3) + 4 * (g % 3) + n, edges[at : at + EDGE_ROWS, :], x)
        block[block.shape[0] - EDGE_ROWS :, :] = pltpu.roll(x, back, 1)


def march_kernel(
    own_block, mine_0, mine_1, mine_2, mine_3, other_0, other_1, other_2, other_3, strip, given,
    even_a, odd_a, even_b, odd_b, even_keep, odd_keep, wide_a, wide_b, wide_keep, small_a, small_b, small_keep, second_guess, sums,
):
    tm, space = lax.axis_index("tm"), lax.axis_index("space")
    rows = (own_block.shape[0] - EDGE_ROWS) // 8
    planes = even_keep.shape[0] // rows
    count = planes // 2
    part = rows // 2
    height, wide_height, small_height = rows + 2 * PAD, rows + 2 * PAD, part + 2 * PAD
    lead, centre, slope, lows = weights(*F_CONST)
    small_lead, small_centre, small_slope, small_lows = weights(*C_CONST)
    small_scale = jnp.float32(small_lead**CSTEPS)
    scale = jnp.float32(lead**FSTEPS)
    fine_a, fine_b, fine_keep = (even_a, odd_a), (even_b, odd_b), (even_keep, odd_keep)
    lane = iota((part, LANES), 1)
    even_quarter = ((lane >> 5) & 1) == 0

    def some(index, height, first, size):
        return pl.ds(pl.multiple_of(index * height + first, 8), size)

    in_half = iota((rows, LANES), 1) & 63
    left, right = in_half < 4, inside(in_half, 36, 40)
    blocks = [(own_block, None, space)]
    for masks, mine, other in zip(WAY_IN, (mine_0, mine_1, mine_2), (other_0, other_1, other_2)):
        blocks.append((mine, None, sent_to(masks)))
        blocks.append((other, None, sent_to(masks[::-1])))
    blocks.append((mine_3, other_3, space ^ WAY_IN[-1][0]))
    for number, (block, if_second, k) in enumerate(blocks):

        def read(first, size, block=block, if_second=if_second):
            if if_second is None:
                return block[first : first + size, :]
            if first < 4 * rows:
                return jnp.where(tm == 0, block[first : first + size, :], if_second[first : first + size, :])
            first -= 4 * rows
            return jnp.where(tm == 0, if_second[first : first + size, :], block[first : first + size, :])

        totals = []
        for n in range(2):
            total = None
            for z in range(2):
                for e in range(2):
                    x = read((4 * n + 2 * z + e) * rows, rows)
                    if n == 0:
                        fine_a[e][some(2 * k + z + 1, height, PAD, rows), :] = x
                    else:
                        fine_keep[e][some(2 * k + z, rows, 0, rows), :] = centre - slope * x
                    total = x if total is None else total + x
            temp = (2 * number + n) * rows
            sums[temp : temp + rows, :] = total * 0.125
            totals.append(temp)
        edge = read(8 * rows, EDGE_ROWS)
        small = [sums[pl.ds(temp, part, 2), :] + sums[pl.ds(temp + 1, part, 2), :] for temp in totals]
        small_keep[some(k, part, 0, part), :] = small_centre - small_slope * small[1]
        windows = []
        for n in range(2):
            inner = jnp.concatenate([roll(small[n], 4), roll(small[n], -28)], 0)
            lefts = jnp.concatenate([roll(edge, -16 * g - 8 * n) for g in range(rows // EDGE_ROWS)], 0)
            rights = jnp.concatenate([roll(edge, 32 - 16 * g - 8 * n) for g in range(rows // EDGE_ROWS)], 0)
            windows.append(jnp.where(left, lefts, jnp.where(right, rights, inner)))
        wide_a[some(k + 1, wide_height, PAD, rows), :] = windows[0]
        wide_keep[some(k, rows, 0, rows), :] = small_centre - small_slope * windows[1]
    def coarse_run():
        wrap_rows(small_a, count, part, 32)
        for _ in range(CSTEPS // 2):
            one_step((small_a,), (small_b,), (small_keep,), count, part, small_lows, QUARTER_CHUNKS, 32)
            one_step((small_b,), (small_a,), (small_keep,), count, part, small_lows, QUARTER_CHUNKS, 32)

    @pl.when(tm != 0)
    def _():
        wrap_rows(wide_a, count, rows, 64)
        for _ in range(CSTEPS // 2):
            one_step((wide_a,), (wide_b,), (wide_keep,), count, rows, small_lows, HALF_CHUNKS, 64)
            one_step((wide_b,), (wide_a,), (wide_keep,), count, rows, small_lows, HALF_CHUNKS, 64)
        for k in range(count):
            at = (k + 1) * wide_height + PAD
            upper, lower = wide_a[at : at + part, :], wide_a[at + part : at + rows, :]
            guess = jnp.where(even_quarter, roll(upper, -4), roll(lower, 28)) * small_scale
            strip[k, 2 * rows :, :] = guess
            to = (k + 1) * small_height + PAD
            small_a[to : to + part, :] = guess
            for z in range(2):
                for e in range(2):
                    to = (2 * k + z + 1) * height + PAD
                    fine_a[e][pl.ds(to, part, 2), :] = guess
                    fine_a[e][pl.ds(to + 1, part, 2), :] = guess
        coarse_run()
        for k in range(count):
            at = (k + 1) * small_height + PAD
            second_guess[k * part : (k + 1) * part, :] = small_a[at : at + part, :] * small_scale

    for field in fine_a:
        wrap_rows(field, planes, rows, 32)

    def turn(_, carry):
        one_step(fine_a, fine_b, fine_keep, planes, rows, lows, FINE_CHUNKS, 32)
        one_step(fine_b, fine_a, fine_keep, planes, rows, lows, FINE_CHUNKS, 32)
        return carry

    lax.fori_loop(0, FSTEPS // 2, turn, 0)

    own = inside(lane & 31, 8, 24)
    for k in range(count):
        less = jnp.where(tm == 0, 0.0, second_guess[k * part : (k + 1) * part, :])
        total = None
        for e in range(2):
            for odd in range(2):
                value = [fine_a[e][pl.ds((2 * k + z + 1) * height + PAD + odd, part, 2), :] * scale - less for z in range(2)]
                total = value[0] + value[1] if total is None else total + (value[0] + value[1])
                strip[k, pl.ds(e * rows + odd, part, 2), :] = jnp.where(own, value[0], roll(value[1], 16))
        to = (k + 1) * small_height + PAD
        small_a[to : to + part, :] = jnp.where(own, total * 0.125, 0.0)

    @pl.when(tm == 0)
    def _():
        coarse_run()
        for k in range(count):
            at = (k + 1) * small_height + PAD
            strip[k, 2 * rows :, :] = small_a[at : at + part, :] * small_scale

    for n, (dest, (first, last)) in enumerate(zip(served(WAY_OUT, True), given_rows(WAY_OUT, part))):
        given[first:last, :] = strip[dest, 5 * part - (last - first) :, :]


def send_kernel(mine, other, *blocks):
    tm = lax.axis_index("tm")
    part = mine.shape[1] // 5
    rows = 2 * part
    in_quarter = iota((part, LANES), 1) & 31
    own = inside(in_quarter, 8, 24)
    spill = (inside(in_quarter, 4, 8) | inside(in_quarter, 24, 28))[:8]
    for dest, block, (first_row, last_row) in zip(served(WAY_OUT), blocks, given_rows(WAY_OUT, part)):
        kept, came = mine[dest, 2 * rows :, :], other[last_row - part : last_row, :]
        change, first = jnp.where(tm == 0, kept, came), jnp.where(tm == 0, came, kept)
        short = block.shape[0] < 4 * rows
        if short:
            change, first = jnp.where(tm == 0, 0.0, came), came
        h = [jnp.where(own, x, roll(x, 16)) for x in (first, change)]
        for e in range(2):
            for odd in range(2):
                at = pl.ds(e * rows + odd, part, 2)
                to = pl.ds((2 + e) * rows + odd, part, 2)
                if short:
                    block[at, :] = (h[0] + mine[dest, at, :]) - jnp.where(tm == 0, h[0], 0.0)
                else:
                    kept, came = mine[dest, at, :], other[pl.ds(first_row + e * rows + odd, part, 2), :]
                    block[at, :] = (h[0] + jnp.where(tm == 0, kept, came)) - h[0]
                    block[to, :] = h[1] + jnp.where(tm == 0, came, kept)
        packed = None
        for g, by in enumerate(SPILL_TURNS):
            piece = roll(jnp.where(spill, change[8 * g : 8 * g + 8], 0.0), by)
            packed = piece if packed is None else packed + piece
        block[block.shape[0] - 8 :, :] = packed


def join_kernel(*refs):
    *blocks, joined = refs
    for n, block in enumerate(blocks):
        joined[n] = block[...]


def unpack_kernel(joined, *refs):
    shared, alone = by_kind(WAY_OUT)
    *came, out_hbm, strips, spilled, turned, halves, out, left = refs
    tm, space = lax.axis_index("tm"), lax.axis_index("space")
    count = strips.shape[0]
    rows = out.shape[1] // 4
    part = rows // 2
    strips[space] = joined[0]
    for n, masks in enumerate(alone):
        strips[space ^ masks[0]] = joined[n + 1]
    blocks = []
    for masks, mine, other in zip(shared, came[: len(shared)], came[len(shared) :]):
        blocks += [(mine, sent_to(masks)), (other, sent_to(masks[::-1]))]
    for block, k in blocks:
        strips[k, : 2 * rows, :] = jnp.where(tm == 0, block[: 2 * rows, :], block[2 * rows : 4 * rows, :])
        strips[k, 2 * rows :, :] = jnp.where(tm == 0, 0.0, block[4 * rows :, :])

    def lined_up(read, first, size):
        quarter = ((iota((size, LANES), 1) - first) & (LANES - 1)) >> 5
        for c in range(count):
            x = [read((c + 2 * j) % count) for j in range(4)]
            yield jnp.where(quarter == 0, x[0], jnp.where(quarter == 1, x[1], jnp.where(quarter == 2, x[2], x[3])))

    def at_strips(parts, j, hit):
        total = None
        for c, x in enumerate(parts):
            s = (c + 2 * j) % count
            total = jnp.where(hit[s], x, 0.0 if total is None else total)
        return total

    lane = iota((8, LANES), 1)
    hit = []
    for s in range(count):
        off = (lane - (16 * s - 4)) & (LANES - 1)
        hit.append((off < 4) | inside(off, 20, 24))
    pieces = list(lined_up(lambda s: strips[s, 2 * rows : 2 * rows + 8, :], 4, 8))
    for g, by in enumerate(SPILL_TURNS):
        parts = [roll(x, 16 * c - 8 - by) for c, x in enumerate(pieces)]
        for j in range(4):
            x = at_strips(parts, j, hit)
            at = j * rows + 16 * g
            spilled[pl.ds(at, 8, 2), :] = x
            spilled[pl.ds(at + 1, 8, 2), :] = x

    lane = iota((rows, LANES), 1)
    low_half = lane < 64
    from_first = ((lane & 1) << 6) + (lane >> 1)
    from_second = from_first ^ 64
    hit = [[inside((lane + 64 * e) & (LANES - 1), 16 * s, 16 * s + 16) for s in range(count)] for e in range(2)]
    for e in range(2):
        pieces = list(lined_up(lambda s, e=e: strips[s, e * rows : (e + 1) * rows, :], 8, rows))
        for z in range(2):
            parts = [roll(x, 16 * c - 8 - 16 * z + 64 * e) for c, x in enumerate(pieces)]
            for j in range(4):
                to = ((2 * z + e) * 4 + j) * rows
                halves[to : to + rows, :] = at_strips(parts, j, hit[e])
    for j in range(4):
        at = slice(j * rows, (j + 1) * rows)
        turned[at, :] = roll(spilled[at, :], 64)
    copies = []
    for z in range(2):
        for j in range(4):
            at = slice(j * rows, (j + 1) * rows)
            even, odd = (halves[((2 * z + e) * 4 + j) * rows : ((2 * z + e) * 4 + j + 1) * rows, :] for e in range(2))
            even, odd = even + spilled[at, :], odd + turned[at, :]
            out[z, at, :LANES] = take(jnp.where(low_half, even, odd), from_first)
            out[z, at, LANES:] = take(jnp.where(low_half, odd, even), from_second)
        copies.append(pltpu.make_async_copy(out.at[z], out_hbm.at[z], left.at[z]))
        copies[-1].start()
    for copy in copies:
        copy.wait()


VMEM = pl.BlockSpec(memory_space=pltpu.VMEM)
HBM = pl.BlockSpec(memory_space=pltpu.HBM)


def on_core(kernel, inputs, out_shapes, scratch=(), in_spec=VMEM, out_spec=VMEM, cost=None, room=48 * 1024):
    shapes = [jax.ShapeDtypeStruct(s, jnp.float32) for s in out_shapes]
    return pl.pallas_call(
        kernel,
        out_shape=shapes,
        in_specs=[in_spec] * len(inputs),
        out_specs=[out_spec] * len(shapes),
        cost_estimate=cost,
        scratch_shapes=[pltpu.VMEM(s, jnp.float32) if isinstance(s, tuple) else s for s in scratch],
        compiler_params=pltpu.CompilerParams(vmem_limit_bytes=room * 1024),
    )(*inputs)


def swapped(x):
    return lax.ppermute(x, "tm", [(0, 1), (1, 0)])


def exchanged(blocks, way):
    count = lax.axis_size("space")
    came = []
    for block, masks in zip(blocks, way):
        pairs = [(t * count + i, t * count + (i ^ masks[t])) for t in range(2) for i in range(count)]
        came.append(lax.ppermute(block, ("tm", "space"), pairs))
    return came


def strips_local(initial, reaction):
    count = lax.axis_size("space")
    _, nx, _ = initial.shape
    rows = nx // 4
    part = rows // 2
    planes = 2 * count
    block = (8 * rows + EDGE_ROWS, LANES)
    *blocks, own_block = on_core(
        pack_kernel,
        [initial, reaction],
        [block] * 3 + [(4 * rows + EDGE_ROWS, LANES), block],
        [initial.shape] * 2
        + [(16 * rows, LANES)] * 2
        + [(4 * rows, LANES)] * 2
        + [(16 * rows, LANES), (4 * rows + PAD, LANES), (2 * rows, LANES), pltpu.SemaphoreType.DMA((2,))],
        in_spec=HBM,
        room=PACK_ROOM,
    )
    mine = exchanged(blocks, WAY_IN)
    other = [swapped(x) for x in mine]
    fine = ((planes + 2) * (rows + 2 * PAD), LANES)
    wide = ((count + 2) * (rows + 2 * PAD), LANES)
    small = ((count + 2) * (part + 2 * PAD), LANES)
    small_cells = (count * part, LANES)
    strip, given = on_core(
        march_kernel,
        [own_block, *mine, *other],
        [(count, 5 * part, LANES), (given_rows(WAY_OUT, part)[-1][1], LANES)],
        [fine] * 4
        + [(planes * rows, LANES)] * 2
        + [wide, wide, (count * rows, LANES), small, small]
        + [small_cells] * 2
        + [(planes * rows + PAD, LANES)],
    )
    *blocks, own_block = on_core(send_kernel, [strip, swapped(given)], [((2 if a == b else 4) * rows + 8, LANES) for a, b in WAY_OUT + ((0, 0),)])
    came = list(zip(exchanged(blocks, WAY_OUT), WAY_OUT))
    mine = [x for x, (a, b) in came if a != b]
    other = [swapped(x) for x in mine]
    alone = [own_block] + [x for x, (a, b) in came if a == b]
    (joined,) = on_core(join_kernel, alone, [(len(alone), 2 * rows + 8, LANES)], cost=JOIN_COST)
    (out,) = on_core(
        unpack_kernel,
        [joined, *mine, *other],
        [initial.shape],
        [(count, 2 * rows + 8, LANES), (nx + PAD, LANES), (nx, LANES), (16 * rows, LANES), initial.shape, pltpu.SemaphoreType.DMA((2,))],
        out_spec=HBM,
    )
    return out[None]


def fits_strips(mesh, initial):
    planes = initial.shape[0] // (mesh.shape["groups"] * mesh.shape["space"])
    return (
        mesh.shape["space"] == 8
        and mesh.shape["tm"] == 2
        and planes == 2
        and initial.shape[1] == 192
        and initial.shape[2] == 2 * LANES
    )


def solution(mesh):
    in_specs = (P(("groups", "space"), None, None), P(("groups", "space"), None, None))
    out_specs = P(("groups", "tm"), "space", None, None)

    def run(initial, reaction):
        body = strips_local if fits_strips(mesh, initial) else local
        return jax.shard_map(body, mesh=mesh, in_specs=in_specs, out_specs=out_specs, check_vma=False)(initial, reaction)

    return run
```

```python
import functools

import jax
import jax.numpy as jnp
from jax import lax
from jax.experimental import pallas as pl
from jax.experimental.pallas import tpu as pltpu
from jax.sharding import PartitionSpec as P

FSTEPS = 16
CSTEPS = 4


def with_halo(cells, sides, width):
    for axis, dim in sides:
        count = lax.axis_size(axis)
        ends = count - 1
        head = lax.slice_in_dim(cells, 0, width, axis=dim)
        tail = lax.slice_in_dim(cells, cells.shape[dim] - width, cells.shape[dim], axis=dim)
        cells = jnp.concatenate(
            [
                lax.ppermute(tail, axis, [(i, (i + 1) % count) for i in range(ends)]),
                cells,
                lax.ppermute(head, axis, [((i + 1) % count, i) for i in range(ends)]),
            ],
            axis=dim,
        )
    return cells


def passed_along(x, axis, by):
    count = lax.axis_size(axis)
    pairs = [(i, i + by) for i in range(count) if 0 <= i + by < count]
    return lax.ppermute(x, axis, pairs)


def stencil(padded, reaction_rate, step_len, diffusion, upwind_scale):
    middle = padded[1:-1]
    lower_plane = padded[:-2]
    upper_plane = padded[2:]
    x_minus = jnp.roll(middle, 1, 1)
    x_plus = jnp.roll(middle, -1, 1)
    y_minus = jnp.roll(middle, 1, 2)
    y_plus = jnp.roll(middle, -1, 2)
    laplace = upper_plane + lower_plane + x_plus + x_minus + y_plus + y_minus - 6.0 * middle
    upwind = 0.13 * (middle - lower_plane) + 0.12 * (middle - x_minus) + 0.1 * (middle - y_minus)
    return middle + step_len * (
        diffusion * laplace - upwind_scale * upwind - reaction_rate * middle
    )


def restrict(field):
    depth, rows, cols = field.shape
    return field.reshape(depth // 2, 2, rows // 2, 2, cols // 2, 2).mean(axis=(1, 3, 5))


def prolong(coarse_field):
    return jnp.repeat(jnp.repeat(jnp.repeat(coarse_field, 2, 0), 2, 1), 2, 2)


def advance(field, rate_padded, width, steps, exchanger, constants, first_plane, planes_total):
    planes = field.shape[0]

    def block_turn(turn_index, current):
        padded = exchanger(current)
        for inner in range(width):
            rim_after = width - 1 - inner
            rate_slice = rate_padded[inner + 1 : inner + 1 + planes + 2 * rim_after]
            updated = stencil(padded, rate_slice, constants[0], constants[1], constants[2])
            global_plane = first_plane - rim_after + lax.iota(jnp.int32, planes + 2 * rim_after)
            inside = (global_plane >= 0) & (global_plane < planes_total)
            padded = jnp.where(inside[:, None, None], updated, 0.0)
        return padded

    return lax.fori_loop(0, steps // width, block_turn, field)


def local(initial, reaction):
    planes = initial.shape[0]
    planes_total = planes * lax.axis_size("space")
    first_plane = lax.axis_index("space") * planes
    slab_index = lax.axis_index("tm")
    slab_count = lax.axis_size("tm")
    coarse_rate = restrict(reaction)
    no_rim = ((1, 1), (0, 0), (0, 0))
    fine_width = min(planes, FSTEPS)
    fine_rate = with_halo(reaction, (("space", 0),), fine_width)

    def fine_exchange(current):
        return with_halo(current, (("space", 0),), fine_width)

    coarse_width = 1
    coarse_padded = jnp.pad(coarse_rate, no_rim)

    def coarse_exchange(current):
        return with_halo(current, (("space", 0),), 1)

    def coarse_run(field):
        small = advance(
            restrict(field),
            coarse_padded,
            coarse_width,
            CSTEPS,
            coarse_exchange,
            (2.0, 0.025, 0.5),
            first_plane // 2,
            planes_total // 2,
        )
        return prolong(small)

    def sweep(fine_values, previous):
        state = initial
        result = initial
        guess = initial
        for sweep_turn in range(slab_count):
            guess = coarse_run(state)
            if fine_values is None:
                result = guess
            else:
                result = guess + fine_values - previous
            if sweep_turn < slab_count - 1:
                incoming = passed_along(result, "tm", 1)
                state = jnp.where(slab_index == 0, initial, incoming)
        return (result, guess, state)

    result, previous, start = sweep(None, None)
    fine_values = advance(
        start,
        fine_rate,
        fine_width,
        FSTEPS,
        fine_exchange,
        (0.5, 0.1, 1.0),
        first_plane,
        planes_total,
    )
    result, previous, start = sweep(fine_values, previous)
    return result[None]


F_CONST = (0.5, 0.1, 1.0)
C_CONST = (2.0, 0.025, 0.5)
LANES = 128
PAD = 8
SPILL_TURNS = (0, 4, 8)
WAY_IN = ((1, 4), (5, 2), (3, 6), (7, 7))
WAY_OUT = ((5, 7), (1, 6), (2, 3), (4, 4))
JOIN_COST = pl.CostEstimate(flops=10**10, bytes_accessed=10**7, transcendentals=0)
EDGE_ROWS = 16
PACK_ROOM = 54080
FINE_CHUNKS = ((0, 16), (32, 16), (16, 16))
HALF_CHUNKS = ((0, 16), (32, 16), (16, 16))
QUARTER_CHUNKS = ((0, 24),)


def weights(step_len, diffusion, upwind_scale):
    lead = step_len * diffusion
    lag = step_len * upwind_scale
    centre = (1.0 - 6.0 * lead - 0.35 * lag) / lead
    lows = tuple((lead + lag * part) / lead for part in (0.13, 0.12, 0.10))
    return lead, centre, step_len / lead, lows


def iota(shape, dim):
    return lax.broadcasted_iota(jnp.int32, shape, dim)


def roll(x, by):
    by = by % LANES
    return x if by == 0 else pltpu.roll(x, by, 1)


def take(x, lanes):
    return jnp.take_along_axis(x, lanes, axis=1, mode="promise_in_bounds")


def inside(index, first, last):
    return (index >= first) & (index < last)


def wrap_rows(field, planes, rows, quarter):
    height = rows + 2 * PAD
    for z in range(0, planes, 8):
        at = (z + 1) * height + PAD
        field[pl.ds(at - 1, 8, height), :] = roll(field[pl.ds(at + rows - 1, 8, height), :], quarter)
        field[pl.ds(at + rows, 8, height), :] = roll(field[pl.ds(at, 8, height), :], -quarter)


def one_step(src, dst, keep, planes, rows, lows, chunks, quarter):
    low_z, low_x, low_y = lows
    height = rows + 2 * PAD
    several = len(src) == 2
    for first, size in chunks:
        below = [None for _ in src]
        here = [s[height + PAD + first : height + PAD + first + size, :] for s in src]
        for z in range(planes):
            at = (z + 1) * height + PAD + first
            above = [s[at + height : at + height + size, :] if z + 1 < planes else None for s in src]
            for e, s in enumerate(src):
                if several:
                    o = here[1 - e]
                    y_low, y_high = (roll(o, 1), o) if e == 0 else (o, roll(o, -1))
                else:
                    y_low, y_high = roll(here[0], 1), roll(here[0], -1)
                out = keep[e][z * rows + first : z * rows + first + size, :] * here[e] + s[at + 1 : at + 1 + size, :]
                out = out + y_high + low_x * s[at - 1 : at - 1 + size, :] + low_y * y_low
                if above[e] is not None:
                    out = out + above[e]
                if below[e] is not None:
                    out = out + low_z * below[e]
                dst[e][at : at + size, :] = out
            below, here = here, above
    for d in dst:
        wrap_rows(d, planes, rows, quarter)


def sent_to(masks):
    return lax.axis_index("space") ^ jnp.where(lax.axis_index("tm") == 0, masks[0], masks[1])


def served(way, other_core=False):
    return [sent_to(masks[::-1] if other_core else masks) for masks in way] + [lax.axis_index("space")]


def given_rows(way, part):
    sizes = [part if a == b else 5 * part for a, b in way] + [part]
    return [(sum(sizes[:n]), sum(sizes[: n + 1])) for n in range(len(sizes))]


def by_kind(way):
    return [m for m in way if m[0] != m[1]], [m for m in way if m[0] == m[1]]


def prepare(turns, field, arriving, turned, edges, split, sums, coarse):
    rows = field.shape[1] // 4
    part = rows // 2
    lane = iota((rows, LANES), 1)
    low_half = lane < 64
    even_odd = jnp.where(low_half, 2 * lane, 2 * lane - (LANES - 1))
    odd_even = jnp.where(low_half, 2 * lane + 1, 2 * lane - LANES)
    for z in range(2):
        if z == 0:
            arriving[0].wait()
        for j in range(4):
            at = slice(j * rows, (j + 1) * rows)
            for n, (x, lanes) in enumerate(((field[z, at, :LANES], even_odd), (field[z, at, LANES:], odd_even))):
                to = ((2 * z + n) * 4 + j) * rows
                split[to : to + rows, :] = take(x, lanes)
    for z in range(2):
        for j in range(4):
            at = slice(j * rows, (j + 1) * rows)
            left, right = (split[((2 * z + n) * 4 + j) * rows : ((2 * z + n) * 4 + j + 1) * rows, :] for n in range(2))
            even = roll(jnp.where(low_half, left, right), 32 * j)
            odd = roll(jnp.where(low_half, right, left), 32 * j + 64)
            for e, x in enumerate((even, odd)):
                to = ((2 * z + e) * 4 + j) * rows
                turned[to : to + rows, :] = x
            if z == 0:
                sums[at, :] = even + odd
            else:
                sums[at, :] = (sums[at, :] + (even + odd)) * 0.125
    for j in range(4):
        at = j * rows
        x = sums[pl.ds(at, part, 2), :] + sums[pl.ds(at + 1, part, 2), :]
        coarse[j * part : (j + 1) * part, :] = roll(x, -32 * j)
    for g in range(2 * rows // EDGE_ROWS):
        x = coarse[g * EDGE_ROWS : (g + 1) * EDGE_ROWS, :]
        place = 64 * (g // 3) + 16 * (g % 3)
        for n, by in enumerate(turns):
            to = (2 * g + n) * EDGE_ROWS
            edges[to : to + EDGE_ROWS, :] = roll(x, place + by)


def pack_kernel(initial_hbm, reaction_hbm, *refs):
    blocks, (initial, reaction, initial_turned, reaction_turned, initial_edges, reaction_edges), scratch = refs[:5], refs[5:11], refs[11:]
    *scratch, arrived = scratch
    copies = [
        [pltpu.make_async_copy(source, target, arrived.at[n])]
        for n, (source, target) in enumerate(((initial_hbm, initial), (reaction_hbm, reaction)))
    ]
    for copy in copies[0] + copies[1]:
        copy.start()
    prepare((12, -20), initial, copies[0], initial_turned, initial_edges, *scratch)
    prepare((20, -12), reaction, copies[1], reaction_turned, reaction_edges, *scratch)
    rows = initial_turned.shape[0] // 16
    for dest, block in zip(served(WAY_IN), blocks):
        back = (8 - 16 * dest) & (LANES - 1)
        quarter = ((iota((rows, LANES), 1) + back) & (LANES - 1)) >> 5
        short = block.shape[0] < 8 * rows
        for n in range(4 if short else 8):

            def read(j, n=n):
                at = slice((4 * (n % 4) + j) * rows, (4 * (n % 4) + j + 1) * rows)
                if short:
                    return jnp.where(lax.axis_index("tm") == 0, initial_turned[at, :], reaction_turned[at, :])
                return (initial_turned, reaction_turned)[n // 4][at, :]

            x = [read(j) for j in range(4)]
            x = jnp.where(quarter == 0, x[0], jnp.where(quarter == 1, x[1], jnp.where(quarter == 2, x[2], x[3])))
            block[n * rows : (n + 1) * rows, :] = pltpu.roll(x, back, 1)
        back = (-16 * dest) & (LANES - 1)
        slot = ((iota((EDGE_ROWS, LANES), 1) + back) & (LANES - 1)) >> 2
        x = jnp.zeros((EDGE_ROWS, LANES), jnp.float32)
        for g in range(2 * rows // EDGE_ROWS):
            for n in range(4):
                edges = (initial_edges, reaction_edges)[n // 2]
                at = (2 * g + n % 2) * EDGE_ROWS
                x = jnp.where(slot == 16 * (g // 3) + 4 * (g % 3) + n, edges[at : at + EDGE_ROWS, :], x)
        block[block.shape[0] - EDGE_ROWS :, :] = pltpu.roll(x, back, 1)


def march_kernel(
    own_block, mine_0, mine_1, mine_2, mine_3, other_0, other_1, other_2, other_3, strip, given,
    even_a, odd_a, even_b, odd_b, even_keep, odd_keep, wide_a, wide_b, wide_keep, small_a, small_b, small_keep, second_guess, sums,
):
    tm, space = lax.axis_index("tm"), lax.axis_index("space")
    rows = (own_block.shape[0] - EDGE_ROWS) // 8
    planes = even_keep.shape[0] // rows
    count = planes // 2
    part = rows // 2
    height, wide_height, small_height = rows + 2 * PAD, rows + 2 * PAD, part + 2 * PAD
    lead, centre, slope, lows = weights(*F_CONST)
    small_lead, small_centre, small_slope, small_lows = weights(*C_CONST)
    small_scale = jnp.float32(small_lead**CSTEPS)
    scale = jnp.float32(lead**FSTEPS)
    fine_a, fine_b, fine_keep = (even_a, odd_a), (even_b, odd_b), (even_keep, odd_keep)
    lane = iota((part, LANES), 1)
    even_quarter = ((lane >> 5) & 1) == 0

    def some(index, height, first, size):
        return pl.ds(pl.multiple_of(index * height + first, 8), size)

    in_half = iota((rows, LANES), 1) & 63
    left, right = in_half < 4, inside(in_half, 36, 40)
    blocks = [(own_block, None, space)]
    for masks, mine, other in zip(WAY_IN, (mine_0, mine_1, mine_2), (other_0, other_1, other_2)):
        blocks.append((mine, None, sent_to(masks)))
        blocks.append((other, None, sent_to(masks[::-1])))
    blocks.append((mine_3, other_3, space ^ WAY_IN[-1][0]))
    for number, (block, if_second, k) in enumerate(blocks):

        def read(first, size, block=block, if_second=if_second):
            if if_second is None:
                return block[first : first + size, :]
            if first < 4 * rows:
                return jnp.where(tm == 0, block[first : first + size, :], if_second[first : first + size, :])
            first -= 4 * rows
            return jnp.where(tm == 0, if_second[first : first + size, :], block[first : first + size, :])

        totals = []
        for n in range(2):
            total = None
            for z in range(2):
                for e in range(2):
                    x = read((4 * n + 2 * z + e) * rows, rows)
                    if n == 0:
                        fine_a[e][some(2 * k + z + 1, height, PAD, rows), :] = x
                    else:
                        fine_keep[e][some(2 * k + z, rows, 0, rows), :] = centre - slope * x
                    total = x if total is None else total + x
            temp = (2 * number + n) * rows
            sums[temp : temp + rows, :] = total * 0.125
            totals.append(temp)
        edge = read(8 * rows, EDGE_ROWS)
        small = [sums[pl.ds(temp, part, 2), :] + sums[pl.ds(temp + 1, part, 2), :] for temp in totals]
        small_keep[some(k, part, 0, part), :] = small_centre - small_slope * small[1]
        windows = []
        for n in range(2):
            inner = jnp.concatenate([roll(small[n], 4), roll(small[n], -28)], 0)
            lefts = jnp.concatenate([roll(edge, -16 * g - 8 * n) for g in range(rows // EDGE_ROWS)], 0)
            rights = jnp.concatenate([roll(edge, 32 - 16 * g - 8 * n) for g in range(rows // EDGE_ROWS)], 0)
            windows.append(jnp.where(left, lefts, jnp.where(right, rights, inner)))
        wide_a[some(k + 1, wide_height, PAD, rows), :] = windows[0]
        wide_keep[some(k, rows, 0, rows), :] = small_centre - small_slope * windows[1]
    def coarse_run():
        wrap_rows(small_a, count, part, 32)
        for _ in range(CSTEPS // 2):
            one_step((small_a,), (small_b,), (small_keep,), count, part, small_lows, QUARTER_CHUNKS, 32)
            one_step((small_b,), (small_a,), (small_keep,), count, part, small_lows, QUARTER_CHUNKS, 32)

    @pl.when(tm != 0)
    def _():
        wrap_rows(wide_a, count, rows, 64)
        for _ in range(CSTEPS // 2):
            one_step((wide_a,), (wide_b,), (wide_keep,), count, rows, small_lows, HALF_CHUNKS, 64)
            one_step((wide_b,), (wide_a,), (wide_keep,), count, rows, small_lows, HALF_CHUNKS, 64)
        for k in range(count):
            at = (k + 1) * wide_height + PAD
            upper, lower = wide_a[at : at + part, :], wide_a[at + part : at + rows, :]
            guess = jnp.where(even_quarter, roll(upper, -4), roll(lower, 28)) * small_scale
            strip[k, 2 * rows :, :] = guess
            to = (k + 1) * small_height + PAD
            small_a[to : to + part, :] = guess
            for z in range(2):
                for e in range(2):
                    to = (2 * k + z + 1) * height + PAD
                    fine_a[e][pl.ds(to, part, 2), :] = guess
                    fine_a[e][pl.ds(to + 1, part, 2), :] = guess
        coarse_run()
        for k in range(count):
            at = (k + 1) * small_height + PAD
            second_guess[k * part : (k + 1) * part, :] = small_a[at : at + part, :] * small_scale

    for field in fine_a:
        wrap_rows(field, planes, rows, 32)

    def turn(_, carry):
        one_step(fine_a, fine_b, fine_keep, planes, rows, lows, FINE_CHUNKS, 32)
        one_step(fine_b, fine_a, fine_keep, planes, rows, lows, FINE_CHUNKS, 32)
        return carry

    lax.fori_loop(0, FSTEPS // 2, turn, 0)

    own = inside(lane & 31, 8, 24)
    for k in range(count):
        less = jnp.where(tm == 0, 0.0, second_guess[k * part : (k + 1) * part, :])
        total = None
        for e in range(2):
            for odd in range(2):
                value = [fine_a[e][pl.ds((2 * k + z + 1) * height + PAD + odd, part, 2), :] * scale - less for z in range(2)]
                total = value[0] + value[1] if total is None else total + (value[0] + value[1])
                strip[k, pl.ds(e * rows + odd, part, 2), :] = jnp.where(own, value[0], roll(value[1], 16))
        to = (k + 1) * small_height + PAD
        small_a[to : to + part, :] = jnp.where(own, total * 0.125, 0.0)

    @pl.when(tm == 0)
    def _():
        coarse_run()
        for k in range(count):
            at = (k + 1) * small_height + PAD
            strip[k, 2 * rows :, :] = small_a[at : at + part, :] * small_scale

    for n, (dest, (first, last)) in enumerate(zip(served(WAY_OUT, True), given_rows(WAY_OUT, part))):
        given[first:last, :] = strip[dest, 5 * part - (last - first) :, :]


def send_kernel(mine, other, *blocks):
    tm = lax.axis_index("tm")
    part = mine.shape[1] // 5
    rows = 2 * part
    in_quarter = iota((part, LANES), 1) & 31
    own = inside(in_quarter, 8, 24)
    spill = (inside(in_quarter, 4, 8) | inside(in_quarter, 24, 28))[:8]
    for dest, block, (first_row, last_row) in zip(served(WAY_OUT), blocks, given_rows(WAY_OUT, part)):
        kept, came = mine[dest, 2 * rows :, :], other[last_row - part : last_row, :]
        change, first = jnp.where(tm == 0, kept, came), jnp.where(tm == 0, came, kept)
        short = block.shape[0] < 4 * rows
        if short:
            change, first = jnp.where(tm == 0, 0.0, came), came
        h = [jnp.where(own, x, roll(x, 16)) for x in (first, change)]
        for e in range(2):
            for odd in range(2):
                at = pl.ds(e * rows + odd, part, 2)
                to = pl.ds((2 + e) * rows + odd, part, 2)
                if short:
                    block[at, :] = (h[0] + mine[dest, at, :]) - jnp.where(tm == 0, h[0], 0.0)
                else:
                    kept, came = mine[dest, at, :], other[pl.ds(first_row + e * rows + odd, part, 2), :]
                    block[at, :] = (h[0] + jnp.where(tm == 0, kept, came)) - h[0]
                    block[to, :] = h[1] + jnp.where(tm == 0, came, kept)
        packed = None
        for g, by in enumerate(SPILL_TURNS):
            piece = roll(jnp.where(spill, change[8 * g : 8 * g + 8], 0.0), by)
            packed = piece if packed is None else packed + piece
        block[block.shape[0] - 8 :, :] = packed


def join_kernel(*refs):
    *blocks, joined = refs
    for n, block in enumerate(blocks):
        joined[n] = block[...]


def unpack_kernel(joined, *refs):
    shared, alone = by_kind(WAY_OUT)
    *came, out_hbm, strips, spilled, turned, halves, out, left = refs
    tm, space = lax.axis_index("tm"), lax.axis_index("space")
    count = strips.shape[0]
    rows = out.shape[1] // 4
    part = rows // 2
    strips[space] = joined[0]
    for n, masks in enumerate(alone):
        strips[space ^ masks[0]] = joined[n + 1]
    blocks = []
    for masks, mine, other in zip(shared, came[: len(shared)], came[len(shared) :]):
        blocks += [(mine, sent_to(masks)), (other, sent_to(masks[::-1]))]
    for block, k in blocks:
        strips[k, : 2 * rows, :] = jnp.where(tm == 0, block[: 2 * rows, :], block[2 * rows : 4 * rows, :])
        strips[k, 2 * rows :, :] = jnp.where(tm == 0, 0.0, block[4 * rows :, :])

    def lined_up(read, first, size):
        quarter = ((iota((size, LANES), 1) - first) & (LANES - 1)) >> 5
        for c in range(count):
            x = [read((c + 2 * j) % count) for j in range(4)]
            yield jnp.where(quarter == 0, x[0], jnp.where(quarter == 1, x[1], jnp.where(quarter == 2, x[2], x[3])))

    def at_strips(parts, j, hit):
        total = None
        for c, x in enumerate(parts):
            s = (c + 2 * j) % count
            total = jnp.where(hit[s], x, 0.0 if total is None else total)
        return total

    lane = iota((8, LANES), 1)
    hit = []
    for s in range(count):
        off = (lane - (16 * s - 4)) & (LANES - 1)
        hit.append((off < 4) | inside(off, 20, 24))
    pieces = list(lined_up(lambda s: strips[s, 2 * rows : 2 * rows + 8, :], 4, 8))
    for g, by in enumerate(SPILL_TURNS):
        parts = [roll(x, 16 * c - 8 - by) for c, x in enumerate(pieces)]
        for j in range(4):
            x = at_strips(parts, j, hit)
            at = j * rows + 16 * g
            spilled[pl.ds(at, 8, 2), :] = x
            spilled[pl.ds(at + 1, 8, 2), :] = x

    lane = iota((rows, LANES), 1)
    low_half = lane < 64
    from_first = ((lane & 1) << 6) + (lane >> 1)
    from_second = from_first ^ 64
    hit = [[inside((lane + 64 * e) & (LANES - 1), 16 * s, 16 * s + 16) for s in range(count)] for e in range(2)]
    for e in range(2):
        pieces = list(lined_up(lambda s, e=e: strips[s, e * rows : (e + 1) * rows, :], 8, rows))
        for z in range(2):
            parts = [roll(x, 16 * c - 8 - 16 * z + 64 * e) for c, x in enumerate(pieces)]
            for j in range(4):
                to = ((2 * z + e) * 4 + j) * rows
                halves[to : to + rows, :] = at_strips(parts, j, hit[e])
    for j in range(4):
        at = slice(j * rows, (j + 1) * rows)
        turned[at, :] = roll(spilled[at, :], 64)
    copies = []
    for z in range(2):
        for j in range(4):
            at = slice(j * rows, (j + 1) * rows)
            even, odd = (halves[((2 * z + e) * 4 + j) * rows : ((2 * z + e) * 4 + j + 1) * rows, :] for e in range(2))
            even, odd = even + spilled[at, :], odd + turned[at, :]
            out[z, at, :LANES] = take(jnp.where(low_half, even, odd), from_first)
            out[z, at, LANES:] = take(jnp.where(low_half, odd, even), from_second)
            if j % 2 == 1:
                sent = pl.ds((j - 1) * rows, 2 * rows)
                copies.append(pltpu.make_async_copy(out.at[z, sent], out_hbm.at[z, sent], left.at[2 * z + j // 2]))
                copies[-1].start()
    for copy in copies:
        copy.wait()


VMEM = pl.BlockSpec(memory_space=pltpu.VMEM)
HBM = pl.BlockSpec(memory_space=pltpu.HBM)


def on_core(kernel, inputs, out_shapes, scratch=(), in_spec=VMEM, out_spec=VMEM, cost=None, room=48 * 1024):
    shapes = [jax.ShapeDtypeStruct(s, jnp.float32) for s in out_shapes]
    return pl.pallas_call(
        kernel,
        out_shape=shapes,
        in_specs=[in_spec] * len(inputs),
        out_specs=[out_spec] * len(shapes),
        cost_estimate=cost,
        scratch_shapes=[pltpu.VMEM(s, jnp.float32) if isinstance(s, tuple) else s for s in scratch],
        compiler_params=pltpu.CompilerParams(vmem_limit_bytes=room * 1024),
    )(*inputs)


def swapped(x):
    return lax.ppermute(x, "tm", [(0, 1), (1, 0)])


def exchanged(blocks, way):
    count = lax.axis_size("space")
    came = []
    for block, masks in zip(blocks, way):
        pairs = [(t * count + i, t * count + (i ^ masks[t])) for t in range(2) for i in range(count)]
        came.append(lax.ppermute(block, ("tm", "space"), pairs))
    return came


def strips_local(initial, reaction):
    count = lax.axis_size("space")
    _, nx, _ = initial.shape
    rows = nx // 4
    part = rows // 2
    planes = 2 * count
    block = (8 * rows + EDGE_ROWS, LANES)
    *blocks, own_block = on_core(
        pack_kernel,
        [initial, reaction],
        [block] * 3 + [(4 * rows + EDGE_ROWS, LANES), block],
        [initial.shape] * 2
        + [(16 * rows, LANES)] * 2
        + [(4 * rows, LANES)] * 2
        + [(16 * rows, LANES), (4 * rows + PAD, LANES), (2 * rows, LANES), pltpu.SemaphoreType.DMA((2,))],
        in_spec=HBM,
        room=PACK_ROOM,
    )
    mine = exchanged(blocks, WAY_IN)
    other = [swapped(x) for x in mine]
    fine = ((planes + 2) * (rows + 2 * PAD), LANES)
    wide = ((count + 2) * (rows + 2 * PAD), LANES)
    small = ((count + 2) * (part + 2 * PAD), LANES)
    small_cells = (count * part, LANES)
    strip, given = on_core(
        march_kernel,
        [own_block, *mine, *other],
        [(count, 5 * part, LANES), (given_rows(WAY_OUT, part)[-1][1], LANES)],
        [fine] * 4
        + [(planes * rows, LANES)] * 2
        + [wide, wide, (count * rows, LANES), small, small]
        + [small_cells] * 2
        + [(planes * rows + PAD, LANES)],
    )
    *blocks, own_block = on_core(send_kernel, [strip, swapped(given)], [((2 if a == b else 4) * rows + 8, LANES) for a, b in WAY_OUT + ((0, 0),)])
    came = list(zip(exchanged(blocks, WAY_OUT), WAY_OUT))
    mine = [x for x, (a, b) in came if a != b]
    other = [swapped(x) for x in mine]
    alone = [own_block] + [x for x, (a, b) in came if a == b]
    (joined,) = on_core(join_kernel, alone, [(len(alone), 2 * rows + 8, LANES)], cost=JOIN_COST)
    (out,) = on_core(
        unpack_kernel,
        [joined, *mine, *other],
        [initial.shape],
        [(count, 2 * rows + 8, LANES), (nx + PAD, LANES), (nx, LANES), (16 * rows, LANES), initial.shape, pltpu.SemaphoreType.DMA((4,))],
        out_spec=HBM,
    )
    return out[None]


def fits_strips(mesh, initial):
    planes = initial.shape[0] // (mesh.shape["groups"] * mesh.shape["space"])
    return (
        mesh.shape["space"] == 8
        and mesh.shape["tm"] == 2
        and planes == 2
        and initial.shape[1] == 192
        and initial.shape[2] == 2 * LANES
    )


def solution(mesh):
    in_specs = (P(("groups", "space"), None, None), P(("groups", "space"), None, None))
    out_specs = P(("groups", "tm"), "space", None, None)

    def run(initial, reaction):
        body = strips_local if fits_strips(mesh, initial) else local
        return jax.shard_map(body, mesh=mesh, in_specs=in_specs, out_specs=out_specs, check_vma=False)(initial, reaction)

    return run
```
